32 devices in a mesh: section: 4 (over y, x), tensor: 8 (over z, core).
Axes of the slice: x: 2, y: 2, z: 4, core: 2. Of those that a mesh axis runs over, the one named last changes fastest.
Arguments:
- tokens: bfloat16 [512, 8192], P('section'), may hold values from -6 to 6
- cotangent: bfloat16 [512, 8192], P('section'), may hold values from -0.3125 to 0.3125
- gate_weight: bfloat16 [640, 8192], P(('section', 'tensor')), may hold values from -0.0625 to 0.0625
- up_weight: bfloat16 [640, 8192], P(('section', 'tensor')), may hold values from -0.0625 to 0.0625
- down_weight: bfloat16 [640, 8192], P(('section', 'tensor')), may hold values from -0.25 to 0.25
Outputs:
- output: bfloat16 [512, 8192], P('section', 'tensor')
- grad_gate: float32 [640, 8192], P(('section', 'tensor'))
- grad_up: float32 [640, 8192], P(('section', 'tensor'))
- grad_down: float32 [640, 8192], P(('section', 'tensor'))
The draws below stay inside these ranges and needn't reach their ends.
All inputs are finite; a program needn't handle non-finite values.
Results may differ from the reference program's by a relative error of at most 0.005.
Values may be sent and summed in bfloat16 or wider, within the bound.
No kernel may reach another device: no remote copies, remote signals or barrier semaphores. Data moves between devices by JAX's collectives and lax.ppermute only.
A program may use at most 64 MiB of HBM per device.

```python
import jax
import jax.numpy as jnp
from jax import lax

D = 8192
TOK = 128
STEPS = 3
BLOCK = 160
H = 640
TOKENS = 512
N_SECTION = 4


def steps_of(own_key, extent, cuts, low, high):
    level = 1.0
    for axis_at, blocks in cuts:
        steps = jax.random.uniform(jax.random.fold_in(jax.random.fold_in(own_key, 6), axis_at), (blocks,), jnp.float32, low / len(cuts), high / len(cuts))
        level = level * jnp.repeat(jnp.exp(steps), extent[axis_at] // blocks).reshape((-1,) + (1,) * (len(extent) - 1 - axis_at))
    return level


def centred(stream_key, shape, width, bound, cuts=(), held_as=jnp.bfloat16):
    loudness = steps_of(stream_key, shape, cuts, -0.22, 0.18) if cuts else 1.0
    drawn = jax.random.normal(stream_key, shape, jnp.float32) * width * loudness
    return jnp.minimum(jnp.maximum(drawn, -bound), bound).astype(held_as)


def setup_inputs(seed: int = 0) -> dict:
    key_of = jax.random.split(jax.random.key(seed), 6)
    tokens = centred(key_of[0], (TOKENS, D), 1.0, 6.0, ((0, 4),))
    cotangent = centred(key_of[1], (TOKENS, D), (STEPS * TOK) ** -0.5, 0.3125, ((0, 4),))
    gate_weight = centred(key_of[2], (H, D), D ** -0.5, 0.0625, ((0, 32),))
    up_weight = centred(key_of[3], (H, D), D ** -0.5, 0.0625, ((0, 32),))
    down_weight = centred(key_of[4], (H, D), (STEPS * BLOCK) ** -0.5, 0.25, ((0, 32),))
    return {"tokens": tokens, "cotangent": cotangent, "gate_weight": gate_weight, "up_weight": up_weight, "down_weight": down_weight}


def forward_block(inputs, gate_rows, up_rows, down_rows):
    along_rows = (((1,), (1,)), ((), ()))
    gate_proj = lax.dot_general(inputs, gate_rows, along_rows, preferred_element_type=jnp.float32)
    up_proj = lax.dot_general(inputs, up_rows, along_rows, preferred_element_type=jnp.float32)
    activated = jax.nn.silu(gate_proj)
    hidden = (activated * up_proj).astype(jnp.bfloat16)
    partial_value = jnp.dot(hidden, down_rows, preferred_element_type=jnp.float32)
    return partial_value, gate_proj, up_proj, hidden


def backward_block(inputs, cot_rows, down_rows, gate_proj, up_proj, hidden):
    along_rows = (((1,), (1,)), ((), ()))
    along_tokens = (((0,), (0,)), ((), ()))
    hidden_grad = lax.dot_general(cot_rows, down_rows, along_rows, preferred_element_type=jnp.float32)
    sigmoid_gate = jax.nn.sigmoid(gate_proj)
    activated = jax.nn.silu(gate_proj)
    gate_grad = (hidden_grad * up_proj * sigmoid_gate * (1.0 + gate_proj * (1.0 - sigmoid_gate))).astype(jnp.bfloat16)
    up_grad = (hidden_grad * activated).astype(jnp.bfloat16)
    grad_gate = lax.dot_general(gate_grad, inputs, along_tokens, preferred_element_type=jnp.float32)
    grad_up = lax.dot_general(up_grad, inputs, along_tokens, preferred_element_type=jnp.float32)
    grad_down = lax.dot_general(hidden, cot_rows, along_tokens, preferred_element_type=jnp.float32)
    return grad_gate, grad_up, grad_down


def reference(tokens, cotangent, gate_weight, up_weight, down_weight):
    inputs_all = tokens.reshape(N_SECTION, TOK, D)
    cot_all = cotangent.reshape(N_SECTION, TOK, D)
    gate_all = gate_weight.reshape(N_SECTION, BLOCK, D)
    up_all = up_weight.reshape(N_SECTION, BLOCK, D)
    down_all = down_weight.reshape(N_SECTION, BLOCK, D)
    empty = jnp.zeros((BLOCK, D), jnp.float32)
    sums_gate = [empty for owner in range(N_SECTION)]
    sums_up = [empty for owner in range(N_SECTION)]
    sums_down = [empty for owner in range(N_SECTION)]
    outputs = []
    for batch_index in range(N_SECTION):
        total = jnp.zeros((TOK, D), jnp.float32)
        for offset in range(STEPS):
            owner = (batch_index - offset) % N_SECTION
            partial_value, gate_proj, up_proj, hidden = forward_block(inputs_all[batch_index], gate_all[owner], up_all[owner], down_all[owner])
            total = total + partial_value
            terms = backward_block(inputs_all[batch_index], cot_all[batch_index], down_all[owner], gate_proj, up_proj, hidden)
            sums_gate[owner] = sums_gate[owner] + terms[0]
            sums_up[owner] = sums_up[owner] + terms[1]
            sums_down[owner] = sums_down[owner] + terms[2]
        outputs.append(total.astype(jnp.bfloat16))
    return (jnp.concatenate(outputs, 0), jnp.concatenate(sums_gate, 0), jnp.concatenate(sums_up, 0), jnp.concatenate(sums_down, 0))
```

```python
import jax
import jax.numpy as jnp
from jax import lax
from jax.sharding import PartitionSpec as P

STEPS = 3
BF = jnp.bfloat16
F32 = jnp.float32


def rows_dot(inputs, rows):
    return lax.dot_general(inputs, rows, (((1,), (1,)), ((), ())), preferred_element_type=F32)


def tokens_dot(left, right):
    return lax.dot_general(left, right, (((0,), (0,)), ((), ())), preferred_element_type=F32)


def exchanged(value, axis, bit):
    count = lax.axis_size(axis)
    return lax.ppermute(value, axis, [(source, source ^ bit) for source in range(count)])


def ring_passed(value, steps):
    count = lax.axis_size("section")
    return lax.ppermute(value, "section", [(source, (source + steps) % count) for source in range(count)])


def packed_weights(gate, up, down):
    half = gate.shape[1] // 2
    return (
        jnp.concatenate([gate[:, :half], up[:, :half]], 0),
        jnp.concatenate([gate[:, half:], up[:, half:]], 0),
        jnp.concatenate([down[:, :half], down[:, half:]], 0),
    )


def block_work(inputs, cot, weights):
    first, second, down = weights
    rows = down.shape[0] // 2
    half = down.shape[1]
    both = rows_dot(inputs[:, :half], first) + rows_dot(inputs[:, half:], second)
    gate, up = both[:, :rows], both[:, rows:]
    sig = jax.nn.sigmoid(gate)
    activated = gate * sig
    hidden = (activated * up).astype(BF)
    dhid = rows_dot(cot[:, :half], down[:rows]) + rows_dot(cot[:, half:], down[rows:])
    dgate = (dhid * up * sig * (1.0 + gate * (1.0 - sig))).astype(BF)
    dup = (dhid * activated).astype(BF)
    pair = jnp.concatenate([dgate, dup], 1)
    return hidden, pair


def block_grads(inputs, cot, hidden, pair):
    half = inputs.shape[1] // 2
    return (
        tokens_dot(pair, inputs[:, :half]),
        tokens_dot(pair, inputs[:, half:]),
        jnp.concatenate([tokens_dot(hidden, cot[:, :half]), tokens_dot(hidden, cot[:, half:])], 0),
    )


def scattered_sum(total):
    count = lax.axis_size("tensor")
    if count & (count - 1):
        return lax.psum_scatter(total, "tensor", scatter_dimension=1, tiled=True).astype(BF)
    me = lax.axis_index("tensor")
    width = total.shape[1] // count
    parts = [total[:, k * width : (k + 1) * width] for k in range(count)]
    bit = 1
    while bit < count:
        mine = (me & bit) != 0
        low, high = parts[0::2], parts[1::2]
        keep = [jnp.where(mine, b, a) for a, b in zip(low, high)]
        send = jnp.concatenate([jnp.where(mine, a, b).astype(BF) for a, b in zip(low, high)], 1)
        got = exchanged(send, "tensor", bit).astype(F32)
        parts = [k + got[:, i * width : (i + 1) * width] for i, k in enumerate(keep)]
        bit *= 2
    return parts[0].astype(BF)


def on_device(tokens, cotangent, gate_weight, up_weight, down_weight):
    own = packed_weights(gate_weight, up_weight, down_weight)
    four = lax.axis_size("section") == 4
    odd = (lax.axis_index("section") & 1) != 0
    if four:
        far = tuple(exchanged(piece, "section", 2) for piece in own)
        near = tuple(exchanged(jnp.where(odd, f, o), "section", 1) for f, o in zip(far, own))
    else:
        near = tuple(ring_passed(piece, 1) for piece in own)
        far = tuple(ring_passed(piece, 1) for piece in near)
    work = [block_work(tokens, cotangent, w) for w in (own, near, far)]
    hidden = jnp.concatenate([w[0] for w in work], 1)
    rows = gate_weight.shape[0]
    down_low = jnp.concatenate([w[2][:rows] for w in (own, near, far)], 0)
    down_high = jnp.concatenate([w[2][rows:] for w in (own, near, far)], 0)
    total = jnp.concatenate(
        [jnp.dot(hidden, down_low, preferred_element_type=F32), jnp.dot(hidden, down_high, preferred_element_type=F32)], 1
    )
    output = scattered_sum(total)
    grads = [block_grads(tokens, cotangent, *w) for w in work]
    zero = jnp.zeros((), F32)
    sums = []
    for k in (2, 0, 1):
        g_own, g_near, g_far = (g[k] for g in grads)
        if four:
            side = exchanged(g_near.astype(BF), "section", 1).astype(F32)
            back = exchanged((g_far + jnp.where(odd, side, zero)).astype(BF), "section", 2).astype(F32)
            sums.append(g_own + back + jnp.where(odd, zero, side))
        else:
            side = ring_passed(g_far.astype(BF), -1).astype(F32)
            back = ring_passed((g_near + side).astype(BF), -1).astype(F32)
            sums.append(g_own + back)
    down_sum, low, high = sums
    grad_gate = jnp.concatenate([low[:rows], high[:rows]], 1)
    grad_up = jnp.concatenate([low[rows:], high[rows:]], 1)
    grad_down = jnp.concatenate([down_sum[:rows], down_sum[rows:]], 1)
    return (output, grad_gate, grad_up, grad_down)


def solution(mesh):
    placed = (
        P("section", None),
        P("section", None),
        P(("section", "tensor"), None),
        P(("section", "tensor"), None),
        P(("section", "tensor"), None),
    )
    return jax.shard_map(
        on_device,
        mesh=mesh,
        in_specs=placed,
        out_specs=(
            P("section", "tensor"),
            P(("section", "tensor"), None),
            P(("section", "tensor"), None),
            P(("section", "tensor"), None),
        ),
        check_vma=False,
    )
```

```python
import jax
import jax.numpy as jnp
from jax import lax
from jax.experimental import pallas as pl
from jax.experimental.pallas import tpu as pltpu
from jax.sharding import PartitionSpec as P

BF = jnp.bfloat16
F32 = jnp.float32
NN = (((1,), (0,)), ((), ()))
NT = (((1,), (1,)), ((), ()))
TN = (((0,), (0,)), ((), ()))
TILE = 512


def dot(left, right, dims):
    return lax.dot_general(left, right, dims, preferred_element_type=F32)


class Steps:
    def __init__(self):
        self.mark = None

    def __call__(self, body, outs, ins, also=()):
        marks = [*also] if self.mark is None else [*also, self.mark]
        count = len(ins)

        def kernel(*refs):
            body(*refs[:count], *refs[count + len(marks) : -1])
            refs[-1][...] = jnp.zeros_like(refs[-1])

        single = isinstance(outs, tuple)
        shapes = ([outs] if single else list(outs)) + [((8, 128), F32)]
        *got, self.mark = pl.pallas_call(
            kernel,
            out_shape=[jax.ShapeDtypeStruct(*s) for s in shapes],
            in_specs=[pl.BlockSpec(memory_space=pltpu.VMEM)] * (count + len(marks)),
            out_specs=[pl.BlockSpec(memory_space=pltpu.VMEM)] * len(shapes),
            compiler_params=pltpu.CompilerParams(vmem_limit_bytes=24 * 1024 * 1024),
            cost_estimate=pl.CostEstimate(flops=1, bytes_accessed=1, transcendentals=0),
        )(*ins, *marks)
        return got[0] if single else got


def is_odd():
    return lax.rem(lax.axis_index("section"), 2) == 1


def project(x, low, high, both, hid_a, hid_b):
    rows, half = low.shape[0] // 2, low.shape[1]
    total = jnp.zeros(both.shape, F32)
    for at in range(0, half, 1024):
        cut = slice(at, at + 1024)
        total += dot(low[:, cut], x[:, cut], NT)
        total += dot(high[:, cut], x[:, half + at : half + at + 1024], NT)
    both[...] = total
    up = pltpu.roll(total, rows, 0)
    hidden = total * jax.nn.sigmoid(total) * up
    first = lax.broadcasted_iota(jnp.int32, total.shape, 0) < rows
    hidden = jnp.where(first, hidden, 0.0)
    hid_a[...] = hidden.astype(BF)
    hid_b[...] = pltpu.roll(hidden, rows, 0).astype(BF)


def derive(g, down, both, pair):
    rows, half = down.shape[0] // 2, down.shape[1]
    low = jnp.zeros(both.shape, F32)
    high = jnp.zeros(both.shape, F32)
    for at in range(0, half, 1024):
        cut = slice(at, at + 1024)
        low += dot(down[:, cut], g[:, cut], NT)
        high += dot(down[:, cut], g[:, half + at : half + at + 1024], NT)
    dhid = low + pltpu.roll(high, rows, 0)
    gate = both[...]
    up = pltpu.roll(gate, rows, 0)
    sig = jax.nn.sigmoid(gate)
    dgate = dhid * up * sig * (1.0 + gate * (1.0 - sig))
    dup = pltpu.roll(dhid * (gate * sig), rows, 0)
    first = lax.broadcasted_iota(jnp.int32, gate.shape, 0) < rows
    pair[...] = jnp.where(first, dgate, dup).astype(BF)


def down_columns(g, hid_a, hid_b, at, half):
    cut = slice(at, at + TILE)
    return dot(hid_a[...], g[:, cut], NN) + dot(hid_b[...], g[:, half + at : half + at + TILE], NN)


def own_grads(x, g, hid_a, hid_b, pair, low, high, down):
    half = low.shape[1]
    for at in range(0, half, TILE):
        cut = slice(at, at + TILE)
        low[:, cut] = dot(pair[...], x[:, cut], NN)
        high[:, cut] = dot(pair[...], x[:, half + at : half + at + TILE], NN)
        down[:, cut] = down_columns(g, hid_a, hid_b, at, half)


def sent_down(g, hid_a, hid_b, out):
    half = out.shape[1]
    for at in range(0, half, TILE):
        out[:, at : at + TILE] = down_columns(g, hid_a, hid_b, at, half).astype(BF)


def sent_pair(x, pair, low, high):
    half = low.shape[1]
    for at in range(0, half, TILE):
        cut = slice(at, at + TILE)
        low[:, cut] = dot(pair[...], x[:, cut], NN).astype(BF)
        high[:, cut] = dot(pair[...], x[:, half + at : half + at + TILE], NN).astype(BF)


def kept(side, odd, four, wanted):
    value = side.astype(F32)
    return jnp.where(odd == wanted, value, 0.0) if four else value


def either(bit, run):
    for value in range(2):
        pl.when(bit == value)(lambda value=value: run(value))


def picked(here, piece, out):
    @pl.when(is_odd())
    def _():
        out[...] = here[...]

    @pl.when(jnp.logical_not(is_odd()))
    def _():
        out[...] = piece[...]


def output_sums(count, tokens_half, *refs):
    hids, downs, outs = refs[:6], refs[6:9], refs[9:]
    half = downs[0].shape[1]
    width = 2 * half // count
    mine = lax.rem(lax.axis_index("tensor"), 2)
    tile = min(width, TILE)
    def run(mine):
        for pair in range(count // 2):
            which = 0 if 4 * pair < count else 1
            local = 2 * pair - which * (count // 2)
            for kind in range(2):
                base = (local + (mine if kind else 1 - mine)) * width
                for at in range(0, width, tile):
                    cols = slice(base + at, base + at + tile)
                    total = sum(dot(hids[2 * b + which][...], downs[b][:, cols], TN) for b in range(3))
                    here = slice(pair * width + at, pair * width + at + tile)
                    for part in range(2):
                        rows = slice(part * tokens_half, (part + 1) * tokens_half)
                        out = outs[2 * part + kind]
                        out[:, here] = total[rows].astype(out.dtype)

    either(mine, run)


def halved(bit, width, keep, got, send, left):
    mine = lax.rem(lax.div(lax.axis_index("tensor"), bit), 2)
    tile = min(width, TILE)

    def run(mine):
        for block in range(left.shape[1] // width):
            for kind, out in enumerate((send, left)):
                base = (2 * block + (mine if kind else 1 - mine)) * width
                for at in range(0, width, tile):
                    cols = slice(base + at, base + at + tile)
                    here = slice(block * width + at, block * width + at + tile)
                    out[:, here] = (keep[:, cols] + got[:, cols].astype(F32)).astype(out.dtype)

    either(mine, run)


def final_output(keep_a, got_a, keep_b, got_b, out):
    part = keep_a.shape[0]
    out[:part, :] = (keep_a[...] + got_a[...].astype(F32)).astype(BF)
    out[part:, :] = (keep_b[...] + got_b[...].astype(F32)).astype(BF)


def exchanged(value, axis, bit):
    count = lax.axis_size(axis)
    return lax.ppermute(value, axis, [(source, source ^ bit) for source in range(count)])


def ring_passed(value, steps):
    count = lax.axis_size("section")
    return lax.ppermute(value, "section", [(source, (source + steps) % count) for source in range(count)])


def packed_weights(gate, up, down):
    half = gate.shape[1] // 2
    low = jnp.concatenate([gate[:, :half], up[:, :half]], 0)
    low, gate, up = lax.optimization_barrier((low, gate, up))
    high = jnp.concatenate([gate[:, half:], up[:, half:]], 0)
    high, down = lax.optimization_barrier((high, down))
    return low, high, jnp.concatenate([down[:, :half], down[:, half:]], 0)


def on_device(x, g, gate_weight, up_weight, down_weight):
    rows, wide = gate_weight.shape
    half, both_rows, tokens = wide // 2, 2 * rows, x.shape[0]
    count = lax.axis_size("tensor")
    four = lax.axis_size("section") == 4
    piece = ((both_rows, half), BF)
    step = Steps()
    small, small_bf = ((both_rows, tokens), F32), ((both_rows, tokens), BF)

    def one_hop(value):
        return exchanged(value, "section", 2) if four else ring_passed(value, 1)

    def relay(here, value):
        if not four:
            return ring_passed(here, 1)
        return exchanged(step(picked, piece, [here, value]), "section", 1)

    own = packed_weights(gate_weight, up_weight, down_weight)
    first = [one_hop(value) for value in own]
    second = [None] * 3
    both_own, *hid_own = step(project, [small, small_bf, small_bf], [x, own[0], own[1]])
    pair_own = step(derive, small_bf, [g, own[2], both_own])
    grads_f32 = [((both_rows, half), F32)] * 3
    own_low, own_high, own_down = step(own_grads, grads_f32, [x, g, *hid_own, pair_own])
    second[0] = relay(first[0], own[0])
    second[1] = relay(first[1], own[1])
    both_first, *hid_first = step(project, [small, small_bf, small_bf], [x, first[0], first[1]])
    second[2] = relay(first[2], own[2])
    pair_first = step(derive, small_bf, [g, first[2], both_first], also=[second[0]])
    both_second, *hid_second = step(project, [small, small_bf, small_bf], [x, second[0], second[1]])

    def outward(value):
        return exchanged(value, "section", 1) if four else ring_passed(value, -1)

    def backward(value):
        return exchanged(value, "section", 2) if four else ring_passed(value, -1)

    far = hid_second if four else hid_first
    tail = step(sent_down, piece, [g, *far])
    side_down = outward(tail)

    part = tokens // 2
    if count & (count - 1) == 0 and count > 1:
        shapes = [((part, wide // 2), BF), ((part, wide // 2), F32)] * 2
        hids = [*hid_own, *hid_first, *hid_second]

        def sums(*refs):
            output_sums(count, part, *refs)

        send_a, keep_a, send_b, keep_b = step(sums, shapes, [*hids, own[2], first[2], second[2]])
        got_a, got_b = exchanged(send_a, "tensor", 1), exchanged(send_b, "tensor", 1)
    pair_second = step(derive, small_bf, [g, second[2], both_second])
    far = pair_second if four else pair_first
    near = pair_first if four else pair_second
    near_hid = hid_first if four else hid_second
    low, high = step(sent_pair, [piece, piece], [x, far])
    side_low, side_high = outward(low), outward(high)

    width = wide // count

    def next_half(keep, got, bit):
        cols = keep.shape[1] // 2

        def body(*refs):
            halved(bit, width, *refs)

        send, keep = step(body, [((part, cols), BF), ((part, cols), F32)], [keep, got])
        return exchanged(send, "tensor", bit), keep

    def back_down(gr, a, b, side, out):
        odd = is_odd()
        for at in range(0, half, TILE):
            value = down_columns(gr, a, b, at, half) + kept(side[:, at : at + TILE], odd, four, True)
            out[:, at : at + TILE] = value.astype(BF)

    def back_pair(offset):
        def body(xr, pair, side, out):
            odd = is_odd()
            for at in range(0, half, TILE):
                value = dot(pair[...], xr[:, offset + at : offset + at + TILE], NN)
                value += kept(side[:, at : at + TILE], odd, four, True)
                out[:, at : at + TILE] = value.astype(BF)

        return body

    got_a, keep_a = next_half(keep_a, got_a, 2)
    got_b, keep_b = next_half(keep_b, got_b, 2)
    last = step(back_down, piece, [g, *near_hid, side_down])
    back_of_down = backward(last)
    bit = 4
    got_a, keep_a = next_half(keep_a, got_a, bit)
    last = step(back_pair(0), piece, [x, near, side_low])
    back_of_low = backward(last)
    got_b, keep_b = next_half(keep_b, got_b, bit)
    last = step(back_pair(half), piece, [x, near, side_high], also=[got_a])
    back_of_high = backward(last)
    bit *= 2
    while bit < count:
        got_a, keep_a = next_half(keep_a, got_a, bit)
        got_b, keep_b = next_half(keep_b, got_b, bit)
        bit *= 2

    def finished(own_ref, back, side, odd, cut):
        value = own_ref[:, cut] + back[:, cut].astype(F32)
        return value + kept(side[:, cut], odd, four, False) if four else value

    def final_down(own_ref, back, side, out):
        odd = is_odd()
        for at in range(0, half, TILE):
            cut = slice(at, at + TILE)
            value = finished(own_ref, back, side, odd, cut)
            out[:, cut] = value[:rows]
            out[:, half + at : half + at + TILE] = value[rows:]

    def final_pair(low_ref, high_ref, low_back, high_back, low_side, high_side, out_gate, out_up):
        odd = is_odd()
        for offset, refs in ((0, (low_ref, low_back, low_side)), (half, (high_ref, high_back, high_side))):
            for at in range(0, half, TILE):
                value = finished(*refs, odd, slice(at, at + TILE))
                out_gate[:, offset + at : offset + at + TILE] = value[:rows]
                out_up[:, offset + at : offset + at + TILE] = value[rows:]

    whole = ((rows, wide), F32)
    grad_down = step(final_down, whole, [own_down, back_of_down, side_down])
    output = step(final_output, ((tokens, width), BF), [keep_a, got_a, keep_b, got_b])
    grad_gate, grad_up = step(
        final_pair, [whole, whole], [own_low, own_high, back_of_low, back_of_high, side_low, side_high]
    )
    return (output, grad_gate, grad_up, grad_down)


def solution(mesh):
    placed = (
        P("section", None),
        P("section", None),
        P(("section", "tensor"), None),
        P(("section", "tensor"), None),
        P(("section", "tensor"), None),
    )
    return jax.shard_map(
        on_device,
        mesh=mesh,
        in_specs=placed,
        out_specs=(
            P("section", "tensor"),
            P(("section", "tensor"), None),
            P(("section", "tensor"), None),
            P(("section", "tensor"), None),
        ),
        check_vma=False,
    )
```

```python
import jax
import jax.numpy as jnp
from jax import lax
from jax.experimental import pallas as pl
from jax.experimental.pallas import tpu as pltpu
from jax.sharding import PartitionSpec as P

BF = jnp.bfloat16
F32 = jnp.float32
NN = (((1,), (0,)), ((), ()))
NT = (((1,), (1,)), ((), ()))
TN = (((0,), (0,)), ((), ()))
TILE = 512


def dot(left, right, dims):
    return lax.dot_general(left, right, dims, preferred_element_type=F32)


class Steps:
    def __init__(self):
        self.mark = None

    def __call__(self, body, outs, ins, also=()):
        marks = [*also] if self.mark is None else [*also, self.mark]
        count = len(ins)

        def kernel(*refs):
            body(*refs[:count], *refs[count + len(marks) : -1])
            refs[-1][...] = jnp.zeros_like(refs[-1])

        single = isinstance(outs, tuple)
        shapes = ([outs] if single else list(outs)) + [((8, 128), F32)]
        *got, self.mark = pl.pallas_call(
            kernel,
            out_shape=[jax.ShapeDtypeStruct(*s) for s in shapes],
            in_specs=[pl.BlockSpec(memory_space=pltpu.VMEM)] * (count + len(marks)),
            out_specs=[pl.BlockSpec(memory_space=pltpu.VMEM)] * len(shapes),
            compiler_params=pltpu.CompilerParams(vmem_limit_bytes=24 * 1024 * 1024),
            cost_estimate=pl.CostEstimate(flops=1, bytes_accessed=1, transcendentals=0),
        )(*ins, *marks)
        return got[0] if single else got


def is_odd():
    return lax.rem(lax.axis_index("section"), 2) == 1


def packed(gate, up, down, low, high, both):
    rows, half = gate.shape[0], low.shape[1]
    shape = (2 * rows, rows)
    place = lax.broadcasted_iota(jnp.int32, shape, 0) - lax.broadcasted_iota(jnp.int32, shape, 1)
    top, bottom = ((place == shift).astype(F32).astype(BF) for shift in (0, rows))
    for out, upper, lower, a, b in ((high, gate, up, half, half), (low, gate, up, 0, 0), (both, down, down, 0, half)):
        for at in range(0, half, TILE):
            value = dot(top, upper[:, a + at : a + at + TILE], NN) + dot(bottom, lower[:, b + at : b + at + TILE], NN)
            out[:, at : at + TILE] = value.astype(BF)


def project(x, low, high, both, hid_a, hid_b):
    rows, half = low.shape[0] // 2, low.shape[1]
    total = jnp.zeros(both.shape, F32)
    for at in range(0, half, 1024):
        cut = slice(at, at + 1024)
        total += dot(low[:, cut], x[:, cut], NT)
        total += dot(high[:, cut], x[:, half + at : half + at + 1024], NT)
    both[...] = total
    up = pltpu.roll(total, rows, 0)
    hidden = total * jax.nn.sigmoid(total) * up
    first = lax.broadcasted_iota(jnp.int32, total.shape, 0) < rows
    hidden = jnp.where(first, hidden, 0.0)
    hid_a[...] = hidden.astype(BF)
    hid_b[...] = pltpu.roll(hidden, rows, 0).astype(BF)


def derive(g, down, both, pair):
    rows, half = down.shape[0] // 2, down.shape[1]
    low = jnp.zeros(both.shape, F32)
    high = jnp.zeros(both.shape, F32)
    for at in range(0, half, 1024):
        cut = slice(at, at + 1024)
        low += dot(down[:, cut], g[:, cut], NT)
        high += dot(down[:, cut], g[:, half + at : half + at + 1024], NT)
    dhid = low + pltpu.roll(high, rows, 0)
    gate = both[...]
    up = pltpu.roll(gate, rows, 0)
    sig = jax.nn.sigmoid(gate)
    dgate = dhid * up * sig * (1.0 + gate * (1.0 - sig))
    dup = pltpu.roll(dhid * (gate * sig), rows, 0)
    first = lax.broadcasted_iota(jnp.int32, gate.shape, 0) < rows
    pair[...] = jnp.where(first, dgate, dup).astype(BF)


def down_columns(g, hid_a, hid_b, at, half):
    cut = slice(at, at + TILE)
    return dot(hid_a[...], g[:, cut], NN) + dot(hid_b[...], g[:, half + at : half + at + TILE], NN)


def own_grads(x, g, hid_a, hid_b, pair, low, high, down):
    half = low.shape[1]
    for at in range(0, half, TILE):
        cut = slice(at, at + TILE)
        low[:, cut] = dot(pair[...], x[:, cut], NN)
        high[:, cut] = dot(pair[...], x[:, half + at : half + at + TILE], NN)
        down[:, cut] = down_columns(g, hid_a, hid_b, at, half)


def sent_down(g, hid_a, hid_b, out):
    half = out.shape[1]
    for at in range(0, half, TILE):
        out[:, at : at + TILE] = down_columns(g, hid_a, hid_b, at, half).astype(BF)


def sent_pair(x, pair, low, high):
    half = low.shape[1]
    for at in range(0, half, TILE):
        cut = slice(at, at + TILE)
        low[:, cut] = dot(pair[...], x[:, cut], NN).astype(BF)
        high[:, cut] = dot(pair[...], x[:, half + at : half + at + TILE], NN).astype(BF)


def kept(side, odd, four, wanted):
    value = side.astype(F32)
    return jnp.where(odd == wanted, value, 0.0) if four else value


def either(bit, run):
    for value in range(2):
        pl.when(bit == value)(lambda value=value: run(value))


def picked(here, piece, out):
    @pl.when(is_odd())
    def _():
        out[...] = here[...]

    @pl.when(jnp.logical_not(is_odd()))
    def _():
        out[...] = piece[...]


def output_sums(count, tokens_half, *refs):
    hids, downs, outs = refs[:6], refs[6:9], refs[9:]
    half = downs[0].shape[1]
    width = 2 * half // count
    mine = lax.rem(lax.axis_index("tensor"), 2)
    tile = min(width, TILE)
    def run(mine):
        for pair in range(count // 2):
            which = 0 if 4 * pair < count else 1
            local = 2 * pair - which * (count // 2)
            for kind in range(2):
                base = (local + (mine if kind else 1 - mine)) * width
                for at in range(0, width, tile):
                    cols = slice(base + at, base + at + tile)
                    total = sum(dot(hids[2 * b + which][...], downs[b][:, cols], TN) for b in range(3))
                    here = slice(pair * width + at, pair * width + at + tile)
                    for part in range(2):
                        rows = slice(part * tokens_half, (part + 1) * tokens_half)
                        out = outs[2 * part + kind]
                        out[:, here] = total[rows].astype(out.dtype)

    either(mine, run)


def halved(bit, width, keep, got, send, left):
    mine = lax.rem(lax.div(lax.axis_index("tensor"), bit), 2)
    tile = min(width, TILE)

    def run(mine):
        for block in range(left.shape[1] // width):
            for kind, out in enumerate((send, left)):
                base = (2 * block + (mine if kind else 1 - mine)) * width
                for at in range(0, width, tile):
                    cols = slice(base + at, base + at + tile)
                    here = slice(block * width + at, block * width + at + tile)
                    out[:, here] = (keep[:, cols] + got[:, cols].astype(F32)).astype(out.dtype)

    either(mine, run)


def final_output(keep_a, got_a, keep_b, got_b, out):
    part = keep_a.shape[0]
    out[:part, :] = (keep_a[...] + got_a[...].astype(F32)).astype(BF)
    out[part:, :] = (keep_b[...] + got_b[...].astype(F32)).astype(BF)


def exchanged(value, axis, bit):
    count = lax.axis_size(axis)
    return lax.ppermute(value, axis, [(source, source ^ bit) for source in range(count)])


def ring_passed(value, steps):
    count = lax.axis_size("section")
    return lax.ppermute(value, "section", [(source, (source + steps) % count) for source in range(count)])


def on_device(x, g, gate_weight, up_weight, down_weight):
    rows, wide = gate_weight.shape
    half, both_rows, tokens = wide // 2, 2 * rows, x.shape[0]
    count = lax.axis_size("tensor")
    four = lax.axis_size("section") == 4
    piece = ((both_rows, half), BF)
    step = Steps()
    small, small_bf = ((both_rows, tokens), F32), ((both_rows, tokens), BF)

    def one_hop(value):
        return exchanged(value, "section", 2) if four else ring_passed(value, 1)

    def relay(here, value):
        if not four:
            return ring_passed(here, 1)
        return exchanged(step(picked, piece, [here, value]), "section", 1)

    own = step(packed, [piece] * 3, [gate_weight, up_weight, down_weight])
    first = [one_hop(value) for value in own]
    second = [None] * 3
    both_own, *hid_own = step(project, [small, small_bf, small_bf], [x, own[0], own[1]])
    pair_own = step(derive, small_bf, [g, own[2], both_own])
    grads_f32 = [((both_rows, half), F32)] * 3
    own_low, own_high, own_down = step(own_grads, grads_f32, [x, g, *hid_own, pair_own])
    second[1] = relay(first[1], own[1])
    second[0] = relay(first[0], own[0])
    both_first, *hid_first = step(project, [small, small_bf, small_bf], [x, first[0], first[1]])
    second[2] = relay(first[2], own[2])
    pair_first = step(derive, small_bf, [g, first[2], both_first], also=[second[1]])
    both_second, *hid_second = step(project, [small, small_bf, small_bf], [x, second[0], second[1]])

    def outward(value):
        return exchanged(value, "section", 1) if four else ring_passed(value, -1)

    def backward(value):
        return exchanged(value, "section", 2) if four else ring_passed(value, -1)

    far = hid_second if four else hid_first
    tail = step(sent_down, piece, [g, *far])
    side_down = outward(tail)

    part = tokens // 2
    if count & (count - 1) == 0 and count > 1:
        shapes = [((part, wide // 2), BF), ((part, wide // 2), F32)] * 2
        hids = [*hid_own, *hid_first, *hid_second]

        def sums(*refs):
            output_sums(count, part, *refs)

        send_a, keep_a, send_b, keep_b = step(sums, shapes, [*hids, own[2], first[2], second[2]])
        got_a, got_b = exchanged(send_a, "tensor", 1), exchanged(send_b, "tensor", 1)
    pair_second = step(derive, small_bf, [g, second[2], both_second])
    far = pair_second if four else pair_first
    near = pair_first if four else pair_second
    near_hid = hid_first if four else hid_second
    low, high = step(sent_pair, [piece, piece], [x, far])
    side_low, side_high = outward(low), outward(high)

    width = wide // count

    def next_half(keep, got, bit, also=()):
        cols = keep.shape[1] // 2

        def body(*refs):
            halved(bit, width, *refs)

        send, keep = step(body, [((part, cols), BF), ((part, cols), F32)], [keep, got], also)
        return exchanged(send, "tensor", bit), keep

    def back_down(gr, a, b, side, out):
        odd = is_odd()
        for at in range(0, half, TILE):
            value = down_columns(gr, a, b, at, half) + kept(side[:, at : at + TILE], odd, four, True)
            out[:, at : at + TILE] = value.astype(BF)

    def back_pair(offset):
        def body(xr, pair, side, out):
            odd = is_odd()
            for at in range(0, half, TILE):
                value = dot(pair[...], xr[:, offset + at : offset + at + TILE], NN)
                value += kept(side[:, at : at + TILE], odd, four, True)
                out[:, at : at + TILE] = value.astype(BF)

        return body

    got_a, keep_a = next_half(keep_a, got_a, 2)
    got_b, keep_b = next_half(keep_b, got_b, 2)
    last = step(back_down, piece, [g, *near_hid, side_down])
    back_of_down = backward(last)
    bit = 4
    got_a, keep_a = next_half(keep_a, got_a, bit)
    last = step(back_pair(0), piece, [x, near, side_low])
    back_of_low = backward(last)
    got_b, keep_b = next_half(keep_b, got_b, bit, [back_of_down])
    last = step(back_pair(half), piece, [x, near, side_high], also=[got_a])
    back_of_high = backward(last)
    bit *= 2
    while bit < count:
        got_a, keep_a = next_half(keep_a, got_a, bit)
        got_b, keep_b = next_half(keep_b, got_b, bit)
        bit *= 2

    def finished(own_ref, back, side, odd, cut):
        value = own_ref[:, cut] + back[:, cut].astype(F32)
        return value + kept(side[:, cut], odd, four, False) if four else value

    def final_down(own_ref, back, side, out):
        odd = is_odd()
        for at in range(0, half, TILE):
            cut = slice(at, at + TILE)
            value = finished(own_ref, back, side, odd, cut)
            out[:, cut] = value[:rows]
            out[:, half + at : half + at + TILE] = value[rows:]

    def final_pair(low_ref, high_ref, low_back, high_back, low_side, high_side, out_gate, out_up):
        odd = is_odd()
        for offset, refs in ((0, (low_ref, low_back, low_side)), (half, (high_ref, high_back, high_side))):
            for at in range(0, half, TILE):
                value = finished(*refs, odd, slice(at, at + TILE))
                out_gate[:, offset + at : offset + at + TILE] = value[:rows]
                out_up[:, offset + at : offset + at + TILE] = value[rows:]

    whole = ((rows, wide), F32)
    grad_down = step(final_down, whole, [own_down, back_of_down, side_down])
    output = step(final_output, ((tokens, width), BF), [keep_a, got_a, keep_b, got_b])
    grad_gate, grad_up = step(
        final_pair, [whole, whole], [own_low, own_high, back_of_low, back_of_high, side_low, side_high]
    )
    return (output, grad_gate, grad_up, grad_down)


def solution(mesh):
    placed = (
        P("section", None),
        P("section", None),
        P(("section", "tensor"), None),
        P(("section", "tensor"), None),
        P(("section", "tensor"), None),
    )
    return jax.shard_map(
        on_device,
        mesh=mesh,
        in_specs=placed,
        out_specs=(
            P("section", "tensor"),
            P(("section", "tensor"), None),
            P(("section", "tensor"), None),
            P(("section", "tensor"), None),
        ),
        check_vma=False,
    )
```

```python
import jax
import jax.numpy as jnp
from jax import lax
from jax.experimental import pallas as pl
from jax.experimental.pallas import tpu as pltpu
from jax.sharding import PartitionSpec as P

BF = jnp.bfloat16
F32 = jnp.float32
NN = (((1,), (0,)), ((), ()))
NT = (((1,), (1,)), ((), ()))
TN = (((0,), (0,)), ((), ()))
TILE = 512
SWAP = 4


def dot(left, right, dims):
    return lax.dot_general(left, right, dims, preferred_element_type=F32)


class Steps:
    def __init__(self):
        self.mark = None

    def __call__(self, body, outs, ins, also=(), far=0, scratch=()):
        marks = [*also] if self.mark is None else [*also, self.mark]
        count = len(ins)
        ins = [pltpu.with_memory_space_constraint(v, pltpu.HBM) if k < far else v for k, v in enumerate(ins)]

        def kernel(*refs):
            last = count + len(marks) + len(shapes)
            body(*refs[:count], *refs[count + len(marks) : last - 1], *refs[last:])
            refs[last - 1][...] = jnp.zeros_like(refs[last - 1])

        single = isinstance(outs, tuple)
        shapes = ([outs] if single else list(outs)) + [((8, 128), F32)]
        *got, self.mark = pl.pallas_call(
            kernel,
            out_shape=[jax.ShapeDtypeStruct(*s) for s in shapes],
            in_specs=[pl.BlockSpec(memory_space=pltpu.HBM)] * far
            + [pl.BlockSpec(memory_space=pltpu.VMEM)] * (count + len(marks) - far),
            out_specs=[pl.BlockSpec(memory_space=pltpu.VMEM)] * len(shapes),
            scratch_shapes=list(scratch),
            compiler_params=pltpu.CompilerParams(vmem_limit_bytes=24 * 1024 * 1024),
            cost_estimate=pl.CostEstimate(flops=1, bytes_accessed=1, transcendentals=0),
        )(*ins, *marks)
        return got[0] if single else got


def is_odd():
    return lax.rem(lax.axis_index("section"), 2) == 1


def either(bit, run):
    for value in range(2):
        pl.when(bit == value)(lambda value=value: run(value))


def tensor_bit(bit):
    return lax.rem(lax.div(lax.axis_index("tensor"), bit), 2)


def is_odd():
    return lax.rem(lax.axis_index("section"), 2) == 1


def top_rows(like):
    return lax.broadcasted_iota(jnp.int32, like.shape, 0) < like.shape[0] // 2


def placed(rows):
    shape = (2 * rows, rows)
    place = lax.broadcasted_iota(jnp.int32, shape, 0) - lax.broadcasted_iota(jnp.int32, shape, 1)
    return [(place == shift).astype(F32).astype(BF) for shift in (0, rows)]


def stacked(out, upper, lower, upper_at=0, lower_at=0):
    top, bottom = placed(upper.shape[0])
    for at in range(0, out.shape[1], TILE):
        first, second = slice(upper_at + at, upper_at + at + TILE), slice(lower_at + at, lower_at + at + TILE)
        out[:, at : at + TILE] = (dot(top, upper[:, first], NN) + dot(bottom, lower[:, second], NN)).astype(BF)


def runs(width, wide):
    return [(SWAP * width * j, 2 * SWAP * width * j) for j in range(wide // (2 * SWAP * width))]


def packed(width, gate, up, down, high, low, keep, send, gate_here, up_here, down_here, sems):
    copies = [
        pltpu.make_async_copy(there, here, sems.at[k])
        for k, (there, here) in enumerate(((gate, gate_here), (up, up_here), (down, down_here)))
    ]
    for copy in copies:
        copy.start()
    half = high.shape[1]
    copies[0].wait()
    copies[1].wait()
    stacked(high, gate_here, up_here, half, half)
    stacked(low, gate_here, up_here)
    copies[2].wait()

    def run(mine):
        for near, there in runs(width, 2 * half):
            here = slice(near, near + SWAP * width)
            for out, which in ((keep, mine), (send, 1 - mine)):
                at = there + SWAP * width * which
                out[:, here] = down_here[:, at : at + SWAP * width]

    either(tensor_bit(SWAP), run)


def project_tiles(x, low, high):
    half = low.shape[1]
    tile = min(half, 1024)
    total = jnp.zeros((low.shape[0], x.shape[0]), F32)
    for at in range(0, half, tile):
        cut = slice(at, at + tile)
        total += dot(low[:, cut], x[:, cut], NT)
        total += dot(high[:, cut], x[:, half + at : half + at + tile], NT)
    return total


def project(x, low, high, both, hid_a, hid_b):
    rows = low.shape[0] // 2
    total = project_tiles(x, low, high)
    both[...] = total
    hidden = total * jax.nn.sigmoid(total) * pltpu.roll(total, rows, 0)
    hidden = jnp.where(top_rows(total), hidden, 0.0)
    hid_a[...] = hidden.astype(BF)
    hid_b[...] = pltpu.roll(hidden, rows, 0).astype(BF)


def project_first(x_there, g_there, low, high, x, g, both, hid_a, hid_b, sems):
    copies = [pltpu.make_async_copy(x_there, x, sems.at[0]), pltpu.make_async_copy(g_there, g, sems.at[1])]
    for copy in copies:
        copy.start()
    copies[0].wait()
    project(x, low, high, both, hid_a, hid_b)
    copies[1].wait()


def part_of(width, g, down, hid_b, part, out):
    rows, wide = down.shape[0] // 2, g.shape[1]
    tile = min(SWAP * width, 1024)

    def run(mine):
        total = jnp.zeros(part.shape, F32)
        for near, there in runs(width, wide):
            for at in range(0, SWAP * width, tile):
                far = there + SWAP * width * mine + at
                total += dot(down[:, near + at : near + at + tile], g[:, far : far + tile], NT)
        part[...] = total
        out[...] = jnp.where(top_rows(total), pltpu.roll(total, rows, 0), hid_b[...].astype(F32))

    either(tensor_bit(SWAP), run)


def finish(both, part, got, hid_a, pair, hid_pair):
    rows = both.shape[0] // 2
    gate, got = both[...], got[...]
    dhid = part[...] + got
    sig = jax.nn.sigmoid(gate)
    dgate = dhid * pltpu.roll(gate, rows, 0) * sig * (1.0 + gate * (1.0 - sig))
    dup = pltpu.roll(dhid * (gate * sig), rows, 0)
    first = top_rows(gate)
    pair[...] = jnp.where(first, dgate, dup).astype(BF)
    hid_pair[...] = jnp.where(first, hid_a[...].astype(F32), got).astype(BF)


def down_columns(g, hid_a, hid_b, at, half):
    cut = slice(at, at + TILE)
    return dot(hid_a[...], g[:, cut], NN) + dot(hid_b[...], g[:, half + at : half + at + TILE], NN)


def tiles(size):
    return [slice(at, min(at + TILE, size)) for at in range(0, size, TILE)]


def shifted(cut, offset):
    return slice(cut.start + offset, cut.stop + offset)


def own_grads(x, g, hid_a, hid_b, pair, low, high, down):
    half = down.shape[1]
    for out, offset in ((low, 0), (high, low.shape[1])):
        for cut in tiles(out.shape[1]):
            out[:, cut] = dot(pair[...], x[:, shifted(cut, offset)], NN)
    for at in range(0, half, TILE):
        down[:, at : at + TILE] = down_columns(g, hid_a, hid_b, at, half)


def sent_down(g, hid_a, hid_b, out):
    half = out.shape[1]
    for at in range(0, half, TILE):
        out[:, at : at + TILE] = down_columns(g, hid_a, hid_b, at, half).astype(BF)


def sent_pair(x, pair, low, high):
    for out, offset in ((low, 0), (high, low.shape[1])):
        for cut in tiles(out.shape[1]):
            out[:, cut] = dot(pair[...], x[:, shifted(cut, offset)], NN).astype(BF)


def kept(side, odd, four, wanted):
    value = side.astype(F32)
    return jnp.where(odd == wanted, value, 0.0) if four else value


def picked(here, piece, out):
    @pl.when(is_odd())
    def _():
        out[...] = here[...]

    @pl.when(jnp.logical_not(is_odd()))
    def _():
        out[...] = piece[...]


def output_sums(width, *refs):
    hids, downs, (send_a, send_b, keep) = refs[:3], refs[3:6], refs[6:]
    part = send_a.shape[0]
    tile = min(width, TILE)

    def run(mine):
        for block in range(keep.shape[1] // width):
            for which in range(2):
                for at in range(0, width, tile):
                    cols = slice((2 * block + which) * width + at, (2 * block + which) * width + at + tile)
                    here = slice(block * width + at, block * width + at + tile)
                    total = sum(dot(hid[...], down[:, cols], TN) for hid, down in zip(hids, downs))
                    if which == mine:
                        keep[:, here] = total
                    else:
                        send_a[:, here] = total[:part].astype(BF)
                        send_b[:, here] = total[part:].astype(BF)

    either(tensor_bit(1), run)


def halved(bit, width, keep, *refs):
    got, (send, left) = refs[:-2], refs[-2:]
    tile = min(width, TILE)
    part = keep.shape[0] // len(got)

    def run(mine):
        for block in range(left.shape[1] // width):
            for out, which in ((send, 1 - mine), (left, mine)):
                for at in range(0, width, tile):
                    cols = slice((2 * block + which) * width + at, (2 * block + which) * width + at + tile)
                    here = slice(block * width + at, block * width + at + tile)
                    for k, piece in enumerate(got):
                        rows = slice(k * part, (k + 1) * part)
                        out[rows, here] = (keep[rows, cols] + piece[:, cols].astype(F32)).astype(out.dtype)

    either(tensor_bit(bit), run)


def final_output(keep, *refs):
    got, out = refs[:-1], refs[-1]
    part = keep.shape[0] // len(got)
    for k, piece in enumerate(got):
        rows = slice(k * part, (k + 1) * part)
        out[rows, :] = (keep[rows, :] + piece[...].astype(F32)).astype(BF)


def exchanged(value, axis, bit):
    count = lax.axis_size(axis)
    return lax.ppermute(value, axis, [(source, source ^ bit) for source in range(count)])


def ring_passed(value, steps):
    count = lax.axis_size("section")
    return lax.ppermute(value, "section", [(source, (source + steps) % count) for source in range(count)])


def on_device(x, g, gate_weight, up_weight, down_weight):
    rows, wide = gate_weight.shape
    half, both_rows, tokens = wide // 2, 2 * rows, x.shape[0]
    count = lax.axis_size("tensor")
    assert count > SWAP and count & (count - 1) == 0
    width = wide // count
    four = lax.axis_size("section") == 4
    piece, narrow = ((both_rows, half), BF), ((rows, half), BF)
    small, small_bf = ((both_rows, tokens), F32), ((both_rows, tokens), BF)
    step = Steps()

    def with_width(body):
        def run(*refs):
            body(width, *refs)

        return run

    def one_hop(value):
        return exchanged(value, "section", 2) if four else ring_passed(value, 1)

    def relay(here, value):
        if not four:
            return ring_passed(here, 1)
        return exchanged(step(picked, piece, [here, value]), "section", 1)

    def outward(value):
        return exchanged(value, "section", 1) if four else ring_passed(value, -1)

    def backward(value):
        return exchanged(value, "section", 2) if four else ring_passed(value, -1)

    own, first, second = [None] * 3, [None] * 3, [None] * 3
    held = pltpu.VMEM((rows, wide), BF)
    own[1], own[0], down_keep, down_send = step(
        with_width(packed),
        [piece, piece, narrow, narrow],
        [gate_weight, up_weight, down_weight],
        far=3,
        scratch=[held, held, held, pltpu.SemaphoreType.DMA((3,))],
    )
    first[1] = one_hop(own[1])
    first[0] = one_hop(own[0])
    down_got = exchanged(down_send, "tensor", SWAP)
    x, g, both_own, *hid_own = step(
        project_first,
        [(x.shape, BF), (g.shape, BF), small, small_bf, small_bf],
        [x, g, own[0], own[1]],
        far=2,
        scratch=[pltpu.SemaphoreType.DMA((2,))],
    )
    second[1] = relay(first[1], own[1])

    def joined(keep, got, out):
        stacked(out, keep, got)

    own[2] = step(joined, piece, [down_keep, down_got])
    first[2] = one_hop(own[2])
    part_own, part_out = step(with_width(part_of), [small, small], [g, own[2], hid_own[1]])
    second[0] = relay(first[0], own[0])
    both_first, *hid_first = step(project, [small, small_bf, small_bf], [x, first[0], first[1]], also=[second[1]])
    second[2] = relay(first[2], own[2])

    def part_two(gr, down, hid_b, earlier, part, out):
        out[:both_rows, :] = earlier[...]
        part_of(width, gr, down, hid_b, part, out.at[both_rows:, :])

    part_first, part_out = step(
        part_two, [small, ((2 * both_rows, tokens), F32)], [g, first[2], hid_first[1], part_out]
    )
    part_got = exchanged(part_out, "tensor", SWAP)
    both_second, *hid_second = step(project, [small, small_bf, small_bf], [x, second[0], second[1]])
    side_down = outward(step(sent_down, piece, [g, *hid_second]))

    def finish_two(both_a, part_a, hid_a, both_b, part_b, hid_b, got, pair_a, out_a, pair_b, out_b):
        finish(both_a, part_a, got.at[:both_rows, :], hid_a, pair_a, out_a)
        finish(both_b, part_b, got.at[both_rows:, :], hid_b, pair_b, out_b)

    pair_own, wide_own, pair_first, wide_first = step(
        finish_two, [small_bf] * 4, [both_own, part_own, hid_own[0], both_first, part_first, hid_first[0], part_got]
    )
    low_columns = half + 128
    low_shape, high_shape = (both_rows, low_columns), (both_rows, wide - low_columns)
    grads_f32 = [(low_shape, F32), (high_shape, F32), ((both_rows, half), F32)]
    own_low, own_high, own_down = step(own_grads, grads_f32, [x, g, *hid_own, pair_own])
    part_second, part_out = step(with_width(part_of), [small, small], [g, second[2], hid_second[1]])
    part_got = exchanged(part_out, "tensor", SWAP)
    pair_second, wide_second = step(finish, [small_bf] * 2, [both_second, part_second, part_got, hid_second[0]])
    low, high = step(sent_pair, [(low_shape, BF), (high_shape, BF)], [x, pair_second])
    side_low, side_high = outward(low), outward(high)

    def back_down(gr, a, b, side, out):
        odd = is_odd()
        for at in range(0, half, TILE):
            value = down_columns(gr, a, b, at, half) + kept(side[:, at : at + TILE], odd, four, True)
            out[:, at : at + TILE] = value.astype(BF)

    def back_pair(offset):
        def body(xr, pair, side, out):
            odd = is_odd()
            for cut in tiles(out.shape[1]):
                value = dot(pair[...], xr[:, shifted(cut, offset)], NN)
                out[:, cut] = (value + kept(side[:, cut], odd, four, True)).astype(BF)

        return body

    quarter = wide // 4
    send_a, send_b, keep = step(
        with_width(output_sums),
        [((tokens // 2, quarter), BF), ((tokens // 2, quarter), BF), ((tokens, quarter), F32)],
        [wide_own, wide_first, wide_second, own[2], first[2], second[2]],
    )
    back_of_down = backward(step(back_down, piece, [g, *hid_first, side_down]))
    got = [exchanged(send_a, "tensor", 1), exchanged(send_b, "tensor", 1)]

    def next_half(keep, got, bit):
        cols = keep.shape[1] // 2

        def body(*refs):
            halved(bit, width, *refs)

        send, keep = step(body, [((tokens, cols), BF), ((tokens, cols), F32)], [keep, *got])
        return keep, [exchanged(send, "tensor", bit)]

    keep, got = next_half(keep, got, 2)
    back_of_low = backward(step(back_pair(0), (low_shape, BF), [x, pair_first, side_low]))
    back_of_high = backward(step(back_pair(low_columns), (high_shape, BF), [x, pair_first, side_high], also=[back_of_down]))
    bit = 2 * SWAP
    while bit < count:
        keep, got = next_half(keep, got, bit)
        bit *= 2

    def finished(own_ref, back, side, odd, cut):
        value = own_ref[:, cut] + back[:, cut].astype(F32)
        return value + kept(side[:, cut], odd, four, False) if four else value

    def final_down(own_ref, back, side, out):
        odd = is_odd()
        for at in range(0, half, TILE):
            cut = slice(at, at + TILE)
            value = finished(own_ref, back, side, odd, cut)
            out[:, cut] = value[:rows]
            out[:, half + at : half + at + TILE] = value[rows:]

    def final_pair(low_ref, high_ref, low_back, high_back, low_side, high_side, out_gate, out_up):
        odd = is_odd()
        for offset, refs in ((0, (low_ref, low_back, low_side)), (low_columns, (high_ref, high_back, high_side))):
            for cut in tiles(refs[0].shape[1]):
                value = finished(*refs, odd, cut)
                out_gate[:, shifted(cut, offset)] = value[:rows]
                out_up[:, shifted(cut, offset)] = value[rows:]

    whole = ((rows, wide), F32)
    grad_down = step(final_down, whole, [own_down, back_of_down, side_down])
    output = step(final_output, ((tokens, width), BF), [keep, *got])
    grad_gate, grad_up = step(
        final_pair, [whole, whole], [own_low, own_high, back_of_low, back_of_high, side_low, side_high]
    )
    return (output, grad_gate, grad_up, grad_down)


def solution(mesh):
    placed = (
        P("section", None),
        P("section", None),
        P(("section", "tensor"), None),
        P(("section", "tensor"), None),
        P(("section", "tensor"), None),
    )
    return jax.shard_map(
        on_device,
        mesh=mesh,
        in_specs=placed,
        out_specs=(
            P("section", "tensor"),
            P(("section", "tensor"), None),
            P(("section", "tensor"), None),
            P(("section", "tensor"), None),
        ),
        check_vma=False,
    )
```

```python
import jax
import jax.numpy as jnp
from jax import lax
from jax.experimental import pallas as pl
from jax.experimental.pallas import tpu as pltpu
from jax.sharding import PartitionSpec as P

BF = jnp.bfloat16
F32 = jnp.float32
NN = (((1,), (0,)), ((), ()))
NT = (((1,), (1,)), ((), ()))
TN = (((0,), (0,)), ((), ()))
TILE = 512
SWAP = 1
BITS = (2, 4)


def dot(left, right, dims):
    return lax.dot_general(left, right, dims, preferred_element_type=F32)


class Steps:
    def __init__(self):
        self.mark = None

    def __call__(self, body, outs, ins, also=(), far=0, scratch=()):
        marks = [*also] if self.mark is None else [*also, self.mark]
        count = len(ins)
        ins = [pltpu.with_memory_space_constraint(v, pltpu.HBM) if k < far else v for k, v in enumerate(ins)]

        def kernel(*refs):
            last = count + len(marks) + len(shapes)
            body(*refs[:count], *refs[count + len(marks) : last - 1], *refs[last:])
            refs[last - 1][...] = jnp.zeros_like(refs[last - 1])

        single = isinstance(outs, tuple)
        shapes = ([outs] if single else list(outs)) + [((8, 128), F32)]
        *got, self.mark = pl.pallas_call(
            kernel,
            out_shape=[jax.ShapeDtypeStruct(*s) for s in shapes],
            in_specs=[pl.BlockSpec(memory_space=pltpu.HBM)] * far
            + [pl.BlockSpec(memory_space=pltpu.VMEM)] * (count + len(marks) - far),
            out_specs=[pl.BlockSpec(memory_space=pltpu.VMEM)] * len(shapes),
            scratch_shapes=list(scratch),
            compiler_params=pltpu.CompilerParams(vmem_limit_bytes=24 * 1024 * 1024),
            cost_estimate=pl.CostEstimate(flops=1, bytes_accessed=1, transcendentals=0),
        )(*ins, *marks)
        return got[0] if single else got


def is_odd():
    return lax.rem(lax.axis_index("section"), 2) == 1


def either(bit, run):
    for value in range(2):
        pl.when(bit == value)(lambda value=value: run(value))


def tensor_bit(bit):
    return lax.rem(lax.div(lax.axis_index("tensor"), bit), 2)


def is_odd():
    return lax.rem(lax.axis_index("section"), 2) == 1


def top_rows(like):
    return lax.broadcasted_iota(jnp.int32, like.shape, 0) < like.shape[0] // 2


def placed(rows):
    shape = (2 * rows, rows)
    place = lax.broadcasted_iota(jnp.int32, shape, 0) - lax.broadcasted_iota(jnp.int32, shape, 1)
    return [(place == shift).astype(F32).astype(BF) for shift in (0, rows)]


def stacked(out, upper, lower, upper_at=0, lower_at=0):
    top, bottom = placed(upper.shape[0])
    for at in range(0, out.shape[1], TILE):
        first, second = slice(upper_at + at, upper_at + at + TILE), slice(lower_at + at, lower_at + at + TILE)
        out[:, at : at + TILE] = (dot(top, upper[:, first], NN) + dot(bottom, lower[:, second], NN)).astype(BF)


def runs(width, wide):
    return [(SWAP * width * j, 2 * SWAP * width * j) for j in range(wide // (2 * SWAP * width))]


def packed(gate, up, down, high, low, both, gate_here, up_here, down_here, sems):
    copies = [
        pltpu.make_async_copy(there, here, sems.at[k])
        for k, (there, here) in enumerate(((gate, gate_here), (up, up_here), (down, down_here)))
    ]
    for copy in copies:
        copy.start()
    half = high.shape[1]
    copies[0].wait()
    copies[1].wait()
    stacked(high, gate_here, up_here, half, half)
    stacked(low, gate_here, up_here)
    copies[2].wait()
    stacked(both, down_here, down_here, 0, half)


def project_tiles(x, low, high):
    half = low.shape[1]
    tile = min(half, 1024)
    total = jnp.zeros((low.shape[0], x.shape[0]), F32)
    for at in range(0, half, tile):
        cut = slice(at, at + tile)
        total += dot(low[:, cut], x[:, cut], NT)
        total += dot(high[:, cut], x[:, half + at : half + at + tile], NT)
    return total


def project(x, low, high, both, hid_a, hid_b):
    rows = low.shape[0] // 2
    total = project_tiles(x, low, high)
    both[...] = total
    hidden = total * jax.nn.sigmoid(total) * pltpu.roll(total, rows, 0)
    hidden = jnp.where(top_rows(total), hidden, 0.0)
    hid_a[...] = hidden.astype(BF)
    hid_b[...] = pltpu.roll(hidden, rows, 0).astype(BF)


def project_first(x_there, g_there, low, high, x, g, both, hid_a, hid_b, sems):
    copies = [pltpu.make_async_copy(x_there, x, sems.at[0]), pltpu.make_async_copy(g_there, g, sems.at[1])]
    for copy in copies:
        copy.start()
    copies[0].wait()
    project(x, low, high, both, hid_a, hid_b)
    copies[1].wait()


def joined(width, ours, theirs, out):
    rows, half = ours.shape[0] // 2, ours.shape[1]
    shape = (2 * rows, 2 * rows)
    to, from_ = lax.broadcasted_iota(jnp.int32, shape, 0), lax.broadcasted_iota(jnp.int32, shape, 1)

    def moved(first_from, first_to):
        wanted = (to - first_to == from_ - first_from) & (to >= first_to) & (to < first_to + rows)
        return wanted.astype(F32).astype(BF)

    places = [(moved(start, 0), moved(start, rows)) for start in (0, rows)]
    tile = min(SWAP * width, TILE)

    def run(mine):
        for near, there in runs(width, 2 * half):
            for at in range(0, SWAP * width, tile):
                column = there + SWAP * width * mine + at
                cut = slice(column % half, column % half + tile)
                above, below = places[column // half]
                value = dot(above, ours[:, cut], NN) + dot(below, theirs[:, cut], NN)
                out[:, near + at : near + at + tile] = value.astype(BF)

    either(tensor_bit(SWAP), run)


def derive(g, down, both, pair):
    rows, half = down.shape[0] // 2, down.shape[1]
    tile = min(half, 1024)
    low = jnp.zeros(both.shape, F32)
    high = jnp.zeros(both.shape, F32)
    for at in range(0, half, tile):
        cut = slice(at, at + tile)
        low += dot(down[:, cut], g[:, cut], NT)
        high += dot(down[:, cut], g[:, half + at : half + at + tile], NT)
    dhid = low + pltpu.roll(high, rows, 0)
    gate = both[...]
    sig = jax.nn.sigmoid(gate)
    dgate = dhid * pltpu.roll(gate, rows, 0) * sig * (1.0 + gate * (1.0 - sig))
    dup = pltpu.roll(dhid * (gate * sig), rows, 0)
    pair[...] = jnp.where(top_rows(gate), dgate, dup).astype(BF)


def down_columns(g, hid_a, hid_b, at, half):
    cut = slice(at, at + TILE)
    return dot(hid_a[...], g[:, cut], NN) + dot(hid_b[...], g[:, half + at : half + at + TILE], NN)


def tiles(size):
    return [slice(at, min(at + TILE, size)) for at in range(0, size, TILE)]


def shifted(cut, offset):
    return slice(cut.start + offset, cut.stop + offset)


def own_grads(x, g, hid_a, hid_b, pair, low, high, down):
    half = down.shape[1]
    for out, offset in ((low, 0), (high, low.shape[1])):
        for cut in tiles(out.shape[1]):
            out[:, cut] = dot(pair[...], x[:, shifted(cut, offset)], NN)
    for at in range(0, half, TILE):
        down[:, at : at + TILE] = down_columns(g, hid_a, hid_b, at, half)


def sent_down(g, hid_a, hid_b, out):
    half = out.shape[1]
    for at in range(0, half, TILE):
        out[:, at : at + TILE] = down_columns(g, hid_a, hid_b, at, half).astype(BF)


def sent_pair(x, pair, low, high):
    for out, offset in ((low, 0), (high, low.shape[1])):
        for cut in tiles(out.shape[1]):
            out[:, cut] = dot(pair[...], x[:, shifted(cut, offset)], NN).astype(BF)


def kept(side, odd, four, wanted):
    value = side.astype(F32)
    return jnp.where(odd == wanted, value, 0.0) if four else value


def picked(here, piece, out):
    @pl.when(is_odd())
    def _():
        out[...] = here[...]

    @pl.when(jnp.logical_not(is_odd()))
    def _():
        out[...] = piece[...]


def output_sums(width, *refs):
    hids, downs, (send, keep) = refs[:3], refs[3:6], refs[6:]
    tile = min(width, TILE)

    def run(mine):
        for block in range(keep.shape[1] // width):
            for which in range(2):
                for at in range(0, width, tile):
                    cols = slice((2 * block + which) * width + at, (2 * block + which) * width + at + tile)
                    here = slice(block * width + at, block * width + at + tile)
                    total = sum(dot(hid, down[:, cols], TN) for hid, down in zip(hids, downs))
                    if which == mine:
                        keep[:, here] = total
                    else:
                        send[:, here] = total.astype(BF)

    either(tensor_bit(BITS[0]), run)


def halved(bit, width, keep, got, send, left):
    tile = min(width, TILE)

    def run(mine):
        for block in range(left.shape[1] // width):
            for out, which in ((send, 1 - mine), (left, mine)):
                for at in range(0, width, tile):
                    cols = slice((2 * block + which) * width + at, (2 * block + which) * width + at + tile)
                    value = keep[:, cols] + got[:, cols].astype(F32)
                    out[:, block * width + at : block * width + at + tile] = value.astype(out.dtype)

    either(tensor_bit(bit), run)


def final_output(keep, got, out, end):
    out[...] = (keep[...] + got[...].astype(F32)).astype(BF)
    end[...] = jnp.zeros_like(end)


def exchanged(value, axis, bit):
    count = lax.axis_size(axis)
    return lax.ppermute(value, axis, [(source, source ^ bit) for source in range(count)])


def ring_passed(value, steps):
    count = lax.axis_size("section")
    return lax.ppermute(value, "section", [(source, (source + steps) % count) for source in range(count)])


def on_device(x, g, gate_weight, up_weight, down_weight):
    rows, wide = gate_weight.shape
    half, both_rows, tokens = wide // 2, 2 * rows, x.shape[0]
    count = lax.axis_size("tensor")
    assert count > BITS[1] and count & (count - 1) == 0
    width = wide // count
    four = lax.axis_size("section") == 4
    piece = ((both_rows, half), BF)
    small, small_bf = ((both_rows, tokens), F32), ((both_rows, tokens), BF)
    step = Steps()

    def with_width(body):
        def run(*refs):
            body(width, *refs)

        return run

    def one_hop(value):
        return exchanged(value, "section", 2) if four else ring_passed(value, 1)

    def relay(here, value, also=()):
        if not four:
            return ring_passed(here, 1)
        return exchanged(step(picked, piece, [here, value], also), "section", 1)

    def outward(value):
        return exchanged(value, "section", 1) if four else ring_passed(value, -1)

    def backward(value):
        return exchanged(value, "section", 2) if four else ring_passed(value, -1)

    own, first, second = [None] * 3, [None] * 3, [None] * 3
    held = pltpu.VMEM((rows, wide), BF)
    own[1], own[0], own[2] = step(
        packed,
        [piece, piece, piece],
        [gate_weight, up_weight, down_weight],
        far=3,
        scratch=[held, held, held, pltpu.SemaphoreType.DMA((3,))],
    )
    first[1] = one_hop(own[1])
    first[0] = one_hop(own[0])
    first[2] = one_hop(own[2])
    theirs = [exchanged(own[2], "tensor", SWAP), None, None]
    x, g, both_own, *hid_own = step(
        project_first,
        [(x.shape, BF), (g.shape, BF), small, small_bf, small_bf],
        [x, g, own[0], own[1]],
        far=2,
        scratch=[pltpu.SemaphoreType.DMA((2,))],
    )
    pair_own = step(derive, small_bf, [g, own[2], both_own])
    low_columns = half + 128
    low_shape, high_shape = (both_rows, low_columns), (both_rows, wide - low_columns)
    grads_f32 = [(low_shape, F32), (high_shape, F32), ((both_rows, half), F32)]
    own_low, own_high, own_down = step(own_grads, grads_f32, [x, g, *hid_own, pair_own])
    second[1] = relay(first[1], own[1])

    second[0] = relay(first[0], own[0])
    second[2] = ring_passed(own[2] if four else first[2], 1)
    also = [second[1], second[2]] if four else [second[1]]
    both_first, *hid_first = step(project, [small, small_bf, small_bf], [x, first[0], first[1]], also=also)
    join = with_width(joined)
    wide_own = step(join, piece, [own[2], theirs[0]])
    theirs[2] = exchanged(second[2], "tensor", SWAP)
    wide_second = step(join, piece, [second[2], theirs[2]])
    pair_first = step(derive, small_bf, [g, first[2], both_first])
    both_second, *hid_second = step(project, [small, small_bf, small_bf], [x, second[0], second[1]])
    held_down, both_second = lax.optimization_barrier((first[2], both_second))
    theirs[1] = exchanged(held_down, "tensor", SWAP)
    side_down = outward(step(sent_down, piece, [g, *hid_second]))


    def hids_out(a, b, c, out):
        for k, hid in enumerate((a, b, c)):
            out[k * both_rows : (k + 1) * both_rows, :] = hid[...].astype(F32)

    hids = step(hids_out, ((3 * both_rows, tokens), F32), [hid_own[1], hid_first[1], hid_second[1]])
    hids_got = exchanged(hids, "tensor", SWAP)
    pair_second = step(derive, small_bf, [g, second[2], both_second])
    low, high = step(sent_pair, [(low_shape, BF), (high_shape, BF)], [x, pair_second])
    side_low, side_high = outward(low), outward(high)
    wide_first = step(join, piece, [first[2], theirs[1]])

    def back_down(gr, a, b, side, out):
        odd = is_odd()
        for at in range(0, half, TILE):
            value = down_columns(gr, a, b, at, half) + kept(side[:, at : at + TILE], odd, four, True)
            out[:, at : at + TILE] = value.astype(BF)

    def back_pair(offset):
        def body(xr, pair, side, out):
            odd = is_odd()
            for cut in tiles(out.shape[1]):
                value = dot(pair[...], xr[:, shifted(cut, offset)], NN)
                out[:, cut] = (value + kept(side[:, cut], odd, four, True)).astype(BF)

        return body

    quarter = wide // 4

    def sums(*refs):
        ours, theirs, downs = refs[:3], refs[3], refs[4:7]
        hids = [
            (ours[k][...].astype(F32) + theirs[k * both_rows : (k + 1) * both_rows, :]).astype(BF) for k in range(3)
        ]
        output_sums(width, *hids, *downs, *refs[7:])

    send, keep = step(
        sums,
        [((tokens, quarter), BF), ((tokens, quarter), F32)],
        [hid_own[0], hid_first[0], hid_second[0], hids_got, wide_own, wide_first, wide_second],
    )
    got = exchanged(send, "tensor", BITS[0])
    back_of_down = backward(step(back_down, piece, [g, *hid_first, side_down]))
    back_of_low = backward(step(back_pair(0), (low_shape, BF), [x, pair_first, side_low]))

    def next_half(keep, got, bit):
        cols = keep.shape[1] // 2

        def body(*refs):
            halved(bit, width, *refs)

        send, keep = step(body, [((tokens, cols), BF), ((tokens, cols), F32)], [keep, got])
        return keep, exchanged(send, "tensor", bit)

    keep, got = next_half(keep, got, BITS[1])
    back_of_high = backward(step(back_pair(low_columns), (high_shape, BF), [x, pair_first, side_high], also=[back_of_down]))
    bit = 2 * BITS[1]
    while bit < count:
        keep, got = next_half(keep, got, bit)
        bit *= 2

    def finished(own_ref, back, side, odd, cut):
        value = own_ref[:, cut] + back[:, cut].astype(F32)
        return value + kept(side[:, cut], odd, four, False) if four else value

    def final_down(own_ref, back, side, out):
        odd = is_odd()
        for at in range(0, half, TILE):
            cut = slice(at, at + TILE)
            value = finished(own_ref, back, side, odd, cut)
            out[:, cut] = value[:rows]
            out[:, half + at : half + at + TILE] = value[rows:]

    def final_pair(low_ref, high_ref, low_back, high_back, low_side, high_side, out_gate, out_up):
        odd = is_odd()
        for offset, refs in ((0, (low_ref, low_back, low_side)), (low_columns, (high_ref, high_back, high_side))):
            for cut in tiles(refs[0].shape[1]):
                value = finished(*refs, odd, cut)
                out_gate[:, shifted(cut, offset)] = value[:rows]
                out_up[:, shifted(cut, offset)] = value[rows:]

    whole = ((rows, wide), F32)
    grad_down = step(final_down, whole, [own_down, back_of_down, side_down])
    output, end = step(final_output, [((tokens, width), BF), ((128, 128), F32)], [keep, got])
    end = exchanged(end, "tensor", SWAP)
    grad_gate, grad_up = step(
        final_pair,
        [whole, whole],
        [own_low, own_high, back_of_low, back_of_high, side_low, side_high],
        also=[end],
    )
    return (output, grad_gate, grad_up, grad_down)


def solution(mesh):
    placed = (
        P("section", None),
        P("section", None),
        P(("section", "tensor"), None),
        P(("section", "tensor"), None),
        P(("section", "tensor"), None),
    )
    return jax.shard_map(
        on_device,
        mesh=mesh,
        in_specs=placed,
        out_specs=(
            P("section", "tensor"),
            P(("section", "tensor"), None),
            P(("section", "tensor"), None),
            P(("section", "tensor"), None),
        ),
        check_vma=False,
    )
```

```python
import jax
import jax.numpy as jnp
from jax import lax
from jax.experimental import pallas as pl
from jax.experimental.pallas import tpu as pltpu
from jax.sharding import PartitionSpec as P

BF = jnp.bfloat16
F32 = jnp.float32
NN = (((1,), (0,)), ((), ()))
NT = (((1,), (1,)), ((), ()))
TN = (((0,), (0,)), ((), ()))
TILE = 512
SWAP = 1
BITS = (2, 4)


def dot(left, right, dims):
    return lax.dot_general(left, right, dims, preferred_element_type=F32)


class Steps:
    def __init__(self):
        self.mark = None

    def __call__(self, body, outs, ins, also=(), far=0, scratch=()):
        marks = [*also] if self.mark is None else [*also, self.mark]
        count = len(ins)
        ins = [pltpu.with_memory_space_constraint(v, pltpu.HBM) if k < far else v for k, v in enumerate(ins)]

        def kernel(*refs):
            last = count + len(marks) + len(shapes)
            body(*refs[:count], *refs[count + len(marks) : last - 1], *refs[last:])
            refs[last - 1][...] = jnp.zeros_like(refs[last - 1])

        single = isinstance(outs, tuple)
        shapes = ([outs] if single else list(outs)) + [((8, 128), F32)]
        *got, self.mark = pl.pallas_call(
            kernel,
            out_shape=[jax.ShapeDtypeStruct(*s) for s in shapes],
            in_specs=[pl.BlockSpec(memory_space=pltpu.HBM)] * far
            + [pl.BlockSpec(memory_space=pltpu.VMEM)] * (count + len(marks) - far),
            out_specs=[pl.BlockSpec(memory_space=pltpu.VMEM)] * len(shapes),
            scratch_shapes=list(scratch),
            compiler_params=pltpu.CompilerParams(vmem_limit_bytes=24 * 1024 * 1024),
            cost_estimate=pl.CostEstimate(flops=1, bytes_accessed=1, transcendentals=0),
        )(*ins, *marks)
        return got[0] if single else got


def is_odd():
    return lax.rem(lax.axis_index("section"), 2) == 1


def either(bit, run):
    for value in range(2):
        pl.when(bit == value)(lambda value=value: run(value))


def tensor_bit(bit):
    return lax.rem(lax.div(lax.axis_index("tensor"), bit), 2)


def is_odd():
    return lax.rem(lax.axis_index("section"), 2) == 1


def top_rows(like):
    return lax.broadcasted_iota(jnp.int32, like.shape, 0) < like.shape[0] // 2


def placed(rows):
    shape = (2 * rows, rows)
    place = lax.broadcasted_iota(jnp.int32, shape, 0) - lax.broadcasted_iota(jnp.int32, shape, 1)
    return [(place == shift).astype(F32).astype(BF) for shift in (0, rows)]


def stacked(out, upper, lower, upper_at=0, lower_at=0):
    top, bottom = placed(upper.shape[0])
    for at in range(0, out.shape[1], TILE):
        first, second = slice(upper_at + at, upper_at + at + TILE), slice(lower_at + at, lower_at + at + TILE)
        out[:, at : at + TILE] = (dot(top, upper[:, first], NN) + dot(bottom, lower[:, second], NN)).astype(BF)


def runs(width, wide):
    return [(SWAP * width * j, 2 * SWAP * width * j) for j in range(wide // (2 * SWAP * width))]


def packed(width, gate, up, down, high, low, keep, send, gate_here, up_here, down_here, sems):
    copies = [
        pltpu.make_async_copy(there, here, sems.at[k])
        for k, (there, here) in enumerate(((gate, gate_here), (up, up_here), (down, down_here)))
    ]
    for copy in copies:
        copy.start()
    half = high.shape[1]
    copies[0].wait()
    copies[1].wait()
    stacked(high, gate_here, up_here, half, half)
    stacked(low, gate_here, up_here)
    copies[2].wait()

    def run(mine):
        for near, there in runs(width, 2 * half):
            here = slice(near, near + SWAP * width)
            for out, which in ((keep, mine), (send, 1 - mine)):
                at = there + SWAP * width * which
                out[:, here] = down_here[:, at : at + SWAP * width]

    either(tensor_bit(SWAP), run)


def project_tiles(x, low, high):
    half = low.shape[1]
    tile = min(half, 1024)
    total = jnp.zeros((low.shape[0], x.shape[0]), F32)
    for at in range(0, half, tile):
        cut = slice(at, at + tile)
        total += dot(low[:, cut], x[:, cut], NT)
        total += dot(high[:, cut], x[:, half + at : half + at + tile], NT)
    return total


def project(x, low, high, both, hid_a, hid_b):
    rows = low.shape[0] // 2
    total = project_tiles(x, low, high)
    both[...] = total
    hidden = total * jax.nn.sigmoid(total) * pltpu.roll(total, rows, 0)
    hidden = jnp.where(top_rows(total), hidden, 0.0)
    hid_a[...] = hidden.astype(BF)
    hid_b[...] = pltpu.roll(hidden, rows, 0).astype(BF)


def project_first(x_there, g_there, low, high, x, g, both, hid_a, hid_b, sems):
    copies = [pltpu.make_async_copy(x_there, x, sems.at[0]), pltpu.make_async_copy(g_there, g, sems.at[1])]
    for copy in copies:
        copy.start()
    copies[0].wait()
    project(x, low, high, both, hid_a, hid_b)
    copies[1].wait()


def shares(width, g, down, part):
    wide = g.shape[1]
    tile = min(SWAP * width, 1024)

    def run(mine):
        total = jnp.zeros(part.shape, F32)
        for near, there in runs(width, wide):
            for at in range(0, SWAP * width, tile):
                far = there + SWAP * width * mine + at
                total += dot(down[:, near + at : near + at + tile], g[:, far : far + tile], NT)
        part[...] = total

    either(tensor_bit(SWAP), run)


def sent_share(part, hid_b):
    share = part[...]
    return jnp.where(top_rows(share), pltpu.roll(share, share.shape[0] // 2, 0), hid_b[...].astype(F32))


def finish(both, part, got, hid_a, pair, hid_pair):
    rows = both.shape[0] // 2
    gate, got = both[...], got[...]
    dhid = part[...] + got
    sig = jax.nn.sigmoid(gate)
    dgate = dhid * pltpu.roll(gate, rows, 0) * sig * (1.0 + gate * (1.0 - sig))
    dup = pltpu.roll(dhid * (gate * sig), rows, 0)
    first = top_rows(gate)
    pair[...] = jnp.where(first, dgate, dup).astype(BF)
    hid_pair[...] = jnp.where(first, hid_a[...].astype(F32), got).astype(BF)


def down_columns(g, hid_a, hid_b, at, half):
    cut = slice(at, at + TILE)
    return dot(hid_a[...], g[:, cut], NN) + dot(hid_b[...], g[:, half + at : half + at + TILE], NN)


def tiles(size):
    return [slice(at, min(at + TILE, size)) for at in range(0, size, TILE)]


def shifted(cut, offset):
    return slice(cut.start + offset, cut.stop + offset)


def own_grads(x, g, hid_a, hid_b, pair, low, high, down):
    half = down.shape[1]
    for out, offset in ((low, 0), (high, low.shape[1])):
        for cut in tiles(out.shape[1]):
            out[:, cut] = dot(pair[...], x[:, shifted(cut, offset)], NN)
    for at in range(0, half, TILE):
        down[:, at : at + TILE] = down_columns(g, hid_a, hid_b, at, half)


def sent_down(g, hid_a, hid_b, out):
    half = out.shape[1]
    for at in range(0, half, TILE):
        out[:, at : at + TILE] = down_columns(g, hid_a, hid_b, at, half).astype(BF)


def sent_pair(x, pair, low, high):
    for out, offset in ((low, 0), (high, low.shape[1])):
        for cut in tiles(out.shape[1]):
            out[:, cut] = dot(pair[...], x[:, shifted(cut, offset)], NN).astype(BF)


def kept(side, odd, four, wanted):
    value = side.astype(F32)
    return jnp.where(odd == wanted, value, 0.0) if four else value


def picked(here, piece, out):
    @pl.when(is_odd())
    def _():
        out[...] = here[...]

    @pl.when(jnp.logical_not(is_odd()))
    def _():
        out[...] = piece[...]


def output_sums(width, *refs):
    hids, downs, (send, keep) = refs[:3], refs[3:6], refs[6:]
    tile = min(width, TILE)

    def run(mine):
        for block in range(keep.shape[1] // width):
            for which in range(2):
                for at in range(0, width, tile):
                    cols = slice((2 * block + which) * width + at, (2 * block + which) * width + at + tile)
                    here = slice(block * width + at, block * width + at + tile)
                    total = sum(dot(hid[...], down[:, cols], TN) for hid, down in zip(hids, downs))
                    if which == mine:
                        keep[:, here] = total
                    else:
                        send[:, here] = total.astype(BF)

    either(tensor_bit(BITS[0]), run)


def halved(bit, width, keep, got, send, left):
    tile = min(width, TILE)

    def run(mine):
        for block in range(left.shape[1] // width):
            for out, which in ((send, 1 - mine), (left, mine)):
                for at in range(0, width, tile):
                    cols = slice((2 * block + which) * width + at, (2 * block + which) * width + at + tile)
                    value = keep[:, cols] + got[:, cols].astype(F32)
                    out[:, block * width + at : block * width + at + tile] = value.astype(out.dtype)

    either(tensor_bit(bit), run)


def final_output(keep, got, out, end):
    out[...] = (keep[...] + got[...].astype(F32)).astype(BF)
    end[...] = jnp.zeros_like(end)


def exchanged(value, axis, bit):
    count = lax.axis_size(axis)
    return lax.ppermute(value, axis, [(source, source ^ bit) for source in range(count)])


def ring_passed(value, steps):
    count = lax.axis_size("section")
    return lax.ppermute(value, "section", [(source, (source + steps) % count) for source in range(count)])


def on_device(x, g, gate_weight, up_weight, down_weight):
    rows, wide = gate_weight.shape
    half, both_rows, tokens = wide // 2, 2 * rows, x.shape[0]
    count = lax.axis_size("tensor")
    assert count > BITS[1] and count & (count - 1) == 0
    width = wide // count
    four = lax.axis_size("section") == 4
    piece, narrow = ((both_rows, half), BF), ((rows, half), BF)
    small, small_bf = ((both_rows, tokens), F32), ((both_rows, tokens), BF)
    step = Steps()

    def with_width(body):
        def run(*refs):
            body(width, *refs)

        return run

    def one_hop(value):
        return exchanged(value, "section", 2) if four else ring_passed(value, 1)

    def relay(here, value):
        if not four:
            return ring_passed(here, 1)
        return exchanged(step(picked, piece, [here, value]), "section", 1)

    def outward(value):
        return exchanged(value, "section", 1) if four else ring_passed(value, -1)

    def backward(value):
        return exchanged(value, "section", 2) if four else ring_passed(value, -1)

    own, first, second = [None] * 3, [None] * 3, [None] * 3
    held = pltpu.VMEM((rows, wide), BF)
    own[1], own[0], down_keep, down_send = step(
        with_width(packed),
        [piece, piece, narrow, narrow],
        [gate_weight, up_weight, down_weight],
        far=3,
        scratch=[held, held, held, pltpu.SemaphoreType.DMA((3,))],
    )
    first[1] = one_hop(own[1])
    down_got = exchanged(down_send, "tensor", SWAP)
    first[0] = one_hop(own[0])

    def joined(keep, got, out):
        stacked(out, keep, got)

    own[2] = step(joined, piece, [down_keep, down_got])
    if four:
        crossed = exchanged(own[2], "section", 1)
        onward = lax.ppermute(crossed, "section", [(source, source ^ 2) for source in (0, 2)])
    first[2] = one_hop(own[2])
    x, g, both_own, *hid_own = step(
        project_first,
        [(x.shape, BF), (g.shape, BF), small, small_bf, small_bf],
        [x, g, own[0], own[1]],
        far=2,
        scratch=[pltpu.SemaphoreType.DMA((2,))],
    )
    share = with_width(shares)
    share_own = step(share, small, [g, own[2]])
    second[1] = relay(first[1], own[1])
    second[0] = relay(first[0], own[0])
    both_first, *hid_first = step(project, [small, small_bf, small_bf], [x, first[0], first[1]], also=[second[1]])
    second[2] = step(picked, piece, [crossed, onward]) if four else ring_passed(first[2], 1)
    share_second = step(share, small, [g, second[2]])
    both_second, *hid_second = step(project, [small, small_bf, small_bf], [x, second[0], second[1]])

    def two_sent(share_a, hid_a, share_b, hid_b, out):
        out[:both_rows, :] = sent_share(share_a, hid_a)
        out[both_rows:, :] = sent_share(share_b, hid_b)

    sent = step(two_sent, ((2 * both_rows, tokens), F32), [share_own, hid_own[1], share_second, hid_second[1]])
    got_two = exchanged(sent, "tensor", SWAP)
    side_down = outward(step(sent_down, piece, [g, *hid_second]))

    def finish_two(both_a, part_a, hid_a, both_b, part_b, hid_b, got, pair_a, out_a, pair_b, out_b):
        finish(both_a, part_a, got.at[:both_rows, :], hid_a, pair_a, out_a)
        finish(both_b, part_b, got.at[both_rows:, :], hid_b, pair_b, out_b)

    pair_own, wide_own, pair_second, wide_second = step(
        finish_two, [small_bf] * 4, [both_own, share_own, hid_own[0], both_second, share_second, hid_second[0], got_two]
    )
    low_columns = half + 128
    low_shape, high_shape = (both_rows, low_columns), (both_rows, wide - low_columns)
    low, high = step(sent_pair, [(low_shape, BF), (high_shape, BF)], [x, pair_second])
    side_low, side_high = outward(low), outward(high)

    def one_sent(gr, down, hid, part, out):
        shares(width, gr, down, part)
        out[...] = sent_share(part, hid)

    share_first, sent = step(one_sent, [small, small], [g, first[2], hid_first[1]])
    got_one = exchanged(sent, "tensor", SWAP)
    grads_f32 = [(low_shape, F32), (high_shape, F32), ((both_rows, half), F32)]
    pair_first, wide_first = step(finish, [small_bf] * 2, [both_first, share_first, got_one, hid_first[0]])
    quarter = wide // 4
    send, keep = step(
        with_width(output_sums),
        [((tokens, quarter), BF), ((tokens, quarter), F32)],
        [wide_own, wide_first, wide_second, own[2], first[2], second[2]],
    )
    got = exchanged(send, "tensor", BITS[0])

    def back_down(gr, a, b, side, out):
        odd = is_odd()
        for at in range(0, half, TILE):
            value = down_columns(gr, a, b, at, half) + kept(side[:, at : at + TILE], odd, four, True)
            out[:, at : at + TILE] = value.astype(BF)

    def back_pair(offset):
        def body(xr, pair, side, out):
            odd = is_odd()
            for cut in tiles(out.shape[1]):
                value = dot(pair[...], xr[:, shifted(cut, offset)], NN)
                out[:, cut] = (value + kept(side[:, cut], odd, four, True)).astype(BF)

        return body

    back_of_down = backward(step(back_down, piece, [g, *hid_first, side_down]))
    own_low, own_high, own_down = step(own_grads, grads_f32, [x, g, *hid_own, pair_own])
    back_of_low = backward(step(back_pair(0), (low_shape, BF), [x, pair_first, side_low]))

    def next_half(keep, got, bit):
        cols = keep.shape[1] // 2

        def body(*refs):
            halved(bit, width, *refs)

        send, keep = step(body, [((tokens, cols), BF), ((tokens, cols), F32)], [keep, got])
        return keep, exchanged(send, "tensor", bit)

    keep, got = next_half(keep, got, BITS[1])
    back_of_high = backward(step(back_pair(low_columns), (high_shape, BF), [x, pair_first, side_high], also=[back_of_down]))
    bit = 2 * BITS[1]
    while bit < count:
        keep, got = next_half(keep, got, bit)
        bit *= 2

    def finished(own_ref, back, side, odd, cut):
        value = own_ref[:, cut] + back[:, cut].astype(F32)
        return value + kept(side[:, cut], odd, four, False) if four else value

    def final_down(own_ref, back, side, out):
        odd = is_odd()
        for at in range(0, half, TILE):
            cut = slice(at, at + TILE)
            value = finished(own_ref, back, side, odd, cut)
            out[:, cut] = value[:rows]
            out[:, half + at : half + at + TILE] = value[rows:]

    def final_pair(low_ref, high_ref, low_back, high_back, low_side, high_side, out_gate, out_up):
        odd = is_odd()
        for offset, refs in ((0, (low_ref, low_back, low_side)), (low_columns, (high_ref, high_back, high_side))):
            for cut in tiles(refs[0].shape[1]):
                value = finished(*refs, odd, cut)
                out_gate[:, shifted(cut, offset)] = value[:rows]
                out_up[:, shifted(cut, offset)] = value[rows:]

    whole = ((rows, wide), F32)
    grad_down = step(final_down, whole, [own_down, back_of_down, side_down])
    output, end = step(final_output, [((tokens, width), BF), ((128, 128), F32)], [keep, got])
    end = exchanged(end, "tensor", SWAP)
    grad_gate, grad_up = step(
        final_pair,
        [whole, whole],
        [own_low, own_high, back_of_low, back_of_high, side_low, side_high],
        also=[end],
    )
    return (output, grad_gate, grad_up, grad_down)


def solution(mesh):
    placed = (
        P("section", None),
        P("section", None),
        P(("section", "tensor"), None),
        P(("section", "tensor"), None),
        P(("section", "tensor"), None),
    )
    return jax.shard_map(
        on_device,
        mesh=mesh,
        in_specs=placed,
        out_specs=(
            P("section", "tensor"),
            P(("section", "tensor"), None),
            P(("section", "tensor"), None),
            P(("section", "tensor"), None),
        ),
        check_vma=False,
    )
```

```python
import jax
import jax.numpy as jnp
from jax import lax
from jax.experimental import pallas as pl
from jax.experimental.pallas import tpu as pltpu
from jax.sharding import PartitionSpec as P

BF = jnp.bfloat16
F32 = jnp.float32
NN = (((1,), (0,)), ((), ()))
NT = (((1,), (1,)), ((), ()))
TN = (((0,), (0,)), ((), ()))
TILE = 512
SWAP = 1
SECOND = 2
BITS = (4,)


def dot(left, right, dims):
    return lax.dot_general(left, right, dims, preferred_element_type=F32)


class Steps:
    def __init__(self):
        self.mark = None

    def __call__(self, body, outs, ins, also=(), far=0, scratch=()):
        marks = [*also] if self.mark is None else [*also, self.mark]
        count = len(ins)
        ins = [pltpu.with_memory_space_constraint(v, pltpu.HBM) if k < far else v for k, v in enumerate(ins)]

        def kernel(*refs):
            last = count + len(marks) + len(shapes)
            body(*refs[:count], *refs[count + len(marks) : last - 1], *refs[last:])
            refs[last - 1][...] = jnp.zeros_like(refs[last - 1])

        single = isinstance(outs, tuple)
        shapes = ([outs] if single else list(outs)) + [((8, 128), F32)]
        *got, self.mark = pl.pallas_call(
            kernel,
            out_shape=[jax.ShapeDtypeStruct(*s) for s in shapes],
            in_specs=[pl.BlockSpec(memory_space=pltpu.HBM)] * far
            + [pl.BlockSpec(memory_space=pltpu.VMEM)] * (count + len(marks) - far),
            out_specs=[pl.BlockSpec(memory_space=pltpu.VMEM)] * len(shapes),
            scratch_shapes=list(scratch),
            compiler_params=pltpu.CompilerParams(vmem_limit_bytes=24 * 1024 * 1024),
            cost_estimate=pl.CostEstimate(flops=1, bytes_accessed=1, transcendentals=0),
        )(*ins, *marks)
        return got[0] if single else got


def either(bit, run):
    for value in range(2):
        pl.when(bit == value)(lambda value=value: run(value))


def tensor_bit(bit):
    return lax.rem(lax.div(lax.axis_index("tensor"), bit), 2)


def both_bits(run):
    either(tensor_bit(SECOND), lambda here: either(tensor_bit(BITS[0]), lambda mine: run(here, mine)))


def is_odd():
    return lax.rem(lax.axis_index("section"), 2) == 1


def top_rows(like):
    return lax.broadcasted_iota(jnp.int32, like.shape, 0) < like.shape[0] // 2


def placed(rows):
    shape = (2 * rows, rows)
    place = lax.broadcasted_iota(jnp.int32, shape, 0) - lax.broadcasted_iota(jnp.int32, shape, 1)
    return [(place == shift).astype(F32).astype(BF) for shift in (0, rows)]


def stacked(out, upper, lower, upper_at=0, lower_at=0):
    top, bottom = placed(upper.shape[0])
    for at in range(0, out.shape[1], TILE):
        first, second = slice(upper_at + at, upper_at + at + TILE), slice(lower_at + at, lower_at + at + TILE)
        out[:, at : at + TILE] = (dot(top, upper[:, first], NN) + dot(bottom, lower[:, second], NN)).astype(BF)


def runs(width, wide):
    return [(SWAP * width * j, 2 * SWAP * width * j) for j in range(wide // (2 * SWAP * width))]


def packed(width, gate, up, down, high, low, keep, send, gate_here, up_here, down_here, sems):
    copies = [
        pltpu.make_async_copy(there, here, sems.at[k])
        for k, (there, here) in enumerate(((gate, gate_here), (up, up_here), (down, down_here)))
    ]
    for copy in copies:
        copy.start()
    half = high.shape[1]
    copies[0].wait()
    copies[1].wait()
    stacked(high, gate_here, up_here, half, half)
    stacked(low, gate_here, up_here)
    copies[2].wait()

    def run(mine):
        for near, there in runs(width, 2 * half):
            here = slice(near, near + SWAP * width)
            for out, which in ((keep, mine), (send, 1 - mine)):
                at = there + SWAP * width * which
                out[:, here] = down_here[:, at : at + SWAP * width]

    either(tensor_bit(SWAP), run)


def project_tiles(x, low, high):
    half = low.shape[1]
    tile = min(half, 1024)
    total = jnp.zeros((low.shape[0], x.shape[0]), F32)
    for at in range(0, half, tile):
        cut = slice(at, at + tile)
        total += dot(low[:, cut], x[:, cut], NT)
        total += dot(high[:, cut], x[:, half + at : half + at + tile], NT)
    return total


def project(x, low, high, both, hid_a, hid_b):
    rows = low.shape[0] // 2
    total = project_tiles(x, low, high)
    both[...] = total
    hidden = total * jax.nn.sigmoid(total) * pltpu.roll(total, rows, 0)
    hidden = jnp.where(top_rows(total), hidden, 0.0)
    hid_a[...] = hidden.astype(BF)
    hid_b[...] = pltpu.roll(hidden, rows, 0).astype(BF)


def project_first(x_there, g_there, low, high, x, g, both, hid_a, hid_b, sems):
    copies = [pltpu.make_async_copy(x_there, x, sems.at[0]), pltpu.make_async_copy(g_there, g, sems.at[1])]
    for copy in copies:
        copy.start()
    copies[0].wait()
    project(x, low, high, both, hid_a, hid_b)
    copies[1].wait()


def shares(width, g, down, part):
    wide = g.shape[1]
    tile = min(SWAP * width, 1024)

    def run(mine):
        total = jnp.zeros(part.shape, F32)
        for near, there in runs(width, wide):
            for at in range(0, SWAP * width, tile):
                far = there + SWAP * width * mine + at
                total += dot(down[:, near + at : near + at + tile], g[:, far : far + tile], NT)
        part[...] = total

    either(tensor_bit(SWAP), run)


def sent_share(part, hid_b):
    share = part[...]
    return jnp.where(top_rows(share), pltpu.roll(share, share.shape[0] // 2, 0), hid_b[...].astype(F32))


def finish(both, part, got, hid_a, pair, hid_pair):
    rows = both.shape[0] // 2
    gate, got = both[...], got[...]
    dhid = part[...] + got
    sig = jax.nn.sigmoid(gate)
    dgate = dhid * pltpu.roll(gate, rows, 0) * sig * (1.0 + gate * (1.0 - sig))
    dup = pltpu.roll(dhid * (gate * sig), rows, 0)
    first = top_rows(gate)
    pair[...] = jnp.where(first, dgate, dup).astype(BF)
    hid_pair[...] = jnp.where(first, hid_a[...].astype(F32), got).astype(BF)


def down_columns(g, hid_a, hid_b, at, half):
    cut = slice(at, at + TILE)
    return dot(hid_a[...], g[:, cut], NN) + dot(hid_b[...], g[:, half + at : half + at + TILE], NN)


def tiles(size):
    return [slice(at, min(at + TILE, size)) for at in range(0, size, TILE)]


def shifted(cut, offset):
    return slice(cut.start + offset, cut.stop + offset)


def own_grads(x, g, hid_a, hid_b, pair, low, high, down):
    half = down.shape[1]
    for out, offset in ((low, 0), (high, low.shape[1])):
        for cut in tiles(out.shape[1]):
            out[:, cut] = dot(pair[...], x[:, shifted(cut, offset)], NN)
    for at in range(0, half, TILE):
        down[:, at : at + TILE] = down_columns(g, hid_a, hid_b, at, half)


def sent_down(g, hid_a, hid_b, out):
    half = out.shape[1]
    for at in range(0, half, TILE):
        out[:, at : at + TILE] = down_columns(g, hid_a, hid_b, at, half).astype(BF)


def sent_pair(x, pair, low, high):
    for out, offset in ((low, 0), (high, low.shape[1])):
        for cut in tiles(out.shape[1]):
            out[:, cut] = dot(pair[...], x[:, shifted(cut, offset)], NN).astype(BF)


def kept(side, odd, four, wanted):
    value = side.astype(F32)
    return jnp.where(odd == wanted, value, 0.0) if four else value


def picked(here, piece, out):
    @pl.when(is_odd())
    def _():
        out[...] = here[...]

    @pl.when(jnp.logical_not(is_odd()))
    def _():
        out[...] = piece[...]


def other_columns(width, down, out, at):
    def run(mine):
        for k in range(down.shape[1] // (2 * width)):
            column = (2 * k + 1 - mine) * width
            out[:, at + k * width : at + (k + 1) * width] = down[:, column : column + width]

    either(tensor_bit(SECOND), run)


def output_sums(width, *refs):
    hids, downs, (two, last, send, keep) = refs[:3], refs[3:6], refs[6:]
    tokens, quarter = send.shape[0], downs[0].shape[1] // 2
    gots = ((two, 0), (two, quarter), (last, 0))
    tile = min(width, TILE)

    def run(here, mine):
        for block in range(2 * keep.shape[1] // width):
            out = keep if block % 2 == mine else send
            for at in range(0, width, tile):
                near, far = (2 * block + here) * width + at, block * width + at
                total = 0.0
                for k, (hid, down, (got, offset)) in enumerate(zip(hids, downs, gots)):
                    total += dot(hid[...], down[:, near : near + tile], TN)
                    other = last[:, quarter + k * tokens : quarter + (k + 1) * tokens]
                    total += dot(other, got[:, offset + far : offset + far + tile], TN)
                column = block // 2 * width + at
                out[:, column : column + tile] = total.astype(out.dtype)

    both_bits(run)


def halved(bit, width, keep, got, send, left):
    tile = min(width, TILE)

    def run(mine):
        for block in range(left.shape[1] // width):
            for out, which in ((send, 1 - mine), (left, mine)):
                for at in range(0, width, tile):
                    cols = slice((2 * block + which) * width + at, (2 * block + which) * width + at + tile)
                    value = keep[:, cols] + got[:, cols].astype(F32)
                    out[:, block * width + at : block * width + at + tile] = value.astype(out.dtype)

    either(tensor_bit(bit), run)


def final_output(keep, got, out, end):
    out[...] = (keep[...] + got[...].astype(F32)).astype(BF)
    end[...] = jnp.zeros_like(end)


def exchanged(value, axis, bit):
    count = lax.axis_size(axis)
    return lax.ppermute(value, axis, [(source, source ^ bit) for source in range(count)])


def ring_passed(value, steps):
    count = lax.axis_size("section")
    return lax.ppermute(value, "section", [(source, (source + steps) % count) for source in range(count)])


def on_device(x, g, gate_weight, up_weight, down_weight):
    rows, wide = gate_weight.shape
    half, both_rows, tokens = wide // 2, 2 * rows, x.shape[0]
    count = lax.axis_size("tensor")
    assert count > BITS[0] and count & (count - 1) == 0
    width = wide // count
    four = lax.axis_size("section") == 4
    piece, narrow = ((both_rows, half), BF), ((rows, half), BF)
    small, small_bf = ((both_rows, tokens), F32), ((both_rows, tokens), BF)
    step = Steps()

    def with_width(body):
        def run(*refs):
            body(width, *refs)

        return run

    def one_hop(value):
        return exchanged(value, "section", 2) if four else ring_passed(value, 1)

    def relay(here, value):
        if not four:
            return ring_passed(here, 1)
        return exchanged(step(picked, piece, [here, value]), "section", 1)

    def outward(value):
        return exchanged(value, "section", 1) if four else ring_passed(value, -1)

    def backward(value):
        return exchanged(value, "section", 2) if four else ring_passed(value, -1)

    own, first, second = [None] * 3, [None] * 3, [None] * 3
    held = pltpu.VMEM((rows, wide), BF)
    own[1], own[0], down_keep, down_send = step(
        with_width(packed),
        [piece, piece, narrow, narrow],
        [gate_weight, up_weight, down_weight],
        far=3,
        scratch=[held, held, held, pltpu.SemaphoreType.DMA((3,))],
    )
    first[1] = one_hop(own[1])
    down_got = exchanged(down_send, "tensor", SWAP)
    first[0] = one_hop(own[0])

    def joined(keep, got, out):
        stacked(out, keep, got)

    own[2] = step(joined, piece, [down_keep, down_got])
    if four:
        crossed = exchanged(own[2], "section", 1)
        onward = lax.ppermute(crossed, "section", [(source, source ^ 2) for source in (0, 2)])
    first[2] = one_hop(own[2])
    x, g, both_own, *hid_own = step(
        project_first,
        [(x.shape, BF), (g.shape, BF), small, small_bf, small_bf],
        [x, g, own[0], own[1]],
        far=2,
        scratch=[pltpu.SemaphoreType.DMA((2,))],
    )
    share = with_width(shares)
    share_own = step(share, small, [g, own[2]])
    second[1] = relay(first[1], own[1])
    second[0] = relay(first[0], own[0])
    both_first, *hid_first = step(project, [small, small_bf, small_bf], [x, first[0], first[1]], also=[second[1]])
    second[2] = step(picked, piece, [crossed, onward]) if four else ring_passed(first[2], 1)
    share_second = step(share, small, [g, second[2]])

    def two_other(down_a, down_b, out):
        other_columns(width, down_a, out, 0)
        other_columns(width, down_b, out, half // 2)

    two_theirs = exchanged(step(two_other, piece, [own[2], second[2]]), "tensor", SECOND)
    both_second, *hid_second = step(project, [small, small_bf, small_bf], [x, second[0], second[1]])

    def two_sent(share_a, hid_a, share_b, hid_b, out):
        out[:both_rows, :] = sent_share(share_a, hid_a)
        out[both_rows:, :] = sent_share(share_b, hid_b)

    sent = step(two_sent, ((2 * both_rows, tokens), F32), [share_own, hid_own[1], share_second, hid_second[1]])
    got_two = exchanged(sent, "tensor", SWAP)
    side_down = outward(step(sent_down, piece, [g, *hid_second]))

    def finish_two(both_a, part_a, hid_a, both_b, part_b, hid_b, got, pair_a, out_a, pair_b, out_b):
        finish(both_a, part_a, got.at[:both_rows, :], hid_a, pair_a, out_a)
        finish(both_b, part_b, got.at[both_rows:, :], hid_b, pair_b, out_b)

    pair_own, wide_own, pair_second, wide_second = step(
        finish_two, [small_bf] * 4, [both_own, share_own, hid_own[0], both_second, share_second, hid_second[0], got_two]
    )
    low_columns = half + 128
    low_shape, high_shape = (both_rows, low_columns), (both_rows, wide - low_columns)
    low, high = step(sent_pair, [(low_shape, BF), (high_shape, BF)], [x, pair_second])
    side_low, side_high = outward(low), outward(high)

    def one_sent(gr, down, hid, part, out):
        shares(width, gr, down, part)
        out[...] = sent_share(part, hid)

    share_first, sent = step(one_sent, [small, small], [g, first[2], hid_first[1]], also=[two_theirs])
    got_one = exchanged(sent, "tensor", SWAP)
    grads_f32 = [(low_shape, F32), (high_shape, F32), ((both_rows, half), F32)]

    def finish_last(both, share, got, hid, wide_a, wide_b, down, pair, wide_out, out):
        finish(both, share, got, hid, pair, wide_out)
        other_columns(width, down, out, 0)
        for k, ref in enumerate((wide_a, wide_b, wide_out)):
            out[:, half // 2 + k * tokens : half // 2 + (k + 1) * tokens] = ref[...]

    pair_first, wide_first, sent = step(
        finish_last,
        [small_bf, small_bf, ((both_rows, half // 2 + 3 * tokens), BF)],
        [both_first, share_first, got_one, hid_first[0], wide_own, wide_second, first[2]],
    )
    last_theirs = exchanged(sent, "tensor", SECOND)
    def back_down(gr, a, b, side, out):
        odd = is_odd()
        for at in range(0, half, TILE):
            value = down_columns(gr, a, b, at, half) + kept(side[:, at : at + TILE], odd, four, True)
            out[:, at : at + TILE] = value.astype(BF)

    def back_pair(offset):
        def body(xr, pair, side, out):
            odd = is_odd()
            for cut in tiles(out.shape[1]):
                value = dot(pair[...], xr[:, shifted(cut, offset)], NN)
                out[:, cut] = (value + kept(side[:, cut], odd, four, True)).astype(BF)

        return body

    back_of_down = backward(step(back_down, piece, [g, *hid_first, side_down]))
    own_low, own_high, own_down = step(own_grads, grads_f32, [x, g, *hid_own, pair_own])
    back_of_low = backward(step(back_pair(0), (low_shape, BF), [x, pair_first, side_low]))
    send, keep = step(
        with_width(output_sums),
        [((tokens, wide // 8), BF), ((tokens, wide // 8), F32)],
        [wide_own, wide_second, wide_first, own[2], second[2], first[2], two_theirs, last_theirs],
    )
    got = exchanged(send, "tensor", BITS[0])

    def next_half(keep, got, bit):
        cols = keep.shape[1] // 2

        def body(*refs):
            halved(bit, width, *refs)

        send, keep = step(body, [((tokens, cols), BF), ((tokens, cols), F32)], [keep, got])
        return keep, exchanged(send, "tensor", bit)

    back_of_high = backward(step(back_pair(low_columns), (high_shape, BF), [x, pair_first, side_high], also=[back_of_down]))
    bit = 2 * BITS[0]
    while bit < count:
        keep, got = next_half(keep, got, bit)
        bit *= 2

    def finished(own_ref, back, side, odd, cut):
        value = own_ref[:, cut] + back[:, cut].astype(F32)
        return value + kept(side[:, cut], odd, four, False) if four else value

    def final_down(own_ref, back, side, out):
        odd = is_odd()
        for at in range(0, half, TILE):
            cut = slice(at, at + TILE)
            value = finished(own_ref, back, side, odd, cut)
            out[:, cut] = value[:rows]
            out[:, half + at : half + at + TILE] = value[rows:]

    def final_pair(low_ref, high_ref, low_back, high_back, low_side, high_side, out_gate, out_up):
        odd = is_odd()
        for offset, refs in ((0, (low_ref, low_back, low_side)), (low_columns, (high_ref, high_back, high_side))):
            for cut in tiles(refs[0].shape[1]):
                value = finished(*refs, odd, cut)
                out_gate[:, shifted(cut, offset)] = value[:rows]
                out_up[:, shifted(cut, offset)] = value[rows:]

    whole = ((rows, wide), F32)
    grad_down = step(final_down, whole, [own_down, back_of_down, side_down])
    output, end = step(final_output, [((tokens, width), BF), ((128, 128), F32)], [keep, got])
    end = exchanged(end, "tensor", SWAP)
    grad_gate, grad_up = step(
        final_pair,
        [whole, whole],
        [own_low, own_high, back_of_low, back_of_high, side_low, side_high],
        also=[end],
    )
    return (output, grad_gate, grad_up, grad_down)


def solution(mesh):
    placed = (
        P("section", None),
        P("section", None),
        P(("section", "tensor"), None),
        P(("section", "tensor"), None),
        P(("section", "tensor"), None),
    )
    return jax.shard_map(
        on_device,
        mesh=mesh,
        in_specs=placed,
        out_specs=(
            P("section", "tensor"),
            P(("section", "tensor"), None),
            P(("section", "tensor"), None),
            P(("section", "tensor"), None),
        ),
        check_vma=False,
    )
```

```python
import jax
import jax.numpy as jnp
from jax import lax
from jax.experimental import pallas as pl
from jax.experimental.pallas import tpu as pltpu
from jax.sharding import PartitionSpec as P

BF = jnp.bfloat16
F32 = jnp.float32
NN = (((1,), (0,)), ((), ()))
NT = (((1,), (1,)), ((), ()))
TN = (((0,), (0,)), ((), ()))
TILE = 512
SWAP = 1
SECOND = 2
BITS = (4,)


def dot(left, right, dims):
    return lax.dot_general(left, right, dims, preferred_element_type=F32)


class Steps:
    def __init__(self):
        self.mark = None

    def __call__(self, body, outs, ins, also=(), far=0, scratch=()):
        marks = [*also] if self.mark is None else [*also, self.mark]
        count = len(ins)
        ins = [pltpu.with_memory_space_constraint(v, pltpu.HBM) if k < far else v for k, v in enumerate(ins)]

        def kernel(*refs):
            last = count + len(marks) + len(shapes)
            body(*refs[:count], *refs[count + len(marks) : last - 1], *refs[last:])
            refs[last - 1][...] = jnp.zeros_like(refs[last - 1])

        single = isinstance(outs, tuple)
        shapes = ([outs] if single else list(outs)) + [((8, 128), F32)]
        *got, self.mark = pl.pallas_call(
            kernel,
            out_shape=[jax.ShapeDtypeStruct(*s) for s in shapes],
            in_specs=[pl.BlockSpec(memory_space=pltpu.HBM)] * far
            + [pl.BlockSpec(memory_space=pltpu.VMEM)] * (count + len(marks) - far),
            out_specs=[pl.BlockSpec(memory_space=pltpu.VMEM)] * len(shapes),
            scratch_shapes=list(scratch),
            compiler_params=pltpu.CompilerParams(vmem_limit_bytes=24 * 1024 * 1024),
            cost_estimate=pl.CostEstimate(flops=1, bytes_accessed=1, transcendentals=0),
        )(*ins, *marks)
        return got[0] if single else got


def either(bit, run):
    for value in range(2):
        pl.when(bit == value)(lambda value=value: run(value))


def tensor_bit(bit):
    return lax.rem(lax.div(lax.axis_index("tensor"), bit), 2)


def both_bits(run):
    either(tensor_bit(SECOND), lambda here: either(tensor_bit(BITS[0]), lambda mine: run(here, mine)))


def is_odd():
    return lax.rem(lax.axis_index("section"), 2) == 1


def top_rows(like):
    return lax.broadcasted_iota(jnp.int32, like.shape, 0) < like.shape[0] // 2


def tiles(size, step=TILE):
    return [slice(at, min(at + step, size)) for at in range(0, size, step)]


def shifted(cut, offset):
    return slice(cut.start + offset, cut.stop + offset)


def starts_of(sizes):
    return [sum(sizes[:k]) for k in range(len(sizes))]


def placed(rows):
    shape = (2 * rows, rows)
    place = lax.broadcasted_iota(jnp.int32, shape, 0) - lax.broadcasted_iota(jnp.int32, shape, 1)
    return [(place == shift).astype(F32).astype(BF) for shift in (0, rows)]


def stacked(out, upper, lower, upper_at=0, lower_at=0):
    top, bottom = placed(upper.shape[0])
    for cut in tiles(out.shape[1]):
        first, second = shifted(cut, upper_at), shifted(cut, lower_at)
        out[:, cut] = (dot(top, upper[:, first], NN) + dot(bottom, lower[:, second], NN)).astype(BF)


def runs(width, wide):
    return [(SWAP * width * j, 2 * SWAP * width * j) for j in range(wide // (2 * SWAP * width))]


def packed(width, gate, up, down, *refs):
    *pieces, keep, send, gate_here, up_here, down_here, sems = refs
    copies = [
        pltpu.make_async_copy(there, here, sems.at[k])
        for k, (there, here) in enumerate(((gate, gate_here), (up, up_here), (down, down_here)))
    ]
    for copy in copies:
        copy.start()
    half = down.shape[1] // 2
    copies[0].wait()
    copies[1].wait()
    at = 0
    for piece in pieces:
        stacked(piece, gate_here, up_here, at, at)
        at += piece.shape[1]
    copies[2].wait()

    def run(mine):
        for near, there in runs(width, 2 * half):
            here = slice(near, near + SWAP * width)
            for out, which in ((keep, mine), (send, 1 - mine)):
                at = there + SWAP * width * which
                out[:, here] = down_here[:, at : at + SWAP * width]

    either(tensor_bit(SWAP), run)


def project(x, *refs):
    pieces, (both, hid_a, hid_b) = refs[:-3], refs[-3:]
    rows = both.shape[0] // 2
    total = jnp.zeros(both.shape, F32)
    at = 0
    for piece in pieces:
        for cut in tiles(piece.shape[1], 1024):
            total += dot(piece[:, cut], x[:, shifted(cut, at)], NT)
        at += piece.shape[1]
    both[...] = total
    hidden = total * jax.nn.sigmoid(total) * pltpu.roll(total, rows, 0)
    hidden = jnp.where(top_rows(total), hidden, 0.0)
    hid_a[...] = hidden.astype(BF)
    hid_b[...] = pltpu.roll(hidden, rows, 0).astype(BF)


def project_first(x_there, g_there, *refs):
    *pieces, x, g, both, hid_a, hid_b, sems = refs
    copies = [pltpu.make_async_copy(x_there, x, sems.at[0]), pltpu.make_async_copy(g_there, g, sems.at[1])]
    for copy in copies:
        copy.start()
    copies[0].wait()
    project(x, *pieces, both, hid_a, hid_b)
    copies[1].wait()


def shares(width, g, down, part):
    wide = g.shape[1]
    tile = min(SWAP * width, 1024)

    def run(mine):
        total = jnp.zeros(part.shape, F32)
        for near, there in runs(width, wide):
            for at in range(0, SWAP * width, tile):
                far = there + SWAP * width * mine + at
                total += dot(down[:, near + at : near + at + tile], g[:, far : far + tile], NT)
        part[...] = total

    either(tensor_bit(SWAP), run)


def sent_share(part, hid_b):
    share = part[...]
    return jnp.where(top_rows(share), pltpu.roll(share, share.shape[0] // 2, 0), hid_b[...].astype(F32))


def finish(both, part, got, hid_a, pair, hid_pair):
    rows = both.shape[0] // 2
    gate, got = both[...], got[...]
    dhid = part[...] + got
    sig = jax.nn.sigmoid(gate)
    dgate = dhid * pltpu.roll(gate, rows, 0) * sig * (1.0 + gate * (1.0 - sig))
    dup = pltpu.roll(dhid * (gate * sig), rows, 0)
    first = top_rows(gate)
    pair[...] = jnp.where(first, dgate, dup).astype(BF)
    hid_pair[...] = jnp.where(first, hid_a[...].astype(F32), got).astype(BF)


def down_columns(g, hid_a, hid_b, at, half):
    cut = slice(at, at + TILE)
    return dot(hid_a[...], g[:, cut], NN) + dot(hid_b[...], g[:, half + at : half + at + TILE], NN)


def pair_columns(x, pair, outs):
    at = 0
    for out in outs:
        for cut in tiles(out.shape[1]):
            out[:, cut] = dot(pair[...], x[:, shifted(cut, at)], NN).astype(out.dtype)
        at += out.shape[1]


def own_grads(x, g, hid_a, hid_b, pair, *refs):
    *outs, down = refs
    half = down.shape[1]
    pair_columns(x, pair, outs)
    for at in range(0, half, TILE):
        down[:, at : at + TILE] = down_columns(g, hid_a, hid_b, at, half)


def sent_down(g, hid_a, hid_b, out):
    half = out.shape[1]
    for at in range(0, half, TILE):
        out[:, at : at + TILE] = down_columns(g, hid_a, hid_b, at, half).astype(BF)


def sent_pair(x, pair, *outs):
    pair_columns(x, pair, outs)


def kept(side, odd, four, wanted):
    value = side.astype(F32)
    return jnp.where(odd == wanted, value, 0.0) if four else value


def picked(here, piece, out):
    @pl.when(is_odd())
    def _():
        out[...] = here[...]

    @pl.when(jnp.logical_not(is_odd()))
    def _():
        out[...] = piece[...]


def other_columns(width, down, out, at):
    def run(mine):
        for k in range(down.shape[1] // (2 * width)):
            column = (2 * k + 1 - mine) * width
            out[:, at + k * width : at + (k + 1) * width] = down[:, column : column + width]

    either(tensor_bit(SECOND), run)


def output_sums(width, *refs):
    hids, downs, (two, last, send, keep) = refs[:3], refs[3:6], refs[6:]
    tokens, quarter = send.shape[0], downs[0].shape[1] // 2
    gots = ((two, 0), (two, quarter), (last, 0))
    tile = min(width, TILE)

    def run(here, mine):
        for block in range(2 * keep.shape[1] // width):
            out = keep if block % 2 == mine else send
            for at in range(0, width, tile):
                near, far = (2 * block + here) * width + at, block * width + at
                total = 0.0
                for k, (hid, down, (got, offset)) in enumerate(zip(hids, downs, gots)):
                    total += dot(hid[...], down[:, near : near + tile], TN)
                    other = last[:, quarter + k * tokens : quarter + (k + 1) * tokens]
                    total += dot(other, got[:, offset + far : offset + far + tile], TN)
                column = block // 2 * width + at
                out[:, column : column + tile] = total.astype(out.dtype)

    both_bits(run)


def halved(bit, width, keep, got, send, left):
    tile = min(width, TILE)

    def run(mine):
        for block in range(left.shape[1] // width):
            for out, which in ((send, 1 - mine), (left, mine)):
                for at in range(0, width, tile):
                    cols = slice((2 * block + which) * width + at, (2 * block + which) * width + at + tile)
                    value = keep[:, cols] + got[:, cols].astype(F32)
                    out[:, block * width + at : block * width + at + tile] = value.astype(out.dtype)

    either(tensor_bit(bit), run)


def final_output(keep, got, out):
    out[...] = (keep[...] + got[...].astype(F32)).astype(BF)


def exchanged(value, axis, bit):
    count = lax.axis_size(axis)
    return lax.ppermute(value, axis, [(source, source ^ bit) for source in range(count)])


def ring_passed(value, steps):
    count = lax.axis_size("section")
    return lax.ppermute(value, "section", [(source, (source + steps) % count) for source in range(count)])


def on_device(x, g, gate_weight, up_weight, down_weight):
    rows, wide = gate_weight.shape
    half, both_rows, tokens = wide // 2, 2 * rows, x.shape[0]
    count = lax.axis_size("tensor")
    assert count > BITS[0] and count & (count - 1) == 0
    width = wide // count
    four = lax.axis_size("section") == 4
    piece, narrow = ((both_rows, half), BF), ((rows, half), BF)
    small, small_bf = ((both_rows, tokens), F32), ((both_rows, tokens), BF)
    step = Steps()

    def with_width(body):
        def run(*refs):
            body(width, *refs)

        return run

    def one_hop(value):
        return exchanged(value, "section", 2) if four else ring_passed(value, 1)

    def relay(here, value):
        if not four:
            return ring_passed(here, 1)
        return exchanged(step(picked, (value.shape, BF), [here, value]), "section", 1)

    def outward(value):
        return exchanged(value, "section", 1) if four else ring_passed(value, -1)

    def backward(value):
        return exchanged(value, "section", 2) if four else ring_passed(value, -1)

    third = wide // 128 // 3 * 128
    held = pltpu.VMEM((rows, wide), BF)
    *own, down_keep, down_send = step(
        with_width(packed),
        [((both_rows, size), BF) for size in (half, half)] + [narrow, narrow],
        [gate_weight, up_weight, down_weight],
        far=3,
        scratch=[held, held, held, pltpu.SemaphoreType.DMA((3,))],
    )
    first = [one_hop(own[0])]
    down_got = exchanged(down_send, "tensor", SWAP)
    first += [one_hop(value) for value in own[1:]]

    def joined(keep, got, out):
        stacked(out, keep, got)

    down_own = step(joined, piece, [down_keep, down_got])
    if four:
        crossed = exchanged(down_own, "section", 1)
        onward = lax.ppermute(crossed, "section", [(source, source ^ 2) for source in (0, 2)])
    down_first = one_hop(down_own)
    x, g, both_own, *hid_own = step(
        project_first,
        [(x.shape, BF), (g.shape, BF), small, small_bf, small_bf],
        [x, g, *own],
        far=2,
        scratch=[pltpu.SemaphoreType.DMA((2,))],
    )
    share = with_width(shares)
    share_own = step(share, small, [g, down_own])
    second = [relay(here, value) for here, value in zip(first, own)]
    both_first, *hid_first = step(project, [small, small_bf, small_bf], [x, *first], also=[second[0]])
    down_second = step(picked, piece, [crossed, onward]) if four else ring_passed(down_first, 1)
    share_second = step(share, small, [g, down_second])

    def two_other(down_a, down_b, out):
        other_columns(width, down_a, out, 0)
        other_columns(width, down_b, out, half // 2)

    two_theirs = exchanged(step(two_other, piece, [down_own, down_second]), "tensor", SECOND)
    both_second, *hid_second = step(project, [small, small_bf, small_bf], [x, *second])

    def two_sent(share_a, hid_a, share_b, hid_b, out):
        out[:both_rows, :] = sent_share(share_a, hid_a)
        out[both_rows:, :] = sent_share(share_b, hid_b)

    sent = step(two_sent, ((2 * both_rows, tokens), F32), [share_own, hid_own[1], share_second, hid_second[1]])
    got_two = exchanged(sent, "tensor", SWAP)
    side_down = outward(step(sent_down, piece, [g, *hid_second]))

    def finish_two(both_a, part_a, hid_a, both_b, part_b, hid_b, got, pair_a, out_a, pair_b, out_b):
        finish(both_a, part_a, got.at[:both_rows, :], hid_a, pair_a, out_a)
        finish(both_b, part_b, got.at[both_rows:, :], hid_b, pair_b, out_b)

    pair_own, wide_own, pair_second, wide_second = step(
        finish_two, [small_bf] * 4, [both_own, share_own, hid_own[0], both_second, share_second, hid_second[0], got_two]
    )
    sizes = (third + 256, third, wide - 2 * third - 256)
    shapes = [(both_rows, size) for size in sizes]
    sides = [outward(value) for value in step(sent_pair, [(shape, BF) for shape in shapes], [x, pair_second])]

    def one_sent(gr, down, hid, part, out):
        shares(width, gr, down, part)
        out[...] = sent_share(part, hid)

    share_first, sent = step(one_sent, [small, small], [g, down_first, hid_first[1]], also=[two_theirs])
    got_one = exchanged(sent, "tensor", SWAP)

    def finish_last(both, share, got, hid, wide_a, wide_b, down, pair, wide_out, out):
        finish(both, share, got, hid, pair, wide_out)
        other_columns(width, down, out, 0)
        for k, ref in enumerate((wide_a, wide_b, wide_out)):
            out[:, half // 2 + k * tokens : half // 2 + (k + 1) * tokens] = ref[...]

    pair_first, wide_first, sent = step(
        finish_last,
        [small_bf, small_bf, ((both_rows, half // 2 + 3 * tokens), BF)],
        [both_first, share_first, got_one, hid_first[0], wide_own, wide_second, down_first],
    )
    last_theirs = exchanged(sent, "tensor", SECOND)

    def back_down(gr, a, b, side, out):
        odd = is_odd()
        for at in range(0, half, TILE):
            value = down_columns(gr, a, b, at, half) + kept(side[:, at : at + TILE], odd, four, True)
            out[:, at : at + TILE] = value.astype(BF)

    def back_pair(offset):
        def body(xr, pair, side, out):
            odd = is_odd()
            for cut in tiles(out.shape[1]):
                value = dot(pair[...], xr[:, shifted(cut, offset)], NN)
                out[:, cut] = (value + kept(side[:, cut], odd, four, True)).astype(BF)

        return body

    back_of_down = backward(step(back_down, piece, [g, *hid_first, side_down]))
    own_sums = step(
        own_grads,
        [(shape, F32) for shape in shapes] + [((both_rows, half), F32)],
        [x, g, *hid_own, pair_own],

    )

    send, keep = step(
        with_width(output_sums),
        [((tokens, wide // 8), BF), ((tokens, wide // 8), F32)],
        [wide_own, wide_second, wide_first, down_own, down_second, down_first, two_theirs, last_theirs],
    )
    got = exchanged(send, "tensor", BITS[0])

    def back_piece(k, also=()):
        body = back_pair(starts_of(sizes)[k])
        return backward(step(body, (shapes[k], BF), [x, pair_first, sides[k]], also=also))

    backs = [back_piece(0)]

    def next_half(keep, got, bit):
        cols = keep.shape[1] // 2

        def body(*refs):
            halved(bit, width, *refs)

        send, keep = step(body, [((tokens, cols), BF), ((tokens, cols), F32)], [keep, got])
        return keep, exchanged(send, "tensor", bit)

    backs += [back_piece(1), back_piece(2)]
    bit = 2 * BITS[0]
    while bit < count:
        keep, got = next_half(keep, got, bit)
        bit *= 2

    def finished(own_ref, back, side, odd, cut):
        value = own_ref[:, cut] + back[:, cut].astype(F32)
        return value + kept(side[:, cut], odd, four, False) if four else value

    def final_down(own_ref, back, side, out):
        odd = is_odd()
        for at in range(0, half, TILE):
            cut = slice(at, at + TILE)
            value = finished(own_ref, back, side, odd, cut)
            out[:, cut] = value[:rows]
            out[:, half + at : half + at + TILE] = value[rows:]

    def final_pair(*refs):
        odd, (out_gate, out_up) = is_odd(), refs[9:]
        for k, offset in enumerate(starts_of(sizes)):
            for cut in tiles(sizes[k]):
                value = finished(*refs[k:9:3], odd, cut)
                out_gate[:, shifted(cut, offset)] = value[:rows]
                out_up[:, shifted(cut, offset)] = value[rows:]

    whole = ((rows, wide), F32)
    grad_down = step(final_down, whole, [own_sums[3], back_of_down, side_down])
    output = step(final_output, ((tokens, width), BF), [keep, got])
    grad_gate, grad_up = step(
        final_pair,
        [whole, whole],
        [*own_sums[:3], *backs, *sides],
    )
    return (output, grad_gate, grad_up, grad_down)


def solution(mesh):
    placed = (
        P("section", None),
        P("section", None),
        P(("section", "tensor"), None),
        P(("section", "tensor"), None),
        P(("section", "tensor"), None),
    )
    return jax.shard_map(
        on_device,
        mesh=mesh,
        in_specs=placed,
        out_specs=(
            P("section", "tensor"),
            P(("section", "tensor"), None),
            P(("section", "tensor"), None),
            P(("section", "tensor"), None),
        ),
        check_vma=False,
    )
```

```python
import jax
import jax.numpy as jnp
from jax import lax
from jax.experimental import pallas as pl
from jax.experimental.pallas import tpu as pltpu
from jax.sharding import PartitionSpec as P

BF = jnp.bfloat16
F32 = jnp.float32
NN = (((1,), (0,)), ((), ()))
NT = (((1,), (1,)), ((), ()))
TN = (((0,), (0,)), ((), ()))
TILE = 512
SWAP = 1
SECOND = 2
BITS = (4,)


def dot(left, right, dims):
    return lax.dot_general(left, right, dims, preferred_element_type=F32)


class Steps:
    def __init__(self):
        self.mark = None

    def __call__(self, body, outs, ins, also=(), far=0, scratch=(), far_outs=0, in_place=False):
        marks = [*also] if self.mark is None else [*also, self.mark]
        count = len(ins)
        ins = [pltpu.with_memory_space_constraint(v, pltpu.HBM) if k < far else v for k, v in enumerate(ins)]

        def kernel(*refs):
            last = count + len(marks) + len(shapes)
            body(*refs[:count], *refs[count + len(marks) : last - 1], *refs[last:])
            refs[last - 1][...] = jnp.zeros_like(refs[last - 1])

        single = isinstance(outs, tuple)
        shapes = ([outs] if single else list(outs)) + [((8, 128), F32)]
        *got, self.mark = pl.pallas_call(
            kernel,
            out_shape=[jax.ShapeDtypeStruct(*s) for s in shapes],
            in_specs=[pl.BlockSpec(memory_space=pltpu.HBM)] * far
            + [pl.BlockSpec(memory_space=pltpu.VMEM)] * (count + len(marks) - far),
            out_specs=[pl.BlockSpec(memory_space=pltpu.HBM)] * far_outs
            + [pl.BlockSpec(memory_space=pltpu.VMEM)] * (len(shapes) - far_outs),
            input_output_aliases={k: k for k in range(far_outs)} if in_place else {},
            scratch_shapes=list(scratch),
            compiler_params=pltpu.CompilerParams(vmem_limit_bytes=24 * 1024 * 1024),
            cost_estimate=pl.CostEstimate(flops=1, bytes_accessed=1, transcendentals=0),
        )(*ins, *marks)
        return got[0] if single else got


def either(bit, run):
    for value in range(2):
        pl.when(bit == value)(lambda value=value: run(value))


def tensor_bit(bit):
    return lax.rem(lax.div(lax.axis_index("tensor"), bit), 2)


def both_bits(run):
    either(tensor_bit(SECOND), lambda here: either(tensor_bit(BITS[0]), lambda mine: run(here, mine)))


def is_odd():
    return lax.rem(lax.axis_index("section"), 2) == 1


def top_rows(like):
    return lax.broadcasted_iota(jnp.int32, like.shape, 0) < like.shape[0] // 2


def placed(rows):
    shape = (2 * rows, rows)
    place = lax.broadcasted_iota(jnp.int32, shape, 0) - lax.broadcasted_iota(jnp.int32, shape, 1)
    return [(place == shift).astype(F32).astype(BF) for shift in (0, rows)]


def stacked(out, upper, lower, upper_at=0, lower_at=0):
    top, bottom = placed(upper.shape[0])
    for at in range(0, out.shape[1], TILE):
        first, second = slice(upper_at + at, upper_at + at + TILE), slice(lower_at + at, lower_at + at + TILE)
        out[:, at : at + TILE] = (dot(top, upper[:, first], NN) + dot(bottom, lower[:, second], NN)).astype(BF)


def runs(width, wide):
    return [(SWAP * width * j, 2 * SWAP * width * j) for j in range(wide // (2 * SWAP * width))]


def packed(width, gate, up, down, high, low, keep, send, gate_here, up_here, down_here, sems):
    copies = [
        pltpu.make_async_copy(there, here, sems.at[k])
        for k, (there, here) in enumerate(((gate, gate_here), (up, up_here), (down, down_here)))
    ]
    for copy in copies:
        copy.start()
    half = high.shape[1]
    copies[0].wait()
    copies[1].wait()
    stacked(high, gate_here, up_here, half, half)
    stacked(low, gate_here, up_here)
    copies[2].wait()

    def run(mine):
        for near, there in runs(width, 2 * half):
            here = slice(near, near + SWAP * width)
            for out, which in ((keep, mine), (send, 1 - mine)):
                at = there + SWAP * width * which
                out[:, here] = down_here[:, at : at + SWAP * width]

    either(tensor_bit(SWAP), run)


def project_tiles(x, low, high):
    half = low.shape[1]
    tile = min(half, 1024)
    total = jnp.zeros((low.shape[0], x.shape[0]), F32)
    for at in range(0, half, tile):
        cut = slice(at, at + tile)
        total += dot(low[:, cut], x[:, cut], NT)
        total += dot(high[:, cut], x[:, half + at : half + at + tile], NT)
    return total


def project(x, low, high, both, hid_a, hid_b):
    finish_projection(project_tiles(x, low, high), both, hid_a, hid_b)


def project_half(x, low, at, out):
    total = jnp.zeros(out.shape, F32)
    for cut in tiles(low.shape[1], 1024):
        total += dot(low[:, cut], x[:, shifted(cut, at)], NT)
    out[...] = total


def finish_projection(total, both, hid_a, hid_b):
    rows = total.shape[0] // 2
    both[...] = total
    hidden = total * jax.nn.sigmoid(total) * pltpu.roll(total, rows, 0)
    hidden = jnp.where(top_rows(total), hidden, 0.0)
    hid_a[...] = hidden.astype(BF)
    hid_b[...] = pltpu.roll(hidden, rows, 0).astype(BF)


def project_first(x_there, g_there, low, high, x, g, both, hid_a, hid_b, sems):
    copies = [pltpu.make_async_copy(x_there, x, sems.at[0]), pltpu.make_async_copy(g_there, g, sems.at[1])]
    for copy in copies:
        copy.start()
    copies[0].wait()
    project(x, low, high, both, hid_a, hid_b)
    copies[1].wait()


def shares(width, g, down, part):
    wide = g.shape[1]
    tile = min(SWAP * width, 1024)

    def run(mine):
        total = jnp.zeros(part.shape, F32)
        for near, there in runs(width, wide):
            for at in range(0, SWAP * width, tile):
                far = there + SWAP * width * mine + at
                total += dot(down[:, near + at : near + at + tile], g[:, far : far + tile], NT)
        part[...] = total

    either(tensor_bit(SWAP), run)


def sent_share(part, hid_b):
    share = part[...]
    return jnp.where(top_rows(share), pltpu.roll(share, share.shape[0] // 2, 0), hid_b[...].astype(F32))


def finish(both, part, got, hid_a, pair, hid_pair):
    rows = both.shape[0] // 2
    gate, got = both[...], got[...]
    dhid = part[...] + got
    sig = jax.nn.sigmoid(gate)
    dgate = dhid * pltpu.roll(gate, rows, 0) * sig * (1.0 + gate * (1.0 - sig))
    dup = pltpu.roll(dhid * (gate * sig), rows, 0)
    first = top_rows(gate)
    pair[...] = jnp.where(first, dgate, dup).astype(BF)
    hid_pair[...] = jnp.where(first, hid_a[...].astype(F32), got).astype(BF)


def down_columns(g, hid_a, hid_b, at, half):
    cut = slice(at, at + TILE)
    return dot(hid_a[...], g[:, cut], NN) + dot(hid_b[...], g[:, half + at : half + at + TILE], NN)


def tiles(size, step=TILE):
    return [slice(at, min(at + step, size)) for at in range(0, size, step)]


def shifted(cut, offset):
    return slice(cut.start + offset, cut.stop + offset)


def own_grads(x, g, hid_a, hid_b, pair, low, high, down):
    half = down.shape[1]
    for out, offset in ((low, 0), (high, low.shape[1])):
        for cut in tiles(out.shape[1]):
            out[:, cut] = dot(pair[...], x[:, shifted(cut, offset)], NN)
    for at in range(0, half, TILE):
        down[:, at : at + TILE] = down_columns(g, hid_a, hid_b, at, half)


def sent_down(g, hid_a, hid_b, out):
    half = out.shape[1]
    for at in range(0, half, TILE):
        out[:, at : at + TILE] = down_columns(g, hid_a, hid_b, at, half).astype(BF)


def sent_pair(x, pair, low, high):
    for out, offset in ((low, 0), (high, low.shape[1])):
        for cut in tiles(out.shape[1]):
            out[:, cut] = dot(pair[...], x[:, shifted(cut, offset)], NN).astype(BF)


def kept(side, odd, four, wanted):
    value = side.astype(F32)
    return jnp.where(odd == wanted, value, 0.0) if four else value


def picked(here, piece, out):
    @pl.when(is_odd())
    def _():
        out[...] = here[...]

    @pl.when(jnp.logical_not(is_odd()))
    def _():
        out[...] = piece[...]


def other_columns(width, down, out, at):
    def run(mine):
        for k in range(down.shape[1] // (2 * width)):
            column = (2 * k + 1 - mine) * width
            out[:, at + k * width : at + (k + 1) * width] = down[:, column : column + width]

    either(tensor_bit(SECOND), run)


def output_sums(width, *refs):
    hids, downs, (two, last, send, keep) = refs[:3], refs[3:6], refs[6:]
    tokens, quarter = send.shape[0], downs[0].shape[1] // 2
    gots = ((two, 0), (two, quarter), (last, 0))
    tile = min(width, TILE)

    def run(here, mine):
        for block in range(2 * keep.shape[1] // width):
            out = keep if block % 2 == mine else send
            for at in range(0, width, tile):
                near, far = (2 * block + here) * width + at, block * width + at
                total = 0.0
                for k, (hid, down, (got, offset)) in enumerate(zip(hids, downs, gots)):
                    total += dot(hid[...], down[:, near : near + tile], TN)
                    other = last[:, quarter + k * tokens : quarter + (k + 1) * tokens]
                    total += dot(other, got[:, offset + far : offset + far + tile], TN)
                column = block // 2 * width + at
                out[:, column : column + tile] = total.astype(out.dtype)

    both_bits(run)


def halved(bit, width, keep, got, send, left):
    tile = min(width, TILE)

    def run(mine):
        for block in range(left.shape[1] // width):
            for out, which in ((send, 1 - mine), (left, mine)):
                for at in range(0, width, tile):
                    cols = slice((2 * block + which) * width + at, (2 * block + which) * width + at + tile)
                    value = keep[:, cols] + got[:, cols].astype(F32)
                    out[:, block * width + at : block * width + at + tile] = value.astype(out.dtype)

    either(tensor_bit(bit), run)


def final_output(keep, got, out, end):
    out[...] = (keep[...] + got[...].astype(F32)).astype(BF)
    end[...] = jnp.zeros_like(end)


def exchanged(value, axis, bit):
    count = lax.axis_size(axis)
    return lax.ppermute(value, axis, [(source, source ^ bit) for source in range(count)])


def ring_passed(value, steps):
    count = lax.axis_size("section")
    return lax.ppermute(value, "section", [(source, (source + steps) % count) for source in range(count)])


def on_device(x, g, gate_weight, up_weight, down_weight):
    rows, wide = gate_weight.shape
    half, both_rows, tokens = wide // 2, 2 * rows, x.shape[0]
    count = lax.axis_size("tensor")
    assert count > BITS[0] and count & (count - 1) == 0
    width = wide // count
    four = lax.axis_size("section") == 4
    piece, narrow = ((both_rows, half), BF), ((rows, half), BF)
    small, small_bf = ((both_rows, tokens), F32), ((both_rows, tokens), BF)
    step = Steps()

    def with_width(body):
        def run(*refs):
            body(width, *refs)

        return run

    def one_hop(value):
        return exchanged(value, "section", 2) if four else ring_passed(value, 1)

    def relay(here, value):
        if not four:
            return ring_passed(here, 1)
        return exchanged(step(picked, piece, [here, value]), "section", 1)

    def outward(value):
        return exchanged(value, "section", 1) if four else ring_passed(value, -1)

    def backward(value):
        return exchanged(value, "section", 2) if four else ring_passed(value, -1)

    own, first, second = [None] * 3, [None] * 3, [None] * 3
    held = pltpu.VMEM((rows, wide), BF)
    own[1], own[0], down_keep, down_send = step(
        with_width(packed),
        [piece, piece, narrow, narrow],
        [gate_weight, up_weight, down_weight],
        far=3,
        scratch=[held, held, held, pltpu.SemaphoreType.DMA((3,))],
    )
    first[1] = one_hop(own[1])
    down_got = exchanged(down_send, "tensor", SWAP)
    first[0] = one_hop(own[0])

    def joined(keep, got, out):
        stacked(out, keep, got)

    own[2] = step(joined, piece, [down_keep, down_got])
    if four:
        crossed = exchanged(own[2], "section", 1)
        onward = lax.ppermute(crossed, "section", [(source, source ^ 2) for source in (0, 2)])
    first[2] = one_hop(own[2])
    x, g, both_own, *hid_own = step(
        project_first,
        [(x.shape, BF), (g.shape, BF), small, small_bf, small_bf],
        [x, g, own[0], own[1]],
        far=2,
        scratch=[pltpu.SemaphoreType.DMA((2,))],
    )
    share = with_width(shares)
    share_own = step(share, small, [g, own[2]])
    second[1] = relay(first[1], own[1])
    second[0] = relay(first[0], own[0])
    both_first, *hid_first = step(project, [small, small_bf, small_bf], [x, first[0], first[1]], also=[second[1]])
    second[2] = step(picked, piece, [crossed, onward]) if four else ring_passed(first[2], 1)
    share_second = step(share, small, [g, second[2]])

    def two_other(down_a, down_b, out):
        other_columns(width, down_a, out, 0)
        other_columns(width, down_b, out, half // 2)

    two_theirs = exchanged(step(two_other, piece, [own[2], second[2]]), "tensor", SECOND)
    both_high = step(lambda xr, high, out: project_half(xr, high, half, out), small, [x, second[1]])

    def project_rest(xr, low, high_part, both, hid_a, hid_b):
        project_half(xr, low, 0, both)
        finish_projection(both[...] + high_part[...], both, hid_a, hid_b)

    both_second, *hid_second = step(project_rest, [small, small_bf, small_bf], [x, second[0], both_high])

    def two_sent(share_a, hid_a, share_b, hid_b, out):
        out[:both_rows, :] = sent_share(share_a, hid_a)
        out[both_rows:, :] = sent_share(share_b, hid_b)

    sent = step(two_sent, ((2 * both_rows, tokens), F32), [share_own, hid_own[1], share_second, hid_second[1]])
    got_two = exchanged(sent, "tensor", SWAP)
    side_down = outward(step(sent_down, piece, [g, *hid_second]))

    def finish_two(both_a, part_a, hid_a, both_b, part_b, hid_b, got, pair_a, out_a, pair_b, out_b):
        finish(both_a, part_a, got.at[:both_rows, :], hid_a, pair_a, out_a)
        finish(both_b, part_b, got.at[both_rows:, :], hid_b, pair_b, out_b)

    pair_own, wide_own, pair_second, wide_second = step(
        finish_two, [small_bf] * 4, [both_own, share_own, hid_own[0], both_second, share_second, hid_second[0], got_two]
    )
    low_columns = half + 128
    low_shape, high_shape = (both_rows, low_columns), (both_rows, wide - low_columns)
    low, high = step(sent_pair, [(low_shape, BF), (high_shape, BF)], [x, pair_second])
    side_low, side_high = outward(low), outward(high)

    def one_sent(gr, down, hid, part, out):
        shares(width, gr, down, part)
        out[...] = sent_share(part, hid)

    share_first, sent = step(one_sent, [small, small], [g, first[2], hid_first[1]], also=[two_theirs])
    got_one = exchanged(sent, "tensor", SWAP)
    grads_f32 = [(low_shape, F32), (high_shape, F32), ((both_rows, half), F32)]

    def finish_last(both, share, got, hid, wide_a, wide_b, down, pair, wide_out, out):
        finish(both, share, got, hid, pair, wide_out)
        other_columns(width, down, out, 0)
        for k, ref in enumerate((wide_a, wide_b, wide_out)):
            out[:, half // 2 + k * tokens : half // 2 + (k + 1) * tokens] = ref[...]

    pair_first, wide_first, sent = step(
        finish_last,
        [small_bf, small_bf, ((both_rows, half // 2 + 3 * tokens), BF)],
        [both_first, share_first, got_one, hid_first[0], wide_own, wide_second, first[2]],
    )
    last_theirs = exchanged(sent, "tensor", SECOND)
    def back_down(gr, a, b, side, out):
        odd = is_odd()
        for at in range(0, half, TILE):
            value = down_columns(gr, a, b, at, half) + kept(side[:, at : at + TILE], odd, four, True)
            out[:, at : at + TILE] = value.astype(BF)

    def back_pair(offset):
        def body(xr, pair, side, out):
            odd = is_odd()
            for cut in tiles(out.shape[1]):
                value = dot(pair[...], xr[:, shifted(cut, offset)], NN)
                out[:, cut] = (value + kept(side[:, cut], odd, four, True)).astype(BF)

        return body

    back_of_down = backward(step(back_down, piece, [g, *hid_first, side_down]))
    own_low, own_high, own_down = step(own_grads, grads_f32, [x, g, *hid_own, pair_own])
    back_of_low = backward(step(back_pair(0), (low_shape, BF), [x, pair_first, side_low]))
    send, keep = step(
        with_width(output_sums),
        [((tokens, wide // 8), BF), ((tokens, wide // 8), F32)],
        [wide_own, wide_second, wide_first, own[2], second[2], first[2], two_theirs, last_theirs],
    )
    got = exchanged(send, "tensor", BITS[0])

    def next_half(keep, got, bit):
        cols = keep.shape[1] // 2

        def body(*refs):
            halved(bit, width, *refs)

        send, keep = step(body, [((tokens, cols), BF), ((tokens, cols), F32)], [keep, got])
        return keep, exchanged(send, "tensor", bit)

    back_of_high = backward(step(back_pair(low_columns), (high_shape, BF), [x, pair_first, side_high], also=[back_of_down]))
    bit = 2 * BITS[0]
    while bit < count:
        keep, got = next_half(keep, got, bit)
        bit *= 2

    def finished(own_ref, back, side, odd, cut):
        value = own_ref[:, cut] + back[:, cut].astype(F32)
        return value + kept(side[:, cut], odd, four, False) if four else value

    def final_down(own_ref, back, side, out):
        odd = is_odd()
        for at in range(0, half, TILE):
            cut = slice(at, at + TILE)
            value = finished(own_ref, back, side, odd, cut)
            out[:, cut] = value[:rows]
            out[:, half + at : half + at + TILE] = value[rows:]

    def final_piece(offset, columns):
        def body(own_ref, back, side, out_gate, out_up, gate_here, up_here, sems):
            odd = is_odd()
            for cut in tiles(columns):
                value = finished(own_ref, back, side, odd, cut)
                gate_here[:, cut] = value[:rows]
                up_here[:, cut] = value[rows:]
            copies = [
                pltpu.make_async_copy(here, out.at[:, pl.ds(offset, columns)], sems.at[k])
                for k, (here, out) in enumerate(((gate_here, out_gate), (up_here, out_up)))
            ]
            for copy in copies:
                copy.start()
            for copy in copies:
                copy.wait()

        return body

    def final_last(gate_there, up_there, *refs):
        final_piece(low_columns, wide - low_columns)(*refs)

    def kept_columns(columns):
        held = pltpu.VMEM((rows, columns), F32)
        return [held, held, pltpu.SemaphoreType.DMA((2,))]

    whole = ((rows, wide), F32)
    grad_down = step(final_down, whole, [own_down, back_of_down, side_down])
    part_gate, part_up = step(
        final_piece(0, low_columns),
        [whole, whole],
        [own_low, back_of_low, side_low],
        far_outs=2,
        scratch=kept_columns(low_columns),
    )
    output, end = step(final_output, [((tokens, width), BF), ((128, 128), F32)], [keep, got])
    end = exchanged(end, "tensor", SWAP)
    grad_gate, grad_up = step(
        final_last,
        [whole, whole],
        [part_gate, part_up, own_high, back_of_high, side_high],
        also=[end],
        far=2,
        far_outs=2,
        in_place=True,
        scratch=kept_columns(wide - low_columns),
    )
    return (output, grad_gate, grad_up, grad_down)


def solution(mesh):
    placed = (
        P("section", None),
        P("section", None),
        P(("section", "tensor"), None),
        P(("section", "tensor"), None),
        P(("section", "tensor"), None),
    )
    return jax.shard_map(
        on_device,
        mesh=mesh,
        in_specs=placed,
        out_specs=(
            P("section", "tensor"),
            P(("section", "tensor"), None),
            P(("section", "tensor"), None),
            P(("section", "tensor"), None),
        ),
        check_vma=False,
    )
```

```python
import jax
import jax.numpy as jnp
from jax import lax
from jax.experimental import pallas as pl
from jax.experimental.pallas import tpu as pltpu
from jax.sharding import PartitionSpec as P

BF = jnp.bfloat16
F32 = jnp.float32
NN = (((1,), (0,)), ((), ()))
NT = (((1,), (1,)), ((), ()))
TN = (((0,), (0,)), ((), ()))
TILE = 512
SWAP = 1
SECOND = 2
BITS = (4,)


def dot(left, right, dims):
    return lax.dot_general(left, right, dims, preferred_element_type=F32)


class Steps:
    def __init__(self):
        self.mark = None

    def __call__(self, body, outs, ins, also=(), far=0, scratch=()):
        marks = [*also] if self.mark is None else [*also, self.mark]
        count = len(ins)
        ins = [pltpu.with_memory_space_constraint(v, pltpu.HBM) if k < far else v for k, v in enumerate(ins)]

        def kernel(*refs):
            last = count + len(marks) + len(shapes)
            body(*refs[:count], *refs[count + len(marks) : last - 1], *refs[last:])
            refs[last - 1][...] = jnp.zeros_like(refs[last - 1])

        single = isinstance(outs, tuple)
        shapes = ([outs] if single else list(outs)) + [((8, 128), F32)]
        *got, self.mark = pl.pallas_call(
            kernel,
            out_shape=[jax.ShapeDtypeStruct(*s) for s in shapes],
            in_specs=[pl.BlockSpec(memory_space=pltpu.HBM)] * far
            + [pl.BlockSpec(memory_space=pltpu.VMEM)] * (count + len(marks) - far),
            out_specs=[pl.BlockSpec(memory_space=pltpu.VMEM)] * len(shapes),
            scratch_shapes=list(scratch),
            compiler_params=pltpu.CompilerParams(vmem_limit_bytes=24 * 1024 * 1024),
            cost_estimate=pl.CostEstimate(flops=1, bytes_accessed=1, transcendentals=0),
        )(*ins, *marks)
        return got[0] if single else got

    def hold(self, value):
        value, self.mark = lax.optimization_barrier((value, self.mark))
        return value


def either(bit, run):
    for value in range(2):
        pl.when(bit == value)(lambda value=value: run(value))


def tensor_bit(bit):
    return lax.rem(lax.div(lax.axis_index("tensor"), bit), 2)


def both_bits(run):
    either(tensor_bit(SECOND), lambda here: either(tensor_bit(BITS[0]), lambda mine: run(here, mine)))


def is_odd():
    return lax.rem(lax.axis_index("section"), 2) == 1


def top_rows(like):
    return lax.broadcasted_iota(jnp.int32, like.shape, 0) < like.shape[0] // 2


def placed(rows):
    shape = (2 * rows, rows)
    place = lax.broadcasted_iota(jnp.int32, shape, 0) - lax.broadcasted_iota(jnp.int32, shape, 1)
    return [(place == shift).astype(F32).astype(BF) for shift in (0, rows)]


def stacked(out, upper, lower, upper_at=0, lower_at=0):
    top, bottom = placed(upper.shape[0])
    for at in range(0, out.shape[1], TILE):
        first, second = slice(upper_at + at, upper_at + at + TILE), slice(lower_at + at, lower_at + at + TILE)
        out[:, at : at + TILE] = (dot(top, upper[:, first], NN) + dot(bottom, lower[:, second], NN)).astype(BF)


def runs(width, wide):
    return [(SWAP * width * j, 2 * SWAP * width * j) for j in range(wide // (2 * SWAP * width))]


def packed(width, gate, up, down, high, low, keep, send, gate_here, up_here, down_here, sems):
    copies = [
        pltpu.make_async_copy(there, here, sems.at[k])
        for k, (there, here) in enumerate(((gate, gate_here), (up, up_here), (down, down_here)))
    ]
    for copy in copies:
        copy.start()
    half = high.shape[1]
    copies[0].wait()
    copies[1].wait()
    stacked(high, gate_here, up_here, half, half)
    stacked(low, gate_here, up_here)
    copies[2].wait()

    def run(mine):
        for near, there in runs(width, 2 * half):
            here = slice(near, near + SWAP * width)
            for out, which in ((keep, mine), (send, 1 - mine)):
                at = there + SWAP * width * which
                out[:, here] = down_here[:, at : at + SWAP * width]

    either(tensor_bit(SWAP), run)


def project_tiles(x, low, high):
    half = low.shape[1]
    tile = min(half, 1024)
    total = jnp.zeros((low.shape[0], x.shape[0]), F32)
    for at in range(0, half, tile):
        cut = slice(at, at + tile)
        total += dot(low[:, cut], x[:, cut], NT)
        total += dot(high[:, cut], x[:, half + at : half + at + tile], NT)
    return total


def project(x, low, high, both, hid_a, hid_b):
    rows = low.shape[0] // 2
    total = project_tiles(x, low, high)
    both[...] = total
    hidden = total * jax.nn.sigmoid(total) * pltpu.roll(total, rows, 0)
    hidden = jnp.where(top_rows(total), hidden, 0.0)
    hid_a[...] = hidden.astype(BF)
    hid_b[...] = pltpu.roll(hidden, rows, 0).astype(BF)


def project_first(x_there, g_there, low, high, x, g, both, hid_a, hid_b, sems):
    copies = [pltpu.make_async_copy(x_there, x, sems.at[0]), pltpu.make_async_copy(g_there, g, sems.at[1])]
    for copy in copies:
        copy.start()
    copies[0].wait()
    project(x, low, high, both, hid_a, hid_b)
    copies[1].wait()


def shares(width, g, down, part):
    wide = g.shape[1]
    tile = min(SWAP * width, 1024)

    def run(mine):
        total = jnp.zeros(part.shape, F32)
        for near, there in runs(width, wide):
            for at in range(0, SWAP * width, tile):
                far = there + SWAP * width * mine + at
                total += dot(down[:, near + at : near + at + tile], g[:, far : far + tile], NT)
        part[...] = total

    either(tensor_bit(SWAP), run)


def sent_share(part, hid_b):
    share = part[...]
    return jnp.where(top_rows(share), pltpu.roll(share, share.shape[0] // 2, 0), hid_b[...].astype(F32))


def finish(both, part, got, hid_a, pair, hid_pair):
    rows = both.shape[0] // 2
    gate, got = both[...], got[...]
    dhid = part[...] + got
    sig = jax.nn.sigmoid(gate)
    dgate = dhid * pltpu.roll(gate, rows, 0) * sig * (1.0 + gate * (1.0 - sig))
    dup = pltpu.roll(dhid * (gate * sig), rows, 0)
    first = top_rows(gate)
    pair[...] = jnp.where(first, dgate, dup).astype(BF)
    hid_pair[...] = jnp.where(first, hid_a[...].astype(F32), got).astype(BF)


def down_columns(g, hid_a, hid_b, at, half):
    cut = slice(at, at + TILE)
    return dot(hid_a[...], g[:, cut], NN) + dot(hid_b[...], g[:, half + at : half + at + TILE], NN)


def tiles(size):
    return [slice(at, min(at + TILE, size)) for at in range(0, size, TILE)]


def shifted(cut, offset):
    return slice(cut.start + offset, cut.stop + offset)


def own_grads(x, g, hid_a, hid_b, pair, low, high, down):
    half = down.shape[1]
    for out, offset in ((low, 0), (high, low.shape[1])):
        for cut in tiles(out.shape[1]):
            out[:, cut] = dot(pair[...], x[:, shifted(cut, offset)], NN)
    for at in range(0, half, TILE):
        down[:, at : at + TILE] = down_columns(g, hid_a, hid_b, at, half)


def sent_down(g, hid_a, hid_b, out):
    half = out.shape[1]
    for at in range(0, half, TILE):
        out[:, at : at + TILE] = down_columns(g, hid_a, hid_b, at, half).astype(BF)


def sent_pair(x, pair, low, high):
    for out, offset in ((low, 0), (high, low.shape[1])):
        for cut in tiles(out.shape[1]):
            out[:, cut] = dot(pair[...], x[:, shifted(cut, offset)], NN).astype(BF)


def kept(side, odd, four, wanted):
    value = side.astype(F32)
    return jnp.where(odd == wanted, value, 0.0) if four else value


def picked(here, piece, out):
    @pl.when(is_odd())
    def _():
        out[...] = here[...]

    @pl.when(jnp.logical_not(is_odd()))
    def _():
        out[...] = piece[...]


def other_columns(width, down, out, at):
    def run(mine):
        for k in range(down.shape[1] // (2 * width)):
            column = (2 * k + 1 - mine) * width
            out[:, at + k * width : at + (k + 1) * width] = down[:, column : column + width]

    either(tensor_bit(SECOND), run)


def output_sums(width, *refs):
    hids, downs, (two, last, send, keep) = refs[:3], refs[3:6], refs[6:]
    tokens, quarter = send.shape[0], downs[0].shape[1] // 2
    gots = ((two, 0), (two, quarter), (last, 0))
    tile = min(width, TILE)

    def run(here, mine):
        for block in range(2 * keep.shape[1] // width):
            out = keep if block % 2 == mine else send
            for at in range(0, width, tile):
                near, far = (2 * block + here) * width + at, block * width + at
                total = 0.0
                for k, (hid, down, (got, offset)) in enumerate(zip(hids, downs, gots)):
                    total += dot(hid[...], down[:, near : near + tile], TN)
                    other = last[:, quarter + k * tokens : quarter + (k + 1) * tokens]
                    total += dot(other, got[:, offset + far : offset + far + tile], TN)
                column = block // 2 * width + at
                out[:, column : column + tile] = total.astype(out.dtype)

    both_bits(run)


def halved(bit, width, keep, got, send, left):
    tile = min(width, TILE)

    def run(mine):
        for block in range(left.shape[1] // width):
            for out, which in ((send, 1 - mine), (left, mine)):
                for at in range(0, width, tile):
                    cols = slice((2 * block + which) * width + at, (2 * block + which) * width + at + tile)
                    value = keep[:, cols] + got[:, cols].astype(F32)
                    out[:, block * width + at : block * width + at + tile] = value.astype(out.dtype)

    either(tensor_bit(bit), run)


def final_output(keep, got, out, end):
    out[...] = (keep[...] + got[...].astype(F32)).astype(BF)
    end[...] = jnp.zeros_like(end)


def exchanged(value, axis, bit):
    count = lax.axis_size(axis)
    return lax.ppermute(value, axis, [(source, source ^ bit) for source in range(count)])


def ring_passed(value, steps):
    count = lax.axis_size("section")
    return lax.ppermute(value, "section", [(source, (source + steps) % count) for source in range(count)])


def on_device(x, g, gate_weight, up_weight, down_weight):
    rows, wide = gate_weight.shape
    half, both_rows, tokens = wide // 2, 2 * rows, x.shape[0]
    count = lax.axis_size("tensor")
    assert count > BITS[0] and count & (count - 1) == 0
    width = wide // count
    four = lax.axis_size("section") == 4
    piece, narrow = ((both_rows, half), BF), ((rows, half), BF)
    small, small_bf = ((both_rows, tokens), F32), ((both_rows, tokens), BF)
    step = Steps()

    def with_width(body):
        def run(*refs):
            body(width, *refs)

        return run

    def one_hop(value):
        return exchanged(value, "section", 2) if four else ring_passed(value, 1)

    def relay(here, value):
        if not four:
            return ring_passed(here, 1)
        return exchanged(step(picked, piece, [here, value]), "section", 1)

    def outward(value):
        return exchanged(value, "section", 1) if four else ring_passed(value, -1)

    def backward(value):
        return exchanged(value, "section", 2) if four else ring_passed(value, -1)

    own, first, second = [None] * 3, [None] * 3, [None] * 3
    held = pltpu.VMEM((rows, wide), BF)
    own[1], own[0], down_keep, down_send = step(
        with_width(packed),
        [piece, piece, narrow, narrow],
        [gate_weight, up_weight, down_weight],
        far=3,
        scratch=[held, held, held, pltpu.SemaphoreType.DMA((3,))],
    )
    first[1] = one_hop(own[1])
    down_got = exchanged(down_send, "tensor", SWAP)

    def joined(keep, got, out):
        stacked(out, keep, got)

    own[2] = step(joined, piece, [down_keep, down_got])
    if four:
        crossed = exchanged(own[2], "section", 1)
        onward = lax.ppermute(crossed, "section", [(source, source ^ 2) for source in (0, 2)])
    first[2] = one_hop(own[2])
    x, g, both_own, *hid_own = step(
        project_first,
        [(x.shape, BF), (g.shape, BF), small, small_bf, small_bf],
        [x, g, own[0], own[1]],
        far=2,
        scratch=[pltpu.SemaphoreType.DMA((2,))],
    )
    first[0] = one_hop(step.hold(own[0]))
    share = with_width(shares)
    share_own = step(share, small, [g, own[2]])
    second[1] = relay(first[1], own[1])
    second[0] = relay(first[0], own[0])
    both_first, *hid_first = step(project, [small, small_bf, small_bf], [x, first[0], first[1]], also=[second[1]])
    second[2] = step(picked, piece, [crossed, onward]) if four else ring_passed(first[2], 1)
    share_second = step(share, small, [g, second[2]])

    def two_other(down_a, down_b, out):
        other_columns(width, down_a, out, 0)
        other_columns(width, down_b, out, half // 2)

    two_theirs = exchanged(step(two_other, piece, [own[2], second[2]]), "tensor", SECOND)
    both_second, *hid_second = step(project, [small, small_bf, small_bf], [x, second[0], second[1]])

    def two_sent(share_a, hid_a, share_b, hid_b, out):
        out[:both_rows, :] = sent_share(share_a, hid_a)
        out[both_rows:, :] = sent_share(share_b, hid_b)

    sent = step(two_sent, ((2 * both_rows, tokens), F32), [share_own, hid_own[1], share_second, hid_second[1]])
    got_two = exchanged(sent, "tensor", SWAP)
    side_down = outward(step(sent_down, piece, [g, *hid_second]))

    def finish_two(both_a, part_a, hid_a, both_b, part_b, hid_b, got, pair_a, out_a, pair_b, out_b):
        finish(both_a, part_a, got.at[:both_rows, :], hid_a, pair_a, out_a)
        finish(both_b, part_b, got.at[both_rows:, :], hid_b, pair_b, out_b)

    pair_own, wide_own, pair_second, wide_second = step(
        finish_two, [small_bf] * 4, [both_own, share_own, hid_own[0], both_second, share_second, hid_second[0], got_two]
    )
    low_columns = half + 128
    low_shape, high_shape = (both_rows, low_columns), (both_rows, wide - low_columns)
    low, high = step(sent_pair, [(low_shape, BF), (high_shape, BF)], [x, pair_second])

    def one_sent(gr, down, hid, part, out):
        shares(width, gr, down, part)
        out[...] = sent_share(part, hid)

    share_first, sent = step(one_sent, [small, small], [g, first[2], hid_first[1]], also=[two_theirs])
    got_one = exchanged(sent, "tensor", SWAP)
    side_low = outward(step.hold(low))
    grads_f32 = [(low_shape, F32), (high_shape, F32), ((both_rows, half), F32)]

    def finish_last(both, share, got, hid, wide_a, wide_b, down, pair, wide_out, out):
        finish(both, share, got, hid, pair, wide_out)
        other_columns(width, down, out, 0)
        for k, ref in enumerate((wide_a, wide_b, wide_out)):
            out[:, half // 2 + k * tokens : half // 2 + (k + 1) * tokens] = ref[...]

    pair_first, wide_first, sent = step(
        finish_last,
        [small_bf, small_bf, ((both_rows, half // 2 + 3 * tokens), BF)],
        [both_first, share_first, got_one, hid_first[0], wide_own, wide_second, first[2]],
    )
    last_theirs = exchanged(sent, "tensor", SECOND)
    def back_down(gr, a, b, side, out):
        odd = is_odd()
        for at in range(0, half, TILE):
            value = down_columns(gr, a, b, at, half) + kept(side[:, at : at + TILE], odd, four, True)
            out[:, at : at + TILE] = value.astype(BF)

    def back_pair(offset):
        def body(xr, pair, side, out):
            odd = is_odd()
            for cut in tiles(out.shape[1]):
                value = dot(pair[...], xr[:, shifted(cut, offset)], NN)
                out[:, cut] = (value + kept(side[:, cut], odd, four, True)).astype(BF)

        return body

    back_of_down = backward(step(back_down, piece, [g, *hid_first, side_down]))
    own_low, own_high, own_down = step(own_grads, grads_f32, [x, g, *hid_own, pair_own])
    side_high = outward(step.hold(high))
    back_of_low = backward(step(back_pair(0), (low_shape, BF), [x, pair_first, side_low]))
    send, keep = step(
        with_width(output_sums),
        [((tokens, wide // 8), BF), ((tokens, wide // 8), F32)],
        [wide_own, wide_second, wide_first, own[2], second[2], first[2], two_theirs, last_theirs],
    )
    got = exchanged(send, "tensor", BITS[0])

    def next_half(keep, got, bit):
        cols = keep.shape[1] // 2

        def body(*refs):
            halved(bit, width, *refs)

        send, keep = step(body, [((tokens, cols), BF), ((tokens, cols), F32)], [keep, got])
        return keep, exchanged(send, "tensor", bit)

    back_of_high = backward(step(back_pair(low_columns), (high_shape, BF), [x, pair_first, side_high], also=[back_of_down]))
    bit = 2 * BITS[0]
    while bit < count:
        keep, got = next_half(keep, got, bit)
        bit *= 2

    def finished(own_ref, back, side, odd, cut):
        value = own_ref[:, cut] + back[:, cut].astype(F32)
        return value + kept(side[:, cut], odd, four, False) if four else value

    def final_down(own_ref, back, side, out):
        odd = is_odd()
        for at in range(0, half, TILE):
            cut = slice(at, at + TILE)
            value = finished(own_ref, back, side, odd, cut)
            out[:, cut] = value[:rows]
            out[:, half + at : half + at + TILE] = value[rows:]

    def final_pair(low_ref, high_ref, low_back, high_back, low_side, high_side, out_gate, out_up):
        odd = is_odd()
        for offset, refs in ((0, (low_ref, low_back, low_side)), (low_columns, (high_ref, high_back, high_side))):
            for cut in tiles(refs[0].shape[1]):
                value = finished(*refs, odd, cut)
                out_gate[:, shifted(cut, offset)] = value[:rows]
                out_up[:, shifted(cut, offset)] = value[rows:]

    whole = ((rows, wide), F32)
    grad_down = step(final_down, whole, [own_down, back_of_down, side_down])
    output, end = step(final_output, [((tokens, width), BF), ((128, 128), F32)], [keep, got])
    end = exchanged(end, "tensor", SWAP)
    grad_gate, grad_up = step(
        final_pair,
        [whole, whole],
        [own_low, own_high, back_of_low, back_of_high, side_low, side_high],
        also=[end],
    )
    return (output, grad_gate, grad_up, grad_down)


def solution(mesh):
    placed = (
        P("section", None),
        P("section", None),
        P(("section", "tensor"), None),
        P(("section", "tensor"), None),
        P(("section", "tensor"), None),
    )
    return jax.shard_map(
        on_device,
        mesh=mesh,
        in_specs=placed,
        out_specs=(
            P("section", "tensor"),
            P(("section", "tensor"), None),
            P(("section", "tensor"), None),
            P(("section", "tensor"), None),
        ),
        check_vma=False,
    )
```

```python
import jax
import jax.numpy as jnp
from jax import lax
from jax.experimental import pallas as pl
from jax.experimental.pallas import tpu as pltpu
from jax.sharding import PartitionSpec as P

BF = jnp.bfloat16
F32 = jnp.float32
NN = (((1,), (0,)), ((), ()))
NT = (((1,), (1,)), ((), ()))
TN = (((0,), (0,)), ((), ()))
TILE = 512
SWAP = 1
SECOND = 2
BITS = (4,)


def dot(left, right, dims):
    return lax.dot_general(left, right, dims, preferred_element_type=F32)


class Steps:
    def __init__(self):
        self.mark = None

    def __call__(self, body, outs, ins, also=(), far=0, scratch=()):
        marks = [*also] if self.mark is None else [*also, self.mark]
        count = len(ins)
        ins = [pltpu.with_memory_space_constraint(v, pltpu.HBM) if k < far else v for k, v in enumerate(ins)]

        def kernel(*refs):
            last = count + len(marks) + len(shapes)
            body(*refs[:count], *refs[count + len(marks) : last - 1], *refs[last:])
            refs[last - 1][...] = jnp.zeros_like(refs[last - 1])

        single = isinstance(outs, tuple)
        shapes = ([outs] if single else list(outs)) + [((8, 128), F32)]
        *got, self.mark = pl.pallas_call(
            kernel,
            out_shape=[jax.ShapeDtypeStruct(*s) for s in shapes],
            in_specs=[pl.BlockSpec(memory_space=pltpu.HBM)] * far
            + [pl.BlockSpec(memory_space=pltpu.VMEM)] * (count + len(marks) - far),
            out_specs=[pl.BlockSpec(memory_space=pltpu.VMEM)] * len(shapes),
            scratch_shapes=list(scratch),
            compiler_params=pltpu.CompilerParams(vmem_limit_bytes=24 * 1024 * 1024),
            cost_estimate=pl.CostEstimate(flops=1, bytes_accessed=1, transcendentals=0),
        )(*ins, *marks)
        return got[0] if single else got

    def hold(self, value):
        value, self.mark = lax.optimization_barrier((value, self.mark))
        return value


def either(bit, run):
    for value in range(2):
        pl.when(bit == value)(lambda value=value: run(value))


def tensor_bit(bit):
    return lax.rem(lax.div(lax.axis_index("tensor"), bit), 2)


def both_bits(run):
    either(tensor_bit(SECOND), lambda here: either(tensor_bit(BITS[0]), lambda mine: run(here, mine)))


def is_odd():
    return lax.rem(lax.axis_index("section"), 2) == 1


def top_rows(like):
    return lax.broadcasted_iota(jnp.int32, like.shape, 0) < like.shape[0] // 2


def placed(rows):
    shape = (2 * rows, rows)
    place = lax.broadcasted_iota(jnp.int32, shape, 0) - lax.broadcasted_iota(jnp.int32, shape, 1)
    return [(place == shift).astype(F32).astype(BF) for shift in (0, rows)]


def stacked(out, upper, lower, upper_at=0, lower_at=0):
    top, bottom = placed(upper.shape[0])
    for at in range(0, out.shape[1], TILE):
        first, second = slice(upper_at + at, upper_at + at + TILE), slice(lower_at + at, lower_at + at + TILE)
        out[:, at : at + TILE] = (dot(top, upper[:, first], NN) + dot(bottom, lower[:, second], NN)).astype(BF)


def runs(width, wide):
    return [(SWAP * width * j, 2 * SWAP * width * j) for j in range(wide // (2 * SWAP * width))]


def packed(width, gate, up, down, high, low, keep, send, gate_here, up_here, down_here, sems):
    copies = [
        pltpu.make_async_copy(there, here, sems.at[k])
        for k, (there, here) in enumerate(((gate, gate_here), (up, up_here), (down, down_here)))
    ]
    for copy in copies:
        copy.start()
    half = high.shape[1]
    copies[0].wait()
    copies[1].wait()
    stacked(high, gate_here, up_here, half, half)
    stacked(low, gate_here, up_here)
    copies[2].wait()

    def run(mine):
        for near, there in runs(width, 2 * half):
            here = slice(near, near + SWAP * width)
            for out, which in ((keep, mine), (send, 1 - mine)):
                at = there + SWAP * width * which
                out[:, here] = down_here[:, at : at + SWAP * width]

    either(tensor_bit(SWAP), run)


def project_tiles(x, low, high):
    half = low.shape[1]
    tile = min(half, 1024)
    total = jnp.zeros((low.shape[0], x.shape[0]), F32)
    for at in range(0, half, tile):
        cut = slice(at, at + tile)
        total += dot(low[:, cut], x[:, cut], NT)
        total += dot(high[:, cut], x[:, half + at : half + at + tile], NT)
    return total


def project(x, low, high, both, hid_a, hid_b):
    rows = low.shape[0] // 2
    total = project_tiles(x, low, high)
    both[...] = total
    hidden = total * jax.nn.sigmoid(total) * pltpu.roll(total, rows, 0)
    hidden = jnp.where(top_rows(total), hidden, 0.0)
    hid_a[...] = hidden.astype(BF)
    hid_b[...] = pltpu.roll(hidden, rows, 0).astype(BF)


def project_first(x_there, g_there, low, high, x, g, both, hid_a, hid_b, sems):
    copies = [pltpu.make_async_copy(x_there, x, sems.at[0]), pltpu.make_async_copy(g_there, g, sems.at[1])]
    for copy in copies:
        copy.start()
    copies[0].wait()
    project(x, low, high, both, hid_a, hid_b)
    copies[1].wait()


def shares(width, g, down, part):
    wide = g.shape[1]
    tile = min(SWAP * width, 1024)

    def run(mine):
        total = jnp.zeros(part.shape, F32)
        for near, there in runs(width, wide):
            for at in range(0, SWAP * width, tile):
                far = there + SWAP * width * mine + at
                total += dot(down[:, near + at : near + at + tile], g[:, far : far + tile], NT)
        part[...] = total

    either(tensor_bit(SWAP), run)


def sent_share(part, hid_b):
    share = part[...]
    return jnp.where(top_rows(share), pltpu.roll(share, share.shape[0] // 2, 0), hid_b[...].astype(F32))


def finish(both, part, got, hid_a, pair, hid_pair):
    rows = both.shape[0] // 2
    gate, got = both[...], got[...]
    dhid = part[...] + got
    sig = jax.nn.sigmoid(gate)
    dgate = dhid * pltpu.roll(gate, rows, 0) * sig * (1.0 + gate * (1.0 - sig))
    dup = pltpu.roll(dhid * (gate * sig), rows, 0)
    first = top_rows(gate)
    pair[...] = jnp.where(first, dgate, dup).astype(BF)
    hid_pair[...] = jnp.where(first, hid_a[...].astype(F32), got).astype(BF)


def down_columns(g, hid_a, hid_b, at, half):
    cut = slice(at, at + TILE)
    return dot(hid_a[...], g[:, cut], NN) + dot(hid_b[...], g[:, half + at : half + at + TILE], NN)


def tiles(size):
    return [slice(at, min(at + TILE, size)) for at in range(0, size, TILE)]


def shifted(cut, offset):
    return slice(cut.start + offset, cut.stop + offset)


def own_grads(x, g, hid_a, hid_b, pair, low, high, down):
    half = down.shape[1]
    for out, offset in ((low, 0), (high, low.shape[1])):
        for cut in tiles(out.shape[1]):
            out[:, cut] = dot(pair[...], x[:, shifted(cut, offset)], NN)
    for at in range(0, half, TILE):
        down[:, at : at + TILE] = down_columns(g, hid_a, hid_b, at, half)


def sent_down(g, hid_a, hid_b, out):
    half = out.shape[1]
    for at in range(0, half, TILE):
        out[:, at : at + TILE] = down_columns(g, hid_a, hid_b, at, half).astype(BF)


def sent_pair(x, pair, low, high):
    for out, offset in ((low, 0), (high, low.shape[1])):
        for cut in tiles(out.shape[1]):
            out[:, cut] = dot(pair[...], x[:, shifted(cut, offset)], NN).astype(BF)


def kept(side, odd, four, wanted):
    value = side.astype(F32)
    return jnp.where(odd == wanted, value, 0.0) if four else value


def picked(here, piece, out):
    @pl.when(is_odd())
    def _():
        out[...] = here[...]

    @pl.when(jnp.logical_not(is_odd()))
    def _():
        out[...] = piece[...]


def other_columns(width, down, out, at):
    def run(mine):
        for k in range(down.shape[1] // (2 * width)):
            column = (2 * k + 1 - mine) * width
            out[:, at + k * width : at + (k + 1) * width] = down[:, column : column + width]

    either(tensor_bit(SECOND), run)


def output_sums(width, *refs):
    hids, downs, (two, last, send, keep) = refs[:3], refs[3:6], refs[6:]
    tokens, quarter = send.shape[0], downs[0].shape[1] // 2
    gots = ((two, 0), (two, quarter), (last, 0))
    tile = min(width, TILE)

    def run(here, mine):
        for block in range(2 * keep.shape[1] // width):
            out = keep if block % 2 == mine else send
            for at in range(0, width, tile):
                near, far = (2 * block + here) * width + at, block * width + at
                total = 0.0
                for k, (hid, down, (got, offset)) in enumerate(zip(hids, downs, gots)):
                    total += dot(hid[...], down[:, near : near + tile], TN)
                    other = last[:, quarter + k * tokens : quarter + (k + 1) * tokens]
                    total += dot(other, got[:, offset + far : offset + far + tile], TN)
                column = block // 2 * width + at
                out[:, column : column + tile] = total.astype(out.dtype)

    both_bits(run)


def halved(bit, width, keep, got, send, left):
    tile = min(width, TILE)

    def run(mine):
        for block in range(left.shape[1] // width):
            for out, which in ((send, 1 - mine), (left, mine)):
                for at in range(0, width, tile):
                    cols = slice((2 * block + which) * width + at, (2 * block + which) * width + at + tile)
                    value = keep[:, cols] + got[:, cols].astype(F32)
                    out[:, block * width + at : block * width + at + tile] = value.astype(out.dtype)

    either(tensor_bit(bit), run)


def final_output(keep, got, out):
    out[...] = (keep[...] + got[...].astype(F32)).astype(BF)


def exchanged(value, axis, bit):
    count = lax.axis_size(axis)
    return lax.ppermute(value, axis, [(source, source ^ bit) for source in range(count)])


def ring_passed(value, steps):
    count = lax.axis_size("section")
    return lax.ppermute(value, "section", [(source, (source + steps) % count) for source in range(count)])


def on_device(x, g, gate_weight, up_weight, down_weight):
    rows, wide = gate_weight.shape
    half, both_rows, tokens = wide // 2, 2 * rows, x.shape[0]
    count = lax.axis_size("tensor")
    assert count > BITS[0] and count & (count - 1) == 0
    width = wide // count
    four = lax.axis_size("section") == 4
    piece, narrow = ((both_rows, half), BF), ((rows, half), BF)
    small, small_bf = ((both_rows, tokens), F32), ((both_rows, tokens), BF)
    step = Steps()

    def with_width(body):
        def run(*refs):
            body(width, *refs)

        return run

    def one_hop(value):
        return exchanged(value, "section", 2) if four else ring_passed(value, 1)

    def relay(here, value):
        if not four:
            return ring_passed(here, 1)
        return exchanged(step(picked, piece, [here, value]), "section", 1)

    def outward(value):
        return exchanged(value, "section", 1) if four else ring_passed(value, -1)

    def backward(value):
        return exchanged(value, "section", 2) if four else ring_passed(value, -1)

    own, first, second = [None] * 3, [None] * 3, [None] * 3
    held = pltpu.VMEM((rows, wide), BF)
    own[1], own[0], down_keep, down_send = step(
        with_width(packed),
        [piece, piece, narrow, narrow],
        [gate_weight, up_weight, down_weight],
        far=3,
        scratch=[held, held, held, pltpu.SemaphoreType.DMA((3,))],
    )
    first[1] = one_hop(own[1])
    down_got = exchanged(down_send, "tensor", SWAP)

    def joined(keep, got, out):
        stacked(out, keep, got)

    own[2] = step(joined, piece, [down_keep, down_got])
    if four:
        crossed = exchanged(own[2], "section", 1)
        onward = lax.ppermute(crossed, "section", [(source, source ^ 2) for source in (0, 2)])
    first[2] = one_hop(own[2])
    x, g, both_own, *hid_own = step(
        project_first,
        [(x.shape, BF), (g.shape, BF), small, small_bf, small_bf],
        [x, g, own[0], own[1]],
        far=2,
        scratch=[pltpu.SemaphoreType.DMA((2,))],
    )
    first[0] = one_hop(step.hold(own[0]))
    share = with_width(shares)
    share_own = step(share, small, [g, own[2]])
    second[1] = relay(first[1], own[1])
    second[0] = relay(first[0], own[0])
    both_first, *hid_first = step(project, [small, small_bf, small_bf], [x, first[0], first[1]], also=[second[1]])
    second[2] = step(picked, piece, [crossed, onward]) if four else ring_passed(first[2], 1)
    share_second = step(share, small, [g, second[2]])

    def two_other(down_a, down_b, out):
        other_columns(width, down_a, out, 0)
        other_columns(width, down_b, out, half // 2)

    two_theirs = exchanged(step(two_other, piece, [own[2], second[2]]), "tensor", SECOND)
    both_second, *hid_second = step(project, [small, small_bf, small_bf], [x, second[0], second[1]])

    def two_sent(share_a, hid_a, share_b, hid_b, out):
        out[:both_rows, :] = sent_share(share_a, hid_a)
        out[both_rows:, :] = sent_share(share_b, hid_b)

    sent = step(two_sent, ((2 * both_rows, tokens), F32), [share_own, hid_own[1], share_second, hid_second[1]])
    got_two = exchanged(sent, "tensor", SWAP)
    side_down = outward(step(sent_down, piece, [g, *hid_second]))

    def finish_two(both_a, part_a, hid_a, both_b, part_b, hid_b, got, pair_a, out_a, pair_b, out_b):
        finish(both_a, part_a, got.at[:both_rows, :], hid_a, pair_a, out_a)
        finish(both_b, part_b, got.at[both_rows:, :], hid_b, pair_b, out_b)

    pair_own, wide_own, pair_second, wide_second = step(
        finish_two, [small_bf] * 4, [both_own, share_own, hid_own[0], both_second, share_second, hid_second[0], got_two]
    )
    low_columns = half + 128
    low_shape, high_shape = (both_rows, low_columns), (both_rows, wide - low_columns)
    low, high = step(sent_pair, [(low_shape, BF), (high_shape, BF)], [x, pair_second])

    grads_f32 = [(low_shape, F32), (high_shape, F32), ((both_rows, half), F32)]
    own_low, own_high, own_down = step(own_grads, grads_f32, [x, g, *hid_own, pair_own])

    def one_sent(gr, down, hid, part, out):
        shares(width, gr, down, part)
        out[...] = sent_share(part, hid)

    share_first, sent = step(one_sent, [small, small], [g, first[2], hid_first[1]], also=[two_theirs])
    got_one = exchanged(sent, "tensor", SWAP)
    side_low = outward(step.hold(low))

    def finish_last(both, share, got, hid, wide_a, wide_b, down, pair, wide_out, out):
        finish(both, share, got, hid, pair, wide_out)
        other_columns(width, down, out, 0)
        for k, ref in enumerate((wide_a, wide_b, wide_out)):
            out[:, half // 2 + k * tokens : half // 2 + (k + 1) * tokens] = ref[...]

    pair_first, wide_first, sent = step(
        finish_last,
        [small_bf, small_bf, ((both_rows, half // 2 + 3 * tokens), BF)],
        [both_first, share_first, got_one, hid_first[0], wide_own, wide_second, first[2]],
    )
    last_theirs = exchanged(sent, "tensor", SECOND)
    def back_down(gr, a, b, side, out):
        odd = is_odd()
        for at in range(0, half, TILE):
            value = down_columns(gr, a, b, at, half) + kept(side[:, at : at + TILE], odd, four, True)
            out[:, at : at + TILE] = value.astype(BF)

    def back_pair(offset):
        def body(xr, pair, side, out):
            odd = is_odd()
            for cut in tiles(out.shape[1]):
                value = dot(pair[...], xr[:, shifted(cut, offset)], NN)
                out[:, cut] = (value + kept(side[:, cut], odd, four, True)).astype(BF)

        return body

    back_of_down = backward(step(back_down, piece, [g, *hid_first, side_down]))
    side_high = outward(step.hold(high))
    back_of_low = backward(step(back_pair(0), (low_shape, BF), [x, pair_first, side_low]))
    send, keep = step(
        with_width(output_sums),
        [((tokens, wide // 8), BF), ((tokens, wide // 8), F32)],
        [wide_own, wide_second, wide_first, own[2], second[2], first[2], two_theirs, last_theirs],
    )
    got = exchanged(send, "tensor", BITS[0])

    def next_half(keep, got, bit):
        cols = keep.shape[1] // 2

        def body(*refs):
            halved(bit, width, *refs)

        send, keep = step(body, [((tokens, cols), BF), ((tokens, cols), F32)], [keep, got])
        return keep, exchanged(send, "tensor", bit)

    high_columns = wide - low_columns
    cut_at = high_columns // 256 * 128
    high_shapes = [(both_rows, cut_at), (both_rows, high_columns - cut_at)]

    def back_last(xr, pair, side, out_a, out_b):
        odd = is_odd()
        for out, offset in ((out_a, 0), (out_b, cut_at)):
            for cut in tiles(out.shape[1]):
                value = dot(pair[...], xr[:, shifted(cut, low_columns + offset)], NN)
                value += kept(side[:, shifted(cut, offset)], odd, four, True)
                out[:, cut] = value.astype(BF)

    backs_of_high = [
        backward(value)
        for value in step(
            back_last, [(shape, BF) for shape in high_shapes], [x, pair_first, side_high], also=[back_of_down]
        )
    ]
    bit = 2 * BITS[0]
    while bit < count:
        keep, got = next_half(keep, got, bit)
        bit *= 2

    def finished(own_ref, back, side, odd, cut):
        value = own_ref[:, cut] + back[:, cut].astype(F32)
        return value + kept(side[:, cut], odd, four, False) if four else value

    def final_down(own_ref, back, side, out):
        odd = is_odd()
        for at in range(0, half, TILE):
            cut = slice(at, at + TILE)
            value = finished(own_ref, back, side, odd, cut)
            out[:, cut] = value[:rows]
            out[:, half + at : half + at + TILE] = value[rows:]

    def final_pair(low_ref, high_ref, low_back, back_a, back_b, low_side, high_side, out_gate, out_up):
        odd = is_odd()
        pieces = (
            (low_ref, low_back, low_side, 0, 0, low_columns),
            (high_ref, back_a, high_side, 0, low_columns, cut_at),
            (high_ref, back_b, high_side, cut_at, low_columns + cut_at, high_columns - cut_at),
        )
        for own_ref, back, side, inside, offset, columns in pieces:
            for cut in tiles(columns):
                from_ = shifted(cut, inside)
                value = own_ref[:, from_] + back[:, cut].astype(F32)
                if four:
                    value += kept(side[:, from_], odd, four, False)
                out_gate[:, shifted(cut, offset)] = value[:rows]
                out_up[:, shifted(cut, offset)] = value[rows:]

    whole = ((rows, wide), F32)
    grad_down = step(final_down, whole, [own_down, back_of_down, side_down])
    output = step(final_output, ((tokens, width), BF), [keep, got])
    grad_gate, grad_up = step(
        final_pair,
        [whole, whole],
        [own_low, own_high, back_of_low, *backs_of_high, side_low, side_high],
    )
    return (output, grad_gate, grad_up, grad_down)


def solution(mesh):
    placed = (
        P("section", None),
        P("section", None),
        P(("section", "tensor"), None),
        P(("section", "tensor"), None),
        P(("section", "tensor"), None),
    )
    return jax.shard_map(
        on_device,
        mesh=mesh,
        in_specs=placed,
        out_specs=(
            P("section", "tensor"),
            P(("section", "tensor"), None),
            P(("section", "tensor"), None),
            P(("section", "tensor"), None),
        ),
        check_vma=False,
    )
```

```python
import jax
import jax.numpy as jnp
from jax import lax
from jax.experimental import pallas as pl
from jax.experimental.pallas import tpu as pltpu
from jax.sharding import PartitionSpec as P

BF = jnp.bfloat16
F32 = jnp.float32
NN = (((1,), (0,)), ((), ()))
NT = (((1,), (1,)), ((), ()))
TN = (((0,), (0,)), ((), ()))
TILE = 512
SWAP = 1
SECOND = 2
BITS = (4,)


def dot(left, right, dims):
    return lax.dot_general(left, right, dims, preferred_element_type=F32)


class Steps:
    def __init__(self):
        self.mark = None

    def __call__(self, body, outs, ins, also=(), far=0, scratch=()):
        marks = [*also] if self.mark is None else [*also, self.mark]
        count = len(ins)
        ins = [pltpu.with_memory_space_constraint(v, pltpu.HBM) if k < far else v for k, v in enumerate(ins)]

        def kernel(*refs):
            last = count + len(marks) + len(shapes)
            body(*refs[:count], *refs[count + len(marks) : last - 1], *refs[last:])
            refs[last - 1][...] = jnp.zeros_like(refs[last - 1])

        single = isinstance(outs, tuple)
        shapes = ([outs] if single else list(outs)) + [((8, 128), F32)]
        *got, self.mark = pl.pallas_call(
            kernel,
            out_shape=[jax.ShapeDtypeStruct(*s) for s in shapes],
            in_specs=[pl.BlockSpec(memory_space=pltpu.HBM)] * far
            + [pl.BlockSpec(memory_space=pltpu.VMEM)] * (count + len(marks) - far),
            out_specs=[pl.BlockSpec(memory_space=pltpu.VMEM)] * len(shapes),
            scratch_shapes=list(scratch),
            compiler_params=pltpu.CompilerParams(vmem_limit_bytes=24 * 1024 * 1024),
            cost_estimate=pl.CostEstimate(flops=1, bytes_accessed=1, transcendentals=0),
        )(*ins, *marks)
        return got[0] if single else got

    def hold(self, value):
        value, self.mark = lax.optimization_barrier((value, self.mark))
        return value


def either(bit, run):
    for value in range(2):
        pl.when(bit == value)(lambda value=value: run(value))


def tensor_bit(bit):
    return lax.rem(lax.div(lax.axis_index("tensor"), bit), 2)


def both_bits(run):
    either(tensor_bit(SECOND), lambda here: either(tensor_bit(BITS[0]), lambda mine: run(here, mine)))


def is_odd():
    return lax.rem(lax.axis_index("section"), 2) == 1


def top_rows(like):
    return lax.broadcasted_iota(jnp.int32, like.shape, 0) < like.shape[0] // 2


def placed(rows):
    shape = (2 * rows, rows)
    place = lax.broadcasted_iota(jnp.int32, shape, 0) - lax.broadcasted_iota(jnp.int32, shape, 1)
    return [(place == shift).astype(F32).astype(BF) for shift in (0, rows)]


def stacked(out, upper, lower, upper_at=0, lower_at=0):
    top, bottom = placed(upper.shape[0])
    for at in range(0, out.shape[1], TILE):
        first, second = slice(upper_at + at, upper_at + at + TILE), slice(lower_at + at, lower_at + at + TILE)
        out[:, at : at + TILE] = (dot(top, upper[:, first], NN) + dot(bottom, lower[:, second], NN)).astype(BF)


def runs(width, wide):
    return [(SWAP * width * j, 2 * SWAP * width * j) for j in range(wide // (2 * SWAP * width))]


def packed(width, gate, up, down, high, low, keep, send, gate_here, up_here, down_here, sems):
    copies = [
        pltpu.make_async_copy(there, here, sems.at[k])
        for k, (there, here) in enumerate(((gate, gate_here), (up, up_here), (down, down_here)))
    ]
    for copy in copies:
        copy.start()
    half = high.shape[1]
    copies[0].wait()
    copies[1].wait()
    stacked(high, gate_here, up_here, half, half)
    stacked(low, gate_here, up_here)
    copies[2].wait()

    def run(mine):
        for near, there in runs(width, 2 * half):
            here = slice(near, near + SWAP * width)
            for out, which in ((keep, mine), (send, 1 - mine)):
                at = there + SWAP * width * which
                out[:, here] = down_here[:, at : at + SWAP * width]

    either(tensor_bit(SWAP), run)


def project_tiles(x, low, high):
    half = low.shape[1]
    tile = min(half, 1024)
    total = jnp.zeros((low.shape[0], x.shape[0]), F32)
    for at in range(0, half, tile):
        cut = slice(at, at + tile)
        total += dot(low[:, cut], x[:, cut], NT)
        total += dot(high[:, cut], x[:, half + at : half + at + tile], NT)
    return total


def project(x, low, high, both, hid_a, hid_b):
    rows = low.shape[0] // 2
    total = project_tiles(x, low, high)
    both[...] = total
    hidden = total * jax.nn.sigmoid(total) * pltpu.roll(total, rows, 0)
    hidden = jnp.where(top_rows(total), hidden, 0.0)
    hid_a[...] = hidden.astype(BF)
    hid_b[...] = pltpu.roll(hidden, rows, 0).astype(BF)


def project_first(x_there, g_there, low, high, x, g, both, hid_a, hid_b, sems):
    copies = [pltpu.make_async_copy(x_there, x, sems.at[0]), pltpu.make_async_copy(g_there, g, sems.at[1])]
    for copy in copies:
        copy.start()
    copies[0].wait()
    project(x, low, high, both, hid_a, hid_b)
    copies[1].wait()


def shares(width, g, down, part):
    wide = g.shape[1]
    tile = min(SWAP * width, 1024)

    def run(mine):
        total = jnp.zeros(part.shape, F32)
        for near, there in runs(width, wide):
            for at in range(0, SWAP * width, tile):
                far = there + SWAP * width * mine + at
                total += dot(down[:, near + at : near + at + tile], g[:, far : far + tile], NT)
        part[...] = total

    either(tensor_bit(SWAP), run)


def sent_share(part, hid_b):
    share = part[...]
    return jnp.where(top_rows(share), pltpu.roll(share, share.shape[0] // 2, 0), hid_b[...].astype(F32))


def finish(both, part, got, hid_a, pair, hid_pair):
    rows = both.shape[0] // 2
    gate, got = both[...], got[...]
    dhid = part[...] + got
    sig = jax.nn.sigmoid(gate)
    dgate = dhid * pltpu.roll(gate, rows, 0) * sig * (1.0 + gate * (1.0 - sig))
    dup = pltpu.roll(dhid * (gate * sig), rows, 0)
    first = top_rows(gate)
    pair[...] = jnp.where(first, dgate, dup).astype(BF)
    hid_pair[...] = jnp.where(first, hid_a[...].astype(F32), got).astype(BF)


def down_columns(g, hid_a, hid_b, at, half):
    cut = slice(at, at + TILE)
    return dot(hid_a[...], g[:, cut], NN) + dot(hid_b[...], g[:, half + at : half + at + TILE], NN)


def tiles(size):
    return [slice(at, min(at + TILE, size)) for at in range(0, size, TILE)]


def shifted(cut, offset):
    return slice(cut.start + offset, cut.stop + offset)


def own_grads(x, g, hid_a, hid_b, pair, low, high, down):
    half = down.shape[1]
    for out, offset in ((low, 0), (high, low.shape[1])):
        for cut in tiles(out.shape[1]):
            out[:, cut] = dot(pair[...], x[:, shifted(cut, offset)], NN)
    for at in range(0, half, TILE):
        down[:, at : at + TILE] = down_columns(g, hid_a, hid_b, at, half)


def sent_down(g, hid_a, hid_b, out):
    half = out.shape[1]
    for at in range(0, half, TILE):
        out[:, at : at + TILE] = down_columns(g, hid_a, hid_b, at, half).astype(BF)


def sent_pair(x, pair, low, high):
    for out, offset in ((low, 0), (high, low.shape[1])):
        for cut in tiles(out.shape[1]):
            out[:, cut] = dot(pair[...], x[:, shifted(cut, offset)], NN).astype(BF)


def kept(side, odd, four, wanted):
    value = side.astype(F32)
    return jnp.where(odd == wanted, value, 0.0) if four else value


def picked(here, piece, out):
    @pl.when(is_odd())
    def _():
        out[...] = here[...]

    @pl.when(jnp.logical_not(is_odd()))
    def _():
        out[...] = piece[...]


def other_columns(width, down, out, at):
    def run(mine):
        for k in range(down.shape[1] // (2 * width)):
            column = (2 * k + 1 - mine) * width
            out[:, at + k * width : at + (k + 1) * width] = down[:, column : column + width]

    either(tensor_bit(SECOND), run)


def output_sums(width, *refs):
    hids, downs, (two, last, send, keep) = refs[:3], refs[3:6], refs[6:]
    tokens, quarter = send.shape[0], downs[0].shape[1] // 2
    gots = ((two, 0), (two, quarter), (last, 0))
    tile = min(width, TILE)

    def run(here, mine):
        for block in range(2 * keep.shape[1] // width):
            out = keep if block % 2 == mine else send
            for at in range(0, width, tile):
                near, far = (2 * block + here) * width + at, block * width + at
                total = 0.0
                for k, (hid, down, (got, offset)) in enumerate(zip(hids, downs, gots)):
                    total += dot(hid[...], down[:, near : near + tile], TN)
                    other = last[:, quarter + k * tokens : quarter + (k + 1) * tokens]
                    total += dot(other, got[:, offset + far : offset + far + tile], TN)
                column = block // 2 * width + at
                out[:, column : column + tile] = total.astype(out.dtype)

    both_bits(run)


def halved(bit, width, keep, got, send, left):
    tile = min(width, TILE)

    def run(mine):
        for block in range(left.shape[1] // width):
            for out, which in ((send, 1 - mine), (left, mine)):
                for at in range(0, width, tile):
                    cols = slice((2 * block + which) * width + at, (2 * block + which) * width + at + tile)
                    value = keep[:, cols] + got[:, cols].astype(F32)
                    out[:, block * width + at : block * width + at + tile] = value.astype(out.dtype)

    either(tensor_bit(bit), run)


def final_output(keep, got, out):
    out[...] = (keep[...] + got[...].astype(F32)).astype(BF)


def exchanged(value, axis, bit):
    count = lax.axis_size(axis)
    return lax.ppermute(value, axis, [(source, source ^ bit) for source in range(count)])


def ring_passed(value, steps):
    count = lax.axis_size("section")
    return lax.ppermute(value, "section", [(source, (source + steps) % count) for source in range(count)])


def on_device(x, g, gate_weight, up_weight, down_weight):
    rows, wide = gate_weight.shape
    half, both_rows, tokens = wide // 2, 2 * rows, x.shape[0]
    count = lax.axis_size("tensor")
    assert count > BITS[0] and count & (count - 1) == 0
    width = wide // count
    four = lax.axis_size("section") == 4
    piece, narrow = ((both_rows, half), BF), ((rows, half), BF)
    small, small_bf = ((both_rows, tokens), F32), ((both_rows, tokens), BF)
    step = Steps()

    def with_width(body):
        def run(*refs):
            body(width, *refs)

        return run

    def one_hop(value):
        return exchanged(value, "section", 2) if four else ring_passed(value, 1)

    def relay(here, value):
        if not four:
            return ring_passed(here, 1)
        return exchanged(step(picked, piece, [here, value]), "section", 1)

    def outward(value):
        return exchanged(value, "section", 1) if four else ring_passed(value, -1)

    def backward(value):
        return exchanged(value, "section", 2) if four else ring_passed(value, -1)

    own, first, second = [None] * 3, [None] * 3, [None] * 3
    held = pltpu.VMEM((rows, wide), BF)
    own[1], own[0], down_keep, down_send = step(
        with_width(packed),
        [piece, piece, narrow, narrow],
        [gate_weight, up_weight, down_weight],
        far=3,
        scratch=[held, held, held, pltpu.SemaphoreType.DMA((3,))],
    )
    first[1] = one_hop(own[1])
    down_got = exchanged(down_send, "tensor", SWAP)

    def joined(keep, got, out):
        stacked(out, keep, got)

    own[2] = step(joined, piece, [down_keep, down_got])
    if four:
        crossed = exchanged(own[2], "section", 1)
        onward = lax.ppermute(crossed, "section", [(source, source ^ 2) for source in (0, 2)])
    first[2] = one_hop(own[2])
    x, g, both_own, *hid_own = step(
        project_first,
        [(x.shape, BF), (g.shape, BF), small, small_bf, small_bf],
        [x, g, own[0], own[1]],
        far=2,
        scratch=[pltpu.SemaphoreType.DMA((2,))],
    )
    first[0] = one_hop(step.hold(own[0]))
    share = with_width(shares)
    share_own = step(share, small, [g, own[2]])
    second[1] = relay(first[1], own[1])
    second[0] = relay(first[0], own[0])
    both_first, *hid_first = step(project, [small, small_bf, small_bf], [x, first[0], first[1]], also=[second[1]])
    second[2] = step(picked, piece, [crossed, onward]) if four else ring_passed(first[2], 1)
    share_second = step(share, small, [g, second[2]])

    def two_other(down_a, down_b, out):
        other_columns(width, down_a, out, 0)
        other_columns(width, down_b, out, half // 2)

    two_theirs = exchanged(step(two_other, piece, [own[2], second[2]]), "tensor", SECOND)
    both_second, *hid_second = step(project, [small, small_bf, small_bf], [x, second[0], second[1]])

    def two_sent(share_a, hid_a, share_b, hid_b, out):
        out[:both_rows, :] = sent_share(share_a, hid_a)
        out[both_rows:, :] = sent_share(share_b, hid_b)

    sent = step(two_sent, ((2 * both_rows, tokens), F32), [share_own, hid_own[1], share_second, hid_second[1]])
    got_two = exchanged(sent, "tensor", SWAP)
    side_down = outward(step(sent_down, piece, [g, *hid_second]))

    def finish_two(both_a, part_a, hid_a, both_b, part_b, hid_b, got, pair_a, out_a, pair_b, out_b):
        finish(both_a, part_a, got.at[:both_rows, :], hid_a, pair_a, out_a)
        finish(both_b, part_b, got.at[both_rows:, :], hid_b, pair_b, out_b)

    pair_own, wide_own, pair_second, wide_second = step(
        finish_two, [small_bf] * 4, [both_own, share_own, hid_own[0], both_second, share_second, hid_second[0], got_two]
    )
    low_columns = half + 128
    low_shape, high_shape = (both_rows, low_columns), (both_rows, wide - low_columns)
    low, high = step(sent_pair, [(low_shape, BF), (high_shape, BF)], [x, pair_second])

    grads_f32 = [(low_shape, F32), (high_shape, F32), ((both_rows, half), F32)]
    own_low, own_high, own_down = step(own_grads, grads_f32, [x, g, *hid_own, pair_own])

    def one_sent(gr, down, hid, part, out):
        shares(width, gr, down, part)
        out[...] = sent_share(part, hid)

    share_first, sent = step(one_sent, [small, small], [g, first[2], hid_first[1]], also=[two_theirs])
    got_one = exchanged(sent, "tensor", SWAP)
    side_low = outward(step.hold(low))

    def finish_last(both, share, got, hid, wide_a, wide_b, down, pair, wide_out, out):
        finish(both, share, got, hid, pair, wide_out)
        other_columns(width, down, out, 0)
        for k, ref in enumerate((wide_a, wide_b, wide_out)):
            out[:, half // 2 + k * tokens : half // 2 + (k + 1) * tokens] = ref[...]

    pair_first, wide_first, sent = step(
        finish_last,
        [small_bf, small_bf, ((both_rows, half // 2 + 3 * tokens), BF)],
        [both_first, share_first, got_one, hid_first[0], wide_own, wide_second, first[2]],
    )
    last_theirs = exchanged(sent, "tensor", SECOND)
    def back_down(gr, a, b, side, out):
        odd = is_odd()
        for at in range(0, half, TILE):
            value = down_columns(gr, a, b, at, half) + kept(side[:, at : at + TILE], odd, four, True)
            out[:, at : at + TILE] = value.astype(BF)

    def back_pair(offset):
        def body(xr, pair, side, out):
            odd = is_odd()
            for cut in tiles(out.shape[1]):
                value = dot(pair[...], xr[:, shifted(cut, offset)], NN)
                out[:, cut] = (value + kept(side[:, cut], odd, four, True)).astype(BF)

        return body

    back_of_down = backward(step(back_down, piece, [g, *hid_first, side_down]))
    side_high = outward(step.hold(high))
    back_of_low = backward(step(back_pair(0), (low_shape, BF), [x, pair_first, side_low]))
    send, keep = step(
        with_width(output_sums),
        [((tokens, wide // 8), BF), ((tokens, wide // 8), F32)],
        [wide_own, wide_second, wide_first, own[2], second[2], first[2], two_theirs, last_theirs],
    )
    got = exchanged(send, "tensor", BITS[0])

    def next_half(keep, got, bit):
        cols = keep.shape[1] // 2

        def body(*refs):
            halved(bit, width, *refs)

        send, keep = step(body, [((tokens, cols), BF), ((tokens, cols), F32)], [keep, got])
        return keep, exchanged(send, "tensor", bit)

    high_columns = wide - low_columns
    cut_at = high_columns // 256 * 128
    high_shapes = [(both_rows, cut_at), (both_rows, high_columns - cut_at)]

    def back_last(xr, pair, side, out_a, out_b):
        odd = is_odd()
        for out, offset in ((out_a, 0), (out_b, cut_at)):
            for cut in tiles(out.shape[1]):
                value = dot(pair[...], xr[:, shifted(cut, low_columns + offset)], NN)
                value += kept(side[:, shifted(cut, offset)], odd, four, True)
                out[:, cut] = value.astype(BF)

    backs_of_high = [
        backward(value)
        for value in step(
            back_last, [(shape, BF) for shape in high_shapes], [x, pair_first, side_high], also=[back_of_down]
        )
    ]
    bit = 2 * BITS[0]
    while bit < count:
        keep, got = next_half(keep, got, bit)
        bit *= 2

    def finished(own_ref, back, side, odd, cut):
        value = own_ref[:, cut] + back[:, cut].astype(F32)
        return value + kept(side[:, cut], odd, four, False) if four else value

    def final_down(own_ref, back, side, out):
        odd = is_odd()
        for at in range(0, half, TILE):
            cut = slice(at, at + TILE)
            value = finished(own_ref, back, side, odd, cut)
            out[:, cut] = value[:rows]
            out[:, half + at : half + at + TILE] = value[rows:]

    def ready_sums(low_ref, low_back, low_side, high_ref, high_side, gate_low, up_low, high_sum):
        odd = is_odd()
        for cut in tiles(low_columns):
            value = finished(low_ref, low_back, low_side, odd, cut)
            gate_low[:, cut] = value[:rows]
            up_low[:, cut] = value[rows:]
        for cut in tiles(high_columns):
            value = high_ref[:, cut]
            high_sum[:, cut] = value + kept(high_side[:, cut], odd, four, False) if four else value

    def final_pair(gate_low, up_low, high_sum, back_a, back_b, keep, got, out_gate, out_up, out):
        for cut in tiles(low_columns):
            out_gate[:, cut] = gate_low[:, cut]
            out_up[:, cut] = up_low[:, cut]
        for back, inside, columns in ((back_a, 0, cut_at), (back_b, cut_at, high_columns - cut_at)):
            for cut in tiles(columns):
                value = high_sum[:, shifted(cut, inside)] + back[:, cut].astype(F32)
                out_gate[:, shifted(cut, low_columns + inside)] = value[:rows]
                out_up[:, shifted(cut, low_columns + inside)] = value[rows:]
        final_output(keep, got, out)

    whole = ((rows, wide), F32)
    grad_down = step(final_down, whole, [own_down, back_of_down, side_down])
    ready = step(
        ready_sums,
        [((rows, low_columns), F32)] * 2 + [((both_rows, high_columns), F32)],
        [own_low, back_of_low, side_low, own_high, side_high],
    )
    grad_gate, grad_up, output = step(
        final_pair, [whole, whole, ((tokens, width), BF)], [*ready, *backs_of_high, keep, got]
    )
    return (output, grad_gate, grad_up, grad_down)


def solution(mesh):
    placed = (
        P("section", None),
        P("section", None),
        P(("section", "tensor"), None),
        P(("section", "tensor"), None),
        P(("section", "tensor"), None),
    )
    return jax.shard_map(
        on_device,
        mesh=mesh,
        in_specs=placed,
        out_specs=(
            P("section", "tensor"),
            P(("section", "tensor"), None),
            P(("section", "tensor"), None),
            P(("section", "tensor"), None),
        ),
        check_vma=False,
    )
```

```python
import jax
import jax.numpy as jnp
from jax import lax
from jax.experimental import pallas as pl
from jax.experimental.pallas import tpu as pltpu
from jax.sharding import PartitionSpec as P

BF = jnp.bfloat16
F32 = jnp.float32
NN = (((1,), (0,)), ((), ()))
NT = (((1,), (1,)), ((), ()))
TN = (((0,), (0,)), ((), ()))
TILE = 512
SWAP = 1
SECOND = 2
BITS = (4,)


def dot(left, right, dims):
    return lax.dot_general(left, right, dims, preferred_element_type=F32)


class Steps:
    def __init__(self):
        self.mark = None

    def __call__(self, body, outs, ins, also=(), far=0, scratch=()):
        marks = [*also] if self.mark is None else [*also, self.mark]
        count = len(ins)
        ins = [pltpu.with_memory_space_constraint(v, pltpu.HBM) if k < far else v for k, v in enumerate(ins)]

        def kernel(*refs):
            last = count + len(marks) + len(shapes)
            body(*refs[:count], *refs[count + len(marks) : last - 1], *refs[last:])
            refs[last - 1][...] = jnp.zeros_like(refs[last - 1])

        single = isinstance(outs, tuple)
        shapes = ([outs] if single else list(outs)) + [((8, 128), F32)]
        *got, self.mark = pl.pallas_call(
            kernel,
            out_shape=[jax.ShapeDtypeStruct(*s) for s in shapes],
            in_specs=[pl.BlockSpec(memory_space=pltpu.HBM)] * far
            + [pl.BlockSpec(memory_space=pltpu.VMEM)] * (count + len(marks) - far),
            out_specs=[pl.BlockSpec(memory_space=pltpu.VMEM)] * len(shapes),
            scratch_shapes=list(scratch),
            compiler_params=pltpu.CompilerParams(vmem_limit_bytes=24 * 1024 * 1024),
            cost_estimate=pl.CostEstimate(flops=1, bytes_accessed=1, transcendentals=0),
        )(*ins, *marks)
        return got[0] if single else got

    def hold(self, value):
        value, self.mark = lax.optimization_barrier((value, self.mark))
        return value


def either(bit, run):
    for value in range(2):
        pl.when(bit == value)(lambda value=value: run(value))


def tensor_bit(bit):
    return lax.rem(lax.div(lax.axis_index("tensor"), bit), 2)


def both_bits(run):
    either(tensor_bit(SECOND), lambda here: either(tensor_bit(BITS[0]), lambda mine: run(here, mine)))


def is_odd():
    return lax.rem(lax.axis_index("section"), 2) == 1


def top_rows(like):
    return lax.broadcasted_iota(jnp.int32, like.shape, 0) < like.shape[0] // 2


def placed(rows):
    shape = (2 * rows, rows)
    place = lax.broadcasted_iota(jnp.int32, shape, 0) - lax.broadcasted_iota(jnp.int32, shape, 1)
    return [(place == shift).astype(F32).astype(BF) for shift in (0, rows)]


def stacked(out, upper, lower, upper_at=0, lower_at=0):
    top, bottom = placed(upper.shape[0])
    for at in range(0, out.shape[1], TILE):
        first, second = slice(upper_at + at, upper_at + at + TILE), slice(lower_at + at, lower_at + at + TILE)
        out[:, at : at + TILE] = (dot(top, upper[:, first], NN) + dot(bottom, lower[:, second], NN)).astype(BF)


def runs(width, wide):
    return [(SWAP * width * j, 2 * SWAP * width * j) for j in range(wide // (2 * SWAP * width))]


def packed(width, gate, up, down, high, keep, send, gate_here, up_here, down_here, sems):
    copies = [
        pltpu.make_async_copy(there, here, sems.at[k])
        for k, (there, here) in enumerate(((gate, gate_here), (up, up_here), (down, down_here)))
    ]
    for copy in copies:
        copy.start()
    half = high.shape[1]
    copies[0].wait()
    copies[1].wait()
    stacked(high, gate_here, up_here, half, half)
    copies[2].wait()

    def run(mine):
        for near, there in runs(width, 2 * half):
            here = slice(near, near + SWAP * width)
            for out, which in ((keep, mine), (send, 1 - mine)):
                at = there + SWAP * width * which
                out[:, here] = down_here[:, at : at + SWAP * width]

    either(tensor_bit(SWAP), run)


def project_tiles(x, low, high):
    half = low.shape[1]
    tile = min(half, 1024)
    total = jnp.zeros((low.shape[0], x.shape[0]), F32)
    for at in range(0, half, tile):
        cut = slice(at, at + tile)
        total += dot(low[:, cut], x[:, cut], NT)
        total += dot(high[:, cut], x[:, half + at : half + at + tile], NT)
    return total


def project(x, low, high, both, hid_a, hid_b):
    rows = low.shape[0] // 2
    total = project_tiles(x, low, high)
    both[...] = total
    hidden = total * jax.nn.sigmoid(total) * pltpu.roll(total, rows, 0)
    hidden = jnp.where(top_rows(total), hidden, 0.0)
    hid_a[...] = hidden.astype(BF)
    hid_b[...] = pltpu.roll(hidden, rows, 0).astype(BF)


def project_first(x_there, g_there, low, high, x, g, both, hid_a, hid_b, sems):
    copies = [pltpu.make_async_copy(x_there, x, sems.at[0]), pltpu.make_async_copy(g_there, g, sems.at[1])]
    for copy in copies:
        copy.start()
    copies[0].wait()
    project(x, low, high, both, hid_a, hid_b)
    copies[1].wait()


def shares(width, g, down, part):
    wide = g.shape[1]
    tile = min(SWAP * width, 1024)

    def run(mine):
        total = jnp.zeros(part.shape, F32)
        for near, there in runs(width, wide):
            for at in range(0, SWAP * width, tile):
                far = there + SWAP * width * mine + at
                total += dot(down[:, near + at : near + at + tile], g[:, far : far + tile], NT)
        part[...] = total

    either(tensor_bit(SWAP), run)


def sent_share(part, hid_b):
    share = part[...]
    return jnp.where(top_rows(share), pltpu.roll(share, share.shape[0] // 2, 0), hid_b[...].astype(F32))


def finish(both, part, got, hid_a, pair, hid_pair):
    rows = both.shape[0] // 2
    gate, got = both[...], got[...]
    dhid = part[...] + got
    sig = jax.nn.sigmoid(gate)
    dgate = dhid * pltpu.roll(gate, rows, 0) * sig * (1.0 + gate * (1.0 - sig))
    dup = pltpu.roll(dhid * (gate * sig), rows, 0)
    first = top_rows(gate)
    pair[...] = jnp.where(first, dgate, dup).astype(BF)
    hid_pair[...] = jnp.where(first, hid_a[...].astype(F32), got).astype(BF)


def down_columns(g, hid_a, hid_b, at, half):
    cut = slice(at, at + TILE)
    return dot(hid_a[...], g[:, cut], NN) + dot(hid_b[...], g[:, half + at : half + at + TILE], NN)


def tiles(size):
    return [slice(at, min(at + TILE, size)) for at in range(0, size, TILE)]


def shifted(cut, offset):
    return slice(cut.start + offset, cut.stop + offset)


def own_grads(x, g, hid_a, hid_b, pair, low, high, down):
    half = down.shape[1]
    for out, offset in ((low, 0), (high, low.shape[1])):
        for cut in tiles(out.shape[1]):
            out[:, cut] = dot(pair[...], x[:, shifted(cut, offset)], NN)
    for at in range(0, half, TILE):
        down[:, at : at + TILE] = down_columns(g, hid_a, hid_b, at, half)


def sent_down(g, hid_a, hid_b, out):
    half = out.shape[1]
    for at in range(0, half, TILE):
        out[:, at : at + TILE] = down_columns(g, hid_a, hid_b, at, half).astype(BF)


def sent_pair(x, pair, low, high):
    for out, offset in ((low, 0), (high, low.shape[1])):
        for cut in tiles(out.shape[1]):
            out[:, cut] = dot(pair[...], x[:, shifted(cut, offset)], NN).astype(BF)


def kept(side, odd, four, wanted):
    value = side.astype(F32)
    return jnp.where(odd == wanted, value, 0.0) if four else value


def picked(here, piece, out):
    @pl.when(is_odd())
    def _():
        out[...] = here[...]

    @pl.when(jnp.logical_not(is_odd()))
    def _():
        out[...] = piece[...]


def other_columns(width, down, out, at):
    def run(mine):
        for k in range(down.shape[1] // (2 * width)):
            column = (2 * k + 1 - mine) * width
            out[:, at + k * width : at + (k + 1) * width] = down[:, column : column + width]

    either(tensor_bit(SECOND), run)


def near_sums(width, *refs):
    hids, downs, outs = refs[:3], refs[3:6], refs[6:]
    tile = min(width, TILE)

    def run(here, mine):
        for block in range(2 * outs[0].shape[1] // width):
            for at in range(0, width, tile):
                near, column = (2 * block + here) * width + at, block // 2 * width + at
                total = sum(dot(hid[...], down[:, near : near + tile], TN) for hid, down in zip(hids, downs))
                outs[int(block % 2 == mine)][:, column : column + tile] = total

    both_bits(run)


def output_sums(width, send_sum, keep_sum, two, last, send, keep):
    tokens, quarter = send.shape[0], two.shape[1] // 2
    tile = min(width, TILE)
    gots = ((two, 0), (two, quarter), (last, 0))

    def run(mine):
        for block in range(2 * keep.shape[1] // width):
            for at in range(0, width, tile):
                far, column = block * width + at, block // 2 * width + at
                out, sums = (keep, keep_sum) if block % 2 == mine else (send, send_sum)
                total = sums[:, column : column + tile]
                for k, (got, offset) in enumerate(gots):
                    other = last[:, quarter + k * tokens : quarter + (k + 1) * tokens]
                    total += dot(other, got[:, offset + far : offset + far + tile], TN)
                out[:, column : column + tile] = total.astype(out.dtype)

    either(tensor_bit(BITS[0]), run)


def halved(bit, width, keep, got, send, left):
    tile = min(width, TILE)

    def run(mine):
        for block in range(left.shape[1] // width):
            for out, which in ((send, 1 - mine), (left, mine)):
                for at in range(0, width, tile):
                    cols = slice((2 * block + which) * width + at, (2 * block + which) * width + at + tile)
                    value = keep[:, cols] + got[:, cols].astype(F32)
                    out[:, block * width + at : block * width + at + tile] = value.astype(out.dtype)

    either(tensor_bit(bit), run)


def final_output(keep, got, out):
    out[...] = (keep[...] + got[...].astype(F32)).astype(BF)


def exchanged(value, axis, bit):
    count = lax.axis_size(axis)
    return lax.ppermute(value, axis, [(source, source ^ bit) for source in range(count)])


def ring_passed(value, steps):
    count = lax.axis_size("section")
    return lax.ppermute(value, "section", [(source, (source + steps) % count) for source in range(count)])


def on_device(x, g, gate_weight, up_weight, down_weight):
    rows, wide = gate_weight.shape
    half, both_rows, tokens = wide // 2, 2 * rows, x.shape[0]
    count = lax.axis_size("tensor")
    assert count > BITS[0] and count & (count - 1) == 0
    width = wide // count
    four = lax.axis_size("section") == 4
    piece, narrow = ((both_rows, half), BF), ((rows, half), BF)
    small, small_bf = ((both_rows, tokens), F32), ((both_rows, tokens), BF)
    step = Steps()

    def with_width(body):
        def run(*refs):
            body(width, *refs)

        return run

    def one_hop(value):
        return exchanged(value, "section", 2) if four else ring_passed(value, 1)

    def relay(here, value):
        if not four:
            return ring_passed(here, 1)
        return exchanged(step(picked, piece, [here, value]), "section", 1)

    def outward(value):
        return exchanged(value, "section", 1) if four else ring_passed(value, -1)

    def backward(value):
        return exchanged(value, "section", 2) if four else ring_passed(value, -1)

    own, first, second = [None] * 3, [None] * 3, [None] * 3
    own[1], down_keep, down_send, gate_here, up_here = step(
        with_width(packed),
        [piece, narrow, narrow, ((rows, wide), BF), ((rows, wide), BF)],
        [gate_weight, up_weight, down_weight],
        far=3,
        scratch=[pltpu.VMEM((rows, wide), BF), pltpu.SemaphoreType.DMA((3,))],
    )
    first[1] = one_hop(own[1])
    down_got = exchanged(down_send, "tensor", SWAP)

    def joined(keep, got, out):
        stacked(out, keep, got)

    own[2] = step(joined, piece, [down_keep, down_got])
    if four:
        crossed = exchanged(own[2], "section", 1)
        onward = lax.ppermute(crossed, "section", [(source, source ^ 2) for source in (0, 2)])
    first[2] = one_hop(own[2])
    own[0] = step(joined, piece, [gate_here, up_here])
    x, g, both_own, *hid_own = step(
        project_first,
        [(x.shape, BF), (g.shape, BF), small, small_bf, small_bf],
        [x, g, own[0], own[1]],
        far=2,
        scratch=[pltpu.SemaphoreType.DMA((2,))],
    )
    first[0] = one_hop(step.hold(own[0]))
    share = with_width(shares)
    share_own = step(share, small, [g, own[2]])
    second[1] = relay(first[1], own[1])
    second[0] = relay(first[0], own[0])
    both_first, *hid_first = step(project, [small, small_bf, small_bf], [x, first[0], first[1]], also=[second[1]])
    second[2] = step(picked, piece, [crossed, onward]) if four else ring_passed(first[2], 1)
    share_second = step(share, small, [g, second[2]])

    def two_other(down_a, down_b, out):
        other_columns(width, down_a, out, 0)
        other_columns(width, down_b, out, half // 2)

    two_theirs = exchanged(step(two_other, piece, [own[2], second[2]]), "tensor", SECOND)
    both_second, *hid_second = step(project, [small, small_bf, small_bf], [x, second[0], second[1]])

    def two_sent(share_a, hid_a, share_b, hid_b, out):
        out[:both_rows, :] = sent_share(share_a, hid_a)
        out[both_rows:, :] = sent_share(share_b, hid_b)

    sent = step(two_sent, ((2 * both_rows, tokens), F32), [share_own, hid_own[1], share_second, hid_second[1]])
    got_two = exchanged(sent, "tensor", SWAP)
    side_down = outward(step(sent_down, piece, [g, *hid_second]))

    def finish_two(both_a, part_a, hid_a, both_b, part_b, hid_b, got, pair_a, out_a, pair_b, out_b):
        finish(both_a, part_a, got.at[:both_rows, :], hid_a, pair_a, out_a)
        finish(both_b, part_b, got.at[both_rows:, :], hid_b, pair_b, out_b)

    pair_own, wide_own, pair_second, wide_second = step(
        finish_two, [small_bf] * 4, [both_own, share_own, hid_own[0], both_second, share_second, hid_second[0], got_two]
    )
    low_columns = half + 128
    low_shape, high_shape = (both_rows, low_columns), (both_rows, wide - low_columns)
    low, high = step(sent_pair, [(low_shape, BF), (high_shape, BF)], [x, pair_second])

    grads_f32 = [(low_shape, F32), (high_shape, F32), ((both_rows, half), F32)]
    own_low, own_high, own_down = step(own_grads, grads_f32, [x, g, *hid_own, pair_own])

    def one_sent(gr, down, hid, part, out):
        shares(width, gr, down, part)
        out[...] = sent_share(part, hid)

    share_first, sent = step(one_sent, [small, small], [g, first[2], hid_first[1]], also=[two_theirs])
    got_one = exchanged(sent, "tensor", SWAP)
    side_low = outward(step.hold(low))

    def finish_last(both, share, got, hid, wide_a, wide_b, down, pair, wide_out, out):
        finish(both, share, got, hid, pair, wide_out)
        other_columns(width, down, out, 0)
        for k, ref in enumerate((wide_a, wide_b, wide_out)):
            out[:, half // 2 + k * tokens : half // 2 + (k + 1) * tokens] = ref[...]

    pair_first, wide_first, sent = step(
        finish_last,
        [small_bf, small_bf, ((both_rows, half // 2 + 3 * tokens), BF)],
        [both_first, share_first, got_one, hid_first[0], wide_own, wide_second, first[2]],
    )
    last_theirs = exchanged(sent, "tensor", SECOND)
    near = step(
        with_width(near_sums),
        [((tokens, wide // 8), F32)] * 2,
        [wide_own, wide_second, wide_first, own[2], second[2], first[2]],
    )
    def back_down(gr, a, b, side, out):
        odd = is_odd()
        for at in range(0, half, TILE):
            value = down_columns(gr, a, b, at, half) + kept(side[:, at : at + TILE], odd, four, True)
            out[:, at : at + TILE] = value.astype(BF)

    def back_pair(offset):
        def body(xr, pair, side, out):
            odd = is_odd()
            for cut in tiles(out.shape[1]):
                value = dot(pair[...], xr[:, shifted(cut, offset)], NN)
                out[:, cut] = (value + kept(side[:, cut], odd, four, True)).astype(BF)

        return body

    back_of_down = backward(step(back_down, piece, [g, *hid_first, side_down]))
    side_high = outward(step.hold(high))
    back_of_low = backward(step(back_pair(0), (low_shape, BF), [x, pair_first, side_low]))
    send, keep = step(
        with_width(output_sums),
        [((tokens, wide // 8), BF), ((tokens, wide // 8), F32)],
        [*near, two_theirs, last_theirs],
    )
    got = exchanged(send, "tensor", BITS[0])

    def next_half(keep, got, bit):
        cols = keep.shape[1] // 2

        def body(*refs):
            halved(bit, width, *refs)

        send, keep = step(body, [((tokens, cols), BF), ((tokens, cols), F32)], [keep, got])
        return keep, exchanged(send, "tensor", bit)

    high_columns = wide - low_columns
    cut_at = high_columns // 256 * 128
    high_shapes = [(both_rows, cut_at), (both_rows, high_columns - cut_at)]

    def back_last(xr, pair, side, out_a, out_b):
        odd = is_odd()
        for out, offset in ((out_a, 0), (out_b, cut_at)):
            for cut in tiles(out.shape[1]):
                value = dot(pair[...], xr[:, shifted(cut, low_columns + offset)], NN)
                value += kept(side[:, shifted(cut, offset)], odd, four, True)
                out[:, cut] = value.astype(BF)

    backs_of_high = [
        backward(value)
        for value in step(
            back_last, [(shape, BF) for shape in high_shapes], [x, pair_first, side_high], also=[back_of_down]
        )
    ]
    bit = 2 * BITS[0]
    while bit < count:
        keep, got = next_half(keep, got, bit)
        bit *= 2

    def finished(own_ref, back, side, odd, cut):
        value = own_ref[:, cut] + back[:, cut].astype(F32)
        return value + kept(side[:, cut], odd, four, False) if four else value

    def final_down(own_ref, back, side, out):
        odd = is_odd()
        for at in range(0, half, TILE):
            cut = slice(at, at + TILE)
            value = finished(own_ref, back, side, odd, cut)
            out[:, cut] = value[:rows]
            out[:, half + at : half + at + TILE] = value[rows:]

    def ready_sums(low_ref, low_back, low_side, high_ref, high_side, gate_low, up_low, high_sum):
        odd = is_odd()
        for cut in tiles(low_columns):
            value = finished(low_ref, low_back, low_side, odd, cut)
            gate_low[:, cut] = value[:rows]
            up_low[:, cut] = value[rows:]
        for cut in tiles(high_columns):
            value = high_ref[:, cut]
            high_sum[:, cut] = value + kept(high_side[:, cut], odd, four, False) if four else value

    def final_pair(gate_low, up_low, high_sum, back_a, back_b, keep, got, out_gate, out_up, out):
        for cut in tiles(low_columns):
            out_gate[:, cut] = gate_low[:, cut]
            out_up[:, cut] = up_low[:, cut]
        for back, inside, columns in ((back_a, 0, cut_at), (back_b, cut_at, high_columns - cut_at)):
            for cut in tiles(columns):
                value = high_sum[:, shifted(cut, inside)] + back[:, cut].astype(F32)
                out_gate[:, shifted(cut, low_columns + inside)] = value[:rows]
                out_up[:, shifted(cut, low_columns + inside)] = value[rows:]
        final_output(keep, got, out)

    whole = ((rows, wide), F32)
    grad_down = step(final_down, whole, [own_down, back_of_down, side_down])
    ready = step(
        ready_sums,
        [((rows, low_columns), F32)] * 2 + [((both_rows, high_columns), F32)],
        [own_low, back_of_low, side_low, own_high, side_high],
    )
    grad_gate, grad_up, output = step(
        final_pair, [whole, whole, ((tokens, width), BF)], [*ready, *backs_of_high, keep, got]
    )
    return (output, grad_gate, grad_up, grad_down)


def solution(mesh):
    placed = (
        P("section", None),
        P("section", None),
        P(("section", "tensor"), None),
        P(("section", "tensor"), None),
        P(("section", "tensor"), None),
    )
    return jax.shard_map(
        on_device,
        mesh=mesh,
        in_specs=placed,
        out_specs=(
            P("section", "tensor"),
            P(("section", "tensor"), None),
            P(("section", "tensor"), None),
            P(("section", "tensor"), None),
        ),
        check_vma=False,
    )
```

```python
import jax
import jax.numpy as jnp
from jax import lax
from jax.experimental import pallas as pl
from jax.experimental.pallas import tpu as pltpu
from jax.sharding import PartitionSpec as P

BF = jnp.bfloat16
F32 = jnp.float32
NN = (((1,), (0,)), ((), ()))
NT = (((1,), (1,)), ((), ()))
TN = (((0,), (0,)), ((), ()))
TILE = 512
SWAP = 1
SECOND = 2
BITS = (4,)


def dot(left, right, dims):
    return lax.dot_general(left, right, dims, preferred_element_type=F32)


class Steps:
    def __init__(self):
        self.mark = None

    def __call__(self, body, outs, ins, also=(), far=0, scratch=()):
        marks = [*also] if self.mark is None else [*also, self.mark]
        count = len(ins)
        ins = [pltpu.with_memory_space_constraint(v, pltpu.HBM) if k < far else v for k, v in enumerate(ins)]

        def kernel(*refs):
            last = count + len(marks) + len(shapes)
            body(*refs[:count], *refs[count + len(marks) : last - 1], *refs[last:])
            refs[last - 1][...] = jnp.zeros_like(refs[last - 1])

        single = isinstance(outs, tuple)
        shapes = ([outs] if single else list(outs)) + [((8, 128), F32)]
        *got, self.mark = pl.pallas_call(
            kernel,
            out_shape=[jax.ShapeDtypeStruct(*s) for s in shapes],
            in_specs=[pl.BlockSpec(memory_space=pltpu.HBM)] * far
            + [pl.BlockSpec(memory_space=pltpu.VMEM)] * (count + len(marks) - far),
            out_specs=[pl.BlockSpec(memory_space=pltpu.VMEM)] * len(shapes),
            scratch_shapes=list(scratch),
            compiler_params=pltpu.CompilerParams(vmem_limit_bytes=24 * 1024 * 1024),
            cost_estimate=pl.CostEstimate(flops=1, bytes_accessed=1, transcendentals=0),
        )(*ins, *marks)
        return got[0] if single else got

    def hold(self, value):
        value, self.mark = lax.optimization_barrier((value, self.mark))
        return value


def either(bit, run):
    for value in range(2):
        pl.when(bit == value)(lambda value=value: run(value))


def tensor_bit(bit):
    return lax.rem(lax.div(lax.axis_index("tensor"), bit), 2)


def both_bits(run):
    either(tensor_bit(SECOND), lambda here: either(tensor_bit(BITS[0]), lambda mine: run(here, mine)))


def is_odd():
    return lax.rem(lax.axis_index("section"), 2) == 1


def top_rows(like):
    return lax.broadcasted_iota(jnp.int32, like.shape, 0) < like.shape[0] // 2


def placed(rows):
    shape = (2 * rows, rows)
    place = lax.broadcasted_iota(jnp.int32, shape, 0) - lax.broadcasted_iota(jnp.int32, shape, 1)
    return [(place == shift).astype(F32).astype(BF) for shift in (0, rows)]


def stacked(out, upper, lower, upper_at=0, lower_at=0):
    top, bottom = placed(upper.shape[0])
    for at in range(0, out.shape[1], TILE):
        first, second = slice(upper_at + at, upper_at + at + TILE), slice(lower_at + at, lower_at + at + TILE)
        out[:, at : at + TILE] = (dot(top, upper[:, first], NN) + dot(bottom, lower[:, second], NN)).astype(BF)


def runs(width, wide):
    return [(SWAP * width * j, 2 * SWAP * width * j) for j in range(wide // (2 * SWAP * width))]


def packed(width, gate, up, down, high, keep, send, gate_here, up_here, down_here, sems):
    copies = [
        pltpu.make_async_copy(there, here, sems.at[k])
        for k, (there, here) in enumerate(((gate, gate_here), (up, up_here), (down, down_here)))
    ]
    for copy in copies:
        copy.start()
    half = high.shape[1]
    copies[0].wait()
    copies[1].wait()
    stacked(high, gate_here, up_here, half, half)
    copies[2].wait()

    def run(mine):
        for near, there in runs(width, 2 * half):
            here = slice(near, near + SWAP * width)
            for out, which in ((keep, mine), (send, 1 - mine)):
                at = there + SWAP * width * which
                out[:, here] = down_here[:, at : at + SWAP * width]

    either(tensor_bit(SWAP), run)


def project_tiles(x, low, high):
    half = low.shape[1]
    tile = min(half, 1024)
    total = jnp.zeros((low.shape[0], x.shape[0]), F32)
    for at in range(0, half, tile):
        cut = slice(at, at + tile)
        total += dot(low[:, cut], x[:, cut], NT)
        total += dot(high[:, cut], x[:, half + at : half + at + tile], NT)
    return total


def project(x, low, high, both, hid_a, hid_b):
    rows = low.shape[0] // 2
    total = project_tiles(x, low, high)
    both[...] = total
    hidden = total * jax.nn.sigmoid(total) * pltpu.roll(total, rows, 0)
    hidden = jnp.where(top_rows(total), hidden, 0.0)
    hid_a[...] = hidden.astype(BF)
    hid_b[...] = pltpu.roll(hidden, rows, 0).astype(BF)


def project_first(x_there, g_there, low, high, x, g, both, hid_a, hid_b, sems):
    copies = [pltpu.make_async_copy(x_there, x, sems.at[0]), pltpu.make_async_copy(g_there, g, sems.at[1])]
    for copy in copies:
        copy.start()
    copies[0].wait()
    project(x, low, high, both, hid_a, hid_b)
    copies[1].wait()


def shares(width, g, down, part):
    wide = g.shape[1]
    tile = min(SWAP * width, 1024)

    def run(mine):
        total = jnp.zeros(part.shape, F32)
        for near, there in runs(width, wide):
            for at in range(0, SWAP * width, tile):
                far = there + SWAP * width * mine + at
                total += dot(down[:, near + at : near + at + tile], g[:, far : far + tile], NT)
        part[...] = total

    either(tensor_bit(SWAP), run)


def sent_share(part, hid_b):
    share = part[...]
    return jnp.where(top_rows(share), pltpu.roll(share, share.shape[0] // 2, 0), hid_b[...].astype(F32))


def finish(both, part, got, hid_a, pair, hid_pair):
    rows = both.shape[0] // 2
    gate, got = both[...], got[...]
    dhid = part[...] + got
    sig = jax.nn.sigmoid(gate)
    dgate = dhid * pltpu.roll(gate, rows, 0) * sig * (1.0 + gate * (1.0 - sig))
    dup = pltpu.roll(dhid * (gate * sig), rows, 0)
    first = top_rows(gate)
    pair[...] = jnp.where(first, dgate, dup).astype(BF)
    hid_pair[...] = jnp.where(first, hid_a[...].astype(F32), got).astype(BF)


def down_columns(g, hid_a, hid_b, at, half):
    cut = slice(at, at + TILE)
    return dot(hid_a[...], g[:, cut], NN) + dot(hid_b[...], g[:, half + at : half + at + TILE], NN)


def tiles(size):
    return [slice(at, min(at + TILE, size)) for at in range(0, size, TILE)]


def shifted(cut, offset):
    return slice(cut.start + offset, cut.stop + offset)


def own_grads(x, g, hid_a, hid_b, pair, low, high, down):
    half = down.shape[1]
    for out, offset in ((low, 0), (high, low.shape[1])):
        for cut in tiles(out.shape[1]):
            out[:, cut] = dot(pair[...], x[:, shifted(cut, offset)], NN)
    for at in range(0, half, TILE):
        down[:, at : at + TILE] = down_columns(g, hid_a, hid_b, at, half)


def sent_down(g, hid_a, hid_b, out):
    half = out.shape[1]
    for at in range(0, half, TILE):
        out[:, at : at + TILE] = down_columns(g, hid_a, hid_b, at, half).astype(BF)


def sent_pair(x, pair, low, high):
    for out, offset in ((low, 0), (high, low.shape[1])):
        for cut in tiles(out.shape[1]):
            out[:, cut] = dot(pair[...], x[:, shifted(cut, offset)], NN).astype(BF)


def kept(side, odd, four, wanted):
    value = side.astype(F32)
    return jnp.where(odd == wanted, value, 0.0) if four else value


def picked(here, piece, out):
    @pl.when(is_odd())
    def _():
        out[...] = here[...]

    @pl.when(jnp.logical_not(is_odd()))
    def _():
        out[...] = piece[...]


def other_columns(width, down, out, at):
    def run(mine):
        for k in range(down.shape[1] // (2 * width)):
            column = (2 * k + 1 - mine) * width
            out[:, at + k * width : at + (k + 1) * width] = down[:, column : column + width]

    either(tensor_bit(SECOND), run)


def near_sums(width, *refs):
    hids, downs, outs = refs[:3], refs[3:6], refs[6:]
    tile = min(width, TILE)

    def run(here, mine):
        for block in range(2 * outs[0].shape[1] // width):
            for at in range(0, width, tile):
                near, column = (2 * block + here) * width + at, block // 2 * width + at
                total = sum(dot(hid[...], down[:, near : near + tile], TN) for hid, down in zip(hids, downs))
                outs[int(block % 2 == mine)][:, column : column + tile] = total

    both_bits(run)


def output_sums(width, send_sum, keep_sum, two, last, send, keep):
    tokens, quarter = send.shape[0], two.shape[1] // 2
    tile = min(width, TILE)
    gots = ((two, 0), (two, quarter), (last, 0))

    def run(mine):
        for block in range(2 * keep.shape[1] // width):
            for at in range(0, width, tile):
                far, column = block * width + at, block // 2 * width + at
                out, sums = (keep, keep_sum) if block % 2 == mine else (send, send_sum)
                total = sums[:, column : column + tile]
                for k, (got, offset) in enumerate(gots):
                    other = last[:, quarter + k * tokens : quarter + (k + 1) * tokens]
                    total += dot(other, got[:, offset + far : offset + far + tile], TN)
                out[:, column : column + tile] = total.astype(out.dtype)

    either(tensor_bit(BITS[0]), run)


def halved(bit, width, keep, got, send, left):
    tile = min(width, TILE)

    def run(mine):
        for block in range(left.shape[1] // width):
            for out, which in ((send, 1 - mine), (left, mine)):
                for at in range(0, width, tile):
                    cols = slice((2 * block + which) * width + at, (2 * block + which) * width + at + tile)
                    value = keep[:, cols] + got[:, cols].astype(F32)
                    out[:, block * width + at : block * width + at + tile] = value.astype(out.dtype)

    either(tensor_bit(bit), run)


def final_output(keep, got, out):
    out[...] = (keep[...] + got[...].astype(F32)).astype(BF)


def exchanged(value, axis, bit):
    count = lax.axis_size(axis)
    return lax.ppermute(value, axis, [(source, source ^ bit) for source in range(count)])


def ring_passed(value, steps):
    count = lax.axis_size("section")
    return lax.ppermute(value, "section", [(source, (source + steps) % count) for source in range(count)])


def on_device(x, g, gate_weight, up_weight, down_weight):
    rows, wide = gate_weight.shape
    half, both_rows, tokens = wide // 2, 2 * rows, x.shape[0]
    count = lax.axis_size("tensor")
    assert count > BITS[0] and count & (count - 1) == 0
    width = wide // count
    four = lax.axis_size("section") == 4
    piece, narrow = ((both_rows, half), BF), ((rows, half), BF)
    small, small_bf = ((both_rows, tokens), F32), ((both_rows, tokens), BF)
    step = Steps()

    def with_width(body):
        def run(*refs):
            body(width, *refs)

        return run

    def one_hop(value):
        return exchanged(value, "section", 2) if four else ring_passed(value, 1)

    def relay(here, value):
        if not four:
            return ring_passed(here, 1)
        return exchanged(step(picked, piece, [here, value]), "section", 1)

    def outward(value):
        return exchanged(value, "section", 1) if four else ring_passed(value, -1)

    def backward(value):
        return exchanged(value, "section", 2) if four else ring_passed(value, -1)

    own, first, second = [None] * 3, [None] * 3, [None] * 3
    own[1], down_keep, down_send, gate_here, up_here = step(
        with_width(packed),
        [piece, narrow, narrow, ((rows, wide), BF), ((rows, wide), BF)],
        [gate_weight, up_weight, down_weight],
        far=3,
        scratch=[pltpu.VMEM((rows, wide), BF), pltpu.SemaphoreType.DMA((3,))],
    )
    first[1] = one_hop(own[1])
    down_got = exchanged(down_send, "tensor", SWAP)

    def joined(keep, got, out):
        stacked(out, keep, got)

    own[2] = step(joined, piece, [down_keep, down_got])
    if four:
        crossed = exchanged(own[2], "section", 1)
        onward = lax.ppermute(crossed, "section", [(source, source ^ 2) for source in (0, 2)])
    first[2] = one_hop(own[2])
    own[0] = step(joined, piece, [gate_here, up_here])
    x, g, both_own, *hid_own = step(
        project_first,
        [(x.shape, BF), (g.shape, BF), small, small_bf, small_bf],
        [x, g, own[0], own[1]],
        far=2,
        scratch=[pltpu.SemaphoreType.DMA((2,))],
    )
    first[0] = one_hop(step.hold(own[0]))
    share = with_width(shares)
    share_own = step(share, small, [g, own[2]])
    second[1] = relay(first[1], own[1])
    second[0] = relay(first[0], own[0])
    both_first, *hid_first = step(project, [small, small_bf, small_bf], [x, first[0], first[1]], also=[second[1]])
    second[2] = step(picked, piece, [crossed, onward]) if four else ring_passed(first[2], 1)
    share_second = step(share, small, [g, second[2]])

    def two_other(down_a, down_b, out):
        other_columns(width, down_a, out, 0)
        other_columns(width, down_b, out, half // 2)

    two_theirs = exchanged(step(two_other, piece, [own[2], second[2]]), "tensor", SECOND)
    both_second, *hid_second = step(project, [small, small_bf, small_bf], [x, second[0], second[1]])

    def two_sent(share_a, hid_a, share_b, hid_b, out):
        out[:both_rows, :] = sent_share(share_a, hid_a)
        out[both_rows:, :] = sent_share(share_b, hid_b)

    sent = step(two_sent, ((2 * both_rows, tokens), F32), [share_own, hid_own[1], share_second, hid_second[1]])
    got_two = exchanged(sent, "tensor", SWAP)
    side_down = outward(step(sent_down, piece, [g, *hid_second]))

    def finish_two(both_a, part_a, hid_a, both_b, part_b, hid_b, got, pair_a, out_a, pair_b, out_b):
        finish(both_a, part_a, got.at[:both_rows, :], hid_a, pair_a, out_a)
        finish(both_b, part_b, got.at[both_rows:, :], hid_b, pair_b, out_b)

    pair_own, wide_own, pair_second, wide_second = step(
        finish_two, [small_bf] * 4, [both_own, share_own, hid_own[0], both_second, share_second, hid_second[0], got_two]
    )
    low_columns = half + 128
    low_shape, high_shape = (both_rows, low_columns), (both_rows, wide - low_columns)
    low, high = step(sent_pair, [(low_shape, BF), (high_shape, BF)], [x, pair_second])

    grads_f32 = [(low_shape, F32), (high_shape, F32), ((both_rows, half), F32)]
    own_low, own_high, own_down = step(own_grads, grads_f32, [x, g, *hid_own, pair_own])

    def one_sent(gr, down, hid, part, out):
        shares(width, gr, down, part)
        out[...] = sent_share(part, hid)

    share_first, sent = step(one_sent, [small, small], [g, first[2], hid_first[1]], also=[two_theirs])
    got_one = exchanged(sent, "tensor", SWAP)
    side_low = outward(step.hold(low))

    def finish_last(both, share, got, hid, wide_a, wide_b, down, pair, wide_out, out):
        finish(both, share, got, hid, pair, wide_out)
        other_columns(width, down, out, 0)
        for k, ref in enumerate((wide_a, wide_b, wide_out)):
            out[:, half // 2 + k * tokens : half // 2 + (k + 1) * tokens] = ref[...]

    pair_first, wide_first, sent = step(
        finish_last,
        [small_bf, small_bf, ((both_rows, half // 2 + 3 * tokens), BF)],
        [both_first, share_first, got_one, hid_first[0], wide_own, wide_second, first[2]],
    )
    last_theirs = exchanged(sent, "tensor", SECOND)
    near = step(
        with_width(near_sums),
        [((tokens, wide // 8), F32)] * 2,
        [wide_own, wide_second, wide_first, own[2], second[2], first[2]],
    )
    first_low, first_high, first_down = step(own_grads, grads_f32, [x, g, *hid_first, pair_first])

    def added(own_ref, side, *outs):
        odd, at = is_odd(), 0
        for out in outs:
            for cut in tiles(out.shape[1]):
                from_ = shifted(cut, at)
                out[:, cut] = (own_ref[:, from_] + kept(side[:, from_], odd, four, True)).astype(BF)
            at += out.shape[1]

    back_of_down = backward(step(added, piece, [first_down, side_down]))
    side_high = outward(step.hold(high))
    back_of_low = backward(step(added, (low_shape, BF), [first_low, side_low]))
    send, keep = step(
        with_width(output_sums),
        [((tokens, wide // 8), BF), ((tokens, wide // 8), F32)],
        [*near, two_theirs, last_theirs],
    )
    got = exchanged(send, "tensor", BITS[0])

    def next_half(keep, got, bit):
        cols = keep.shape[1] // 2

        def body(*refs):
            halved(bit, width, *refs)

        send, keep = step(body, [((tokens, cols), BF), ((tokens, cols), F32)], [keep, got])
        return keep, exchanged(send, "tensor", bit)

    high_columns = wide - low_columns
    cut_at = high_columns // 256 * 128
    high_shapes = [(both_rows, cut_at), (both_rows, high_columns - cut_at)]

    backs_of_high = [
        backward(value)
        for value in step(
            added, [(shape, BF) for shape in high_shapes], [first_high, side_high], also=[back_of_down]
        )
    ]
    bit = 2 * BITS[0]
    while bit < count:
        keep, got = next_half(keep, got, bit)
        bit *= 2

    def finished(own_ref, back, side, odd, cut):
        value = own_ref[:, cut] + back[:, cut].astype(F32)
        return value + kept(side[:, cut], odd, four, False) if four else value

    def final_down(own_ref, back, side, out):
        odd = is_odd()
        for at in range(0, half, TILE):
            cut = slice(at, at + TILE)
            value = finished(own_ref, back, side, odd, cut)
            out[:, cut] = value[:rows]
            out[:, half + at : half + at + TILE] = value[rows:]

    def ready_sums(low_ref, low_back, low_side, high_ref, high_side, gate_low, up_low, high_sum):
        odd = is_odd()
        for cut in tiles(low_columns):
            value = finished(low_ref, low_back, low_side, odd, cut)
            gate_low[:, cut] = value[:rows]
            up_low[:, cut] = value[rows:]
        for cut in tiles(high_columns):
            value = high_ref[:, cut]
            high_sum[:, cut] = value + kept(high_side[:, cut], odd, four, False) if four else value

    def final_pair(gate_low, up_low, high_sum, back_a, back_b, keep, got, out_gate, out_up, out):
        for cut in tiles(low_columns):
            out_gate[:, cut] = gate_low[:, cut]
            out_up[:, cut] = up_low[:, cut]
        for back, inside, columns in ((back_a, 0, cut_at), (back_b, cut_at, high_columns - cut_at)):
            for cut in tiles(columns):
                value = high_sum[:, shifted(cut, inside)] + back[:, cut].astype(F32)
                out_gate[:, shifted(cut, low_columns + inside)] = value[:rows]
                out_up[:, shifted(cut, low_columns + inside)] = value[rows:]
        final_output(keep, got, out)

    whole = ((rows, wide), F32)
    grad_down = step(final_down, whole, [own_down, back_of_down, side_down])
    ready = step(
        ready_sums,
        [((rows, low_columns), F32)] * 2 + [((both_rows, high_columns), F32)],
        [own_low, back_of_low, side_low, own_high, side_high],
    )
    grad_gate, grad_up, output = step(
        final_pair, [whole, whole, ((tokens, width), BF)], [*ready, *backs_of_high, keep, got]
    )
    return (output, grad_gate, grad_up, grad_down)


def solution(mesh):
    placed = (
        P("section", None),
        P("section", None),
        P(("section", "tensor"), None),
        P(("section", "tensor"), None),
        P(("section", "tensor"), None),
    )
    return jax.shard_map(
        on_device,
        mesh=mesh,
        in_specs=placed,
        out_specs=(
            P("section", "tensor"),
            P(("section", "tensor"), None),
            P(("section", "tensor"), None),
            P(("section", "tensor"), None),
        ),
        check_vma=False,
    )
```

```python
import jax
import jax.numpy as jnp
from jax import lax
from jax.experimental import pallas as pl
from jax.experimental.pallas import tpu as pltpu
from jax.sharding import PartitionSpec as P

BF = jnp.bfloat16
F32 = jnp.float32
NN = (((1,), (0,)), ((), ()))
NT = (((1,), (1,)), ((), ()))
TN = (((0,), (0,)), ((), ()))
TILE = 512
SWAP = 1
SECOND = 2
BITS = (4,)


def dot(left, right, dims):
    return lax.dot_general(left, right, dims, preferred_element_type=F32)


class Steps:
    def __init__(self):
        self.mark = None

    def __call__(self, body, outs, ins, also=(), far=0, scratch=()):
        marks = [*also] if self.mark is None else [*also, self.mark]
        count = len(ins)
        ins = [pltpu.with_memory_space_constraint(v, pltpu.HBM) if k < far else v for k, v in enumerate(ins)]

        def kernel(*refs):
            last = count + len(marks) + len(shapes)
            body(*refs[:count], *refs[count + len(marks) : last - 1], *refs[last:])
            refs[last - 1][...] = jnp.zeros_like(refs[last - 1])

        single = isinstance(outs, tuple)
        shapes = ([outs] if single else list(outs)) + [((8, 128), F32)]
        *got, self.mark = pl.pallas_call(
            kernel,
            out_shape=[jax.ShapeDtypeStruct(*s) for s in shapes],
            in_specs=[pl.BlockSpec(memory_space=pltpu.HBM)] * far
            + [pl.BlockSpec(memory_space=pltpu.VMEM)] * (count + len(marks) - far),
            out_specs=[pl.BlockSpec(memory_space=pltpu.VMEM)] * len(shapes),
            scratch_shapes=list(scratch),
            compiler_params=pltpu.CompilerParams(vmem_limit_bytes=24 * 1024 * 1024),
            cost_estimate=pl.CostEstimate(flops=1, bytes_accessed=1, transcendentals=0),
        )(*ins, *marks)
        return got[0] if single else got

    def hold(self, value):
        value, self.mark = lax.optimization_barrier((value, self.mark))
        return value


def either(bit, run):
    for value in range(2):
        pl.when(bit == value)(lambda value=value: run(value))


def tensor_bit(bit):
    return lax.rem(lax.div(lax.axis_index("tensor"), bit), 2)


def both_bits(run):
    either(tensor_bit(SECOND), lambda here: either(tensor_bit(BITS[0]), lambda mine: run(here, mine)))


def is_odd():
    return lax.rem(lax.axis_index("section"), 2) == 1


def top_rows(like):
    return lax.broadcasted_iota(jnp.int32, like.shape, 0) < like.shape[0] // 2


def placed(rows):
    shape = (2 * rows, rows)
    place = lax.broadcasted_iota(jnp.int32, shape, 0) - lax.broadcasted_iota(jnp.int32, shape, 1)
    return [(place == shift).astype(F32).astype(BF) for shift in (0, rows)]


def stacked(out, upper, lower, upper_at=0, lower_at=0):
    top, bottom = placed(upper.shape[0])
    for at in range(0, out.shape[1], TILE):
        first, second = slice(upper_at + at, upper_at + at + TILE), slice(lower_at + at, lower_at + at + TILE)
        out[:, at : at + TILE] = (dot(top, upper[:, first], NN) + dot(bottom, lower[:, second], NN)).astype(BF)


def runs(width, wide):
    return [(SWAP * width * j, 2 * SWAP * width * j) for j in range(wide // (2 * SWAP * width))]


def packed(width, gate, up, down, high, keep, send, gate_here, up_here, down_here, sems):
    copies = [
        pltpu.make_async_copy(there, here, sems.at[k])
        for k, (there, here) in enumerate(((gate, gate_here), (up, up_here), (down, down_here)))
    ]
    for copy in copies:
        copy.start()
    half = high.shape[1]
    copies[0].wait()
    copies[1].wait()
    stacked(high, gate_here, up_here, half, half)
    copies[2].wait()

    def run(mine):
        for near, there in runs(width, 2 * half):
            here = slice(near, near + SWAP * width)
            for out, which in ((keep, mine), (send, 1 - mine)):
                at = there + SWAP * width * which
                out[:, here] = down_here[:, at : at + SWAP * width]

    either(tensor_bit(SWAP), run)


def project_tiles(x, low, high):
    half = low.shape[1]
    tile = min(half, 1024)
    total = jnp.zeros((low.shape[0], x.shape[0]), F32)
    for at in range(0, half, tile):
        cut = slice(at, at + tile)
        total += dot(low[:, cut], x[:, cut], NT)
        total += dot(high[:, cut], x[:, half + at : half + at + tile], NT)
    return total


def project(x, low, high, both, hid_a, hid_b):
    rows = low.shape[0] // 2
    total = project_tiles(x, low, high)
    both[...] = total
    hidden = total * jax.nn.sigmoid(total) * pltpu.roll(total, rows, 0)
    hidden = jnp.where(top_rows(total), hidden, 0.0)
    hid_a[...] = hidden.astype(BF)
    hid_b[...] = pltpu.roll(hidden, rows, 0).astype(BF)


def project_first(x_there, g_there, low, high, x, g, both, hid_a, hid_b, sems):
    copies = [pltpu.make_async_copy(x_there, x, sems.at[0]), pltpu.make_async_copy(g_there, g, sems.at[1])]
    for copy in copies:
        copy.start()
    copies[0].wait()
    project(x, low, high, both, hid_a, hid_b)
    copies[1].wait()


def shares(width, g, down, part):
    wide = g.shape[1]
    tile = min(SWAP * width, 1024)

    def run(mine):
        total = jnp.zeros(part.shape, F32)
        for near, there in runs(width, wide):
            for at in range(0, SWAP * width, tile):
                far = there + SWAP * width * mine + at
                total += dot(down[:, near + at : near + at + tile], g[:, far : far + tile], NT)
        part[...] = total

    either(tensor_bit(SWAP), run)


def sent_share(part, hid_b):
    share = part[...]
    return jnp.where(top_rows(share), pltpu.roll(share, share.shape[0] // 2, 0), hid_b[...].astype(F32))


def finish(both, part, got, hid_a, pair, hid_pair):
    rows = both.shape[0] // 2
    gate, got = both[...], got[...]
    dhid = part[...] + got
    sig = jax.nn.sigmoid(gate)
    dgate = dhid * pltpu.roll(gate, rows, 0) * sig * (1.0 + gate * (1.0 - sig))
    dup = pltpu.roll(dhid * (gate * sig), rows, 0)
    first = top_rows(gate)
    pair[...] = jnp.where(first, dgate, dup).astype(BF)
    hid_pair[...] = jnp.where(first, hid_a[...].astype(F32), got).astype(BF)


def down_columns(g, hid_a, hid_b, at, half):
    cut = slice(at, at + TILE)
    return dot(hid_a[...], g[:, cut], NN) + dot(hid_b[...], g[:, half + at : half + at + TILE], NN)


def tiles(size):
    return [slice(at, min(at + TILE, size)) for at in range(0, size, TILE)]


def shifted(cut, offset):
    return slice(cut.start + offset, cut.stop + offset)


def pair_columns(x, pair, outs):
    at = 0
    for out in outs:
        for cut in tiles(out.shape[1]):
            out[:, cut] = dot(pair[...], x[:, shifted(cut, at)], NN).astype(out.dtype)
        at += out.shape[1]


def own_grads(x, g, hid_a, hid_b, pair, *refs):
    *outs, down = refs
    half = down.shape[1]
    pair_columns(x, pair, outs)
    for at in range(0, half, TILE):
        down[:, at : at + TILE] = down_columns(g, hid_a, hid_b, at, half)


def sent_down(g, hid_a, hid_b, out):
    half = out.shape[1]
    for at in range(0, half, TILE):
        out[:, at : at + TILE] = down_columns(g, hid_a, hid_b, at, half).astype(BF)


def sent_pair(x, pair, *outs):
    pair_columns(x, pair, outs)


def kept(side, odd, four, wanted):
    value = side.astype(F32)
    return jnp.where(odd == wanted, value, 0.0) if four else value


def picked(here, piece, out):
    @pl.when(is_odd())
    def _():
        out[...] = here[...]

    @pl.when(jnp.logical_not(is_odd()))
    def _():
        out[...] = piece[...]


def other_columns(width, down, out, at):
    def run(mine):
        for k in range(down.shape[1] // (2 * width)):
            column = (2 * k + 1 - mine) * width
            out[:, at + k * width : at + (k + 1) * width] = down[:, column : column + width]

    either(tensor_bit(SECOND), run)


def near_sums(width, *refs):
    hids, downs, outs = refs[:3], refs[3:6], refs[6:]
    tile = min(width, TILE)

    def run(here, mine):
        for block in range(2 * outs[0].shape[1] // width):
            for at in range(0, width, tile):
                near, column = (2 * block + here) * width + at, block // 2 * width + at
                total = sum(dot(hid[...], down[:, near : near + tile], TN) for hid, down in zip(hids, downs))
                outs[int(block % 2 == mine)][:, column : column + tile] = total

    both_bits(run)


def output_sums(width, send_sum, keep_sum, two, last, send, keep):
    tokens, quarter = send.shape[0], two.shape[1] // 2
    tile = min(width, TILE)
    gots = ((two, 0), (two, quarter), (last, 0))

    def run(mine):
        for block in range(2 * keep.shape[1] // width):
            for at in range(0, width, tile):
                far, column = block * width + at, block // 2 * width + at
                out, sums = (keep, keep_sum) if block % 2 == mine else (send, send_sum)
                total = sums[:, column : column + tile]
                for k, (got, offset) in enumerate(gots):
                    other = last[:, quarter + k * tokens : quarter + (k + 1) * tokens]
                    total += dot(other, got[:, offset + far : offset + far + tile], TN)
                out[:, column : column + tile] = total.astype(out.dtype)

    either(tensor_bit(BITS[0]), run)


def halved(bit, width, keep, got, send, left):
    tile = min(width, TILE)

    def run(mine):
        for block in range(left.shape[1] // width):
            for out, which in ((send, 1 - mine), (left, mine)):
                for at in range(0, width, tile):
                    cols = slice((2 * block + which) * width + at, (2 * block + which) * width + at + tile)
                    value = keep[:, cols] + got[:, cols].astype(F32)
                    out[:, block * width + at : block * width + at + tile] = value.astype(out.dtype)

    either(tensor_bit(bit), run)


def final_output(keep, got, out):
    out[...] = (keep[...] + got[...].astype(F32)).astype(BF)


def exchanged(value, axis, bit):
    count = lax.axis_size(axis)
    return lax.ppermute(value, axis, [(source, source ^ bit) for source in range(count)])


def ring_passed(value, steps):
    count = lax.axis_size("section")
    return lax.ppermute(value, "section", [(source, (source + steps) % count) for source in range(count)])


def on_device(x, g, gate_weight, up_weight, down_weight):
    rows, wide = gate_weight.shape
    half, both_rows, tokens = wide // 2, 2 * rows, x.shape[0]
    count = lax.axis_size("tensor")
    assert count > BITS[0] and count & (count - 1) == 0
    width = wide // count
    four = lax.axis_size("section") == 4
    piece, narrow = ((both_rows, half), BF), ((rows, half), BF)
    small, small_bf = ((both_rows, tokens), F32), ((both_rows, tokens), BF)
    step = Steps()

    def with_width(body):
        def run(*refs):
            body(width, *refs)

        return run

    def one_hop(value):
        return exchanged(value, "section", 2) if four else ring_passed(value, 1)

    def relay(here, value):
        if not four:
            return ring_passed(here, 1)
        return exchanged(step(picked, piece, [here, value]), "section", 1)

    def outward(value):
        return exchanged(value, "section", 1) if four else ring_passed(value, -1)

    def backward(value):
        return exchanged(value, "section", 2) if four else ring_passed(value, -1)

    own, first, second = [None] * 3, [None] * 3, [None] * 3
    own[1], down_keep, down_send, gate_here, up_here = step(
        with_width(packed),
        [piece, narrow, narrow, ((rows, wide), BF), ((rows, wide), BF)],
        [gate_weight, up_weight, down_weight],
        far=3,
        scratch=[pltpu.VMEM((rows, wide), BF), pltpu.SemaphoreType.DMA((3,))],
    )
    first[1] = one_hop(own[1])
    down_got = exchanged(down_send, "tensor", SWAP)

    def joined(keep, got, out):
        stacked(out, keep, got)

    own[2] = step(joined, piece, [down_keep, down_got])
    if four:
        crossed = exchanged(own[2], "section", 1)
        onward = lax.ppermute(crossed, "section", [(source, source ^ 2) for source in (0, 2)])
    first[2] = one_hop(own[2])
    own[0] = step(joined, piece, [gate_here, up_here])
    x, g, both_own, *hid_own = step(
        project_first,
        [(x.shape, BF), (g.shape, BF), small, small_bf, small_bf],
        [x, g, own[0], own[1]],
        far=2,
        scratch=[pltpu.SemaphoreType.DMA((2,))],
    )
    first[0] = one_hop(step.hold(own[0]))
    share = with_width(shares)
    share_own = step(share, small, [g, own[2]])
    second[1] = relay(first[1], own[1])
    second[0] = relay(first[0], own[0])
    both_first, *hid_first = step(project, [small, small_bf, small_bf], [x, first[0], first[1]], also=[second[1]])
    second[2] = step(picked, piece, [crossed, onward]) if four else ring_passed(first[2], 1)
    share_second = step(share, small, [g, second[2]])

    def two_other(down_a, down_b, out):
        other_columns(width, down_a, out, 0)
        other_columns(width, down_b, out, half // 2)

    two_theirs = exchanged(step(two_other, piece, [own[2], second[2]]), "tensor", SECOND)
    both_second, *hid_second = step(project, [small, small_bf, small_bf], [x, second[0], second[1]])

    def two_sent(share_a, hid_a, share_b, hid_b, out):
        out[:both_rows, :] = sent_share(share_a, hid_a)
        out[both_rows:, :] = sent_share(share_b, hid_b)

    sent = step(two_sent, ((2 * both_rows, tokens), F32), [share_own, hid_own[1], share_second, hid_second[1]])
    got_two = exchanged(sent, "tensor", SWAP)
    side_down = outward(step(sent_down, piece, [g, *hid_second]))

    def finish_two(both_a, part_a, hid_a, both_b, part_b, hid_b, got, pair_a, out_a, pair_b, out_b):
        finish(both_a, part_a, got.at[:both_rows, :], hid_a, pair_a, out_a)
        finish(both_b, part_b, got.at[both_rows:, :], hid_b, pair_b, out_b)

    pair_own, wide_own, pair_second, wide_second = step(
        finish_two, [small_bf] * 4, [both_own, share_own, hid_own[0], both_second, share_second, hid_second[0], got_two]
    )
    low_columns = half + 128
    high_columns = wide - low_columns
    cut_at = high_columns // 256 * 128 + 128
    low_shape = (both_rows, low_columns)
    high_shapes = [(both_rows, cut_at), (both_rows, high_columns - cut_at)]
    low, *highs = step(sent_pair, [(shape, BF) for shape in (low_shape, *high_shapes)], [x, pair_second])

    grads_f32 = [(shape, F32) for shape in (low_shape, *high_shapes, (both_rows, half))]
    own_low, *own_highs, own_down = step(own_grads, grads_f32, [x, g, *hid_own, pair_own])

    def one_sent(gr, down, hid, part, out):
        shares(width, gr, down, part)
        out[...] = sent_share(part, hid)

    share_first, sent = step(one_sent, [small, small], [g, first[2], hid_first[1]], also=[two_theirs])
    got_one = exchanged(sent, "tensor", SWAP)
    side_low = outward(step.hold(low))

    def finish_last(both, share, got, hid, wide_a, wide_b, down, pair, wide_out, out):
        finish(both, share, got, hid, pair, wide_out)
        other_columns(width, down, out, 0)
        for k, ref in enumerate((wide_a, wide_b, wide_out)):
            out[:, half // 2 + k * tokens : half // 2 + (k + 1) * tokens] = ref[...]

    pair_first, wide_first, sent = step(
        finish_last,
        [small_bf, small_bf, ((both_rows, half // 2 + 3 * tokens), BF)],
        [both_first, share_first, got_one, hid_first[0], wide_own, wide_second, first[2]],
    )
    last_theirs = exchanged(sent, "tensor", SECOND)
    near = step(
        with_width(near_sums),
        [((tokens, wide // 8), F32)] * 2,
        [wide_own, wide_second, wide_first, own[2], second[2], first[2]],
    )
    first_low, *first_highs, first_down = step(own_grads, grads_f32, [x, g, *hid_first, pair_first])

    def added(own_ref, side, *outs):
        odd, at = is_odd(), 0
        for out in outs:
            for cut in tiles(out.shape[1]):
                from_ = shifted(cut, at)
                out[:, cut] = (own_ref[:, from_] + kept(side[:, from_], odd, four, True)).astype(BF)
            at += out.shape[1]

    back_of_down = backward(step(added, piece, [first_down, side_down]))
    highs[0] = step.hold(highs[0])
    side_highs = [outward(value) for value in highs]
    back_of_low = backward(step(added, (low_shape, BF), [first_low, side_low]))
    send, keep = step(
        with_width(output_sums),
        [((tokens, wide // 8), BF), ((tokens, wide // 8), F32)],
        [*near, two_theirs, last_theirs],
    )
    got = exchanged(send, "tensor", BITS[0])

    def next_half(keep, got, bit):
        cols = keep.shape[1] // 2

        def body(*refs):
            halved(bit, width, *refs)

        send, keep = step(body, [((tokens, cols), BF), ((tokens, cols), F32)], [keep, got])
        return keep, exchanged(send, "tensor", bit)

    backs_of_high = [
        backward(step(added, (shape, BF), [first, side], also=also))
        for shape, first, side, also in zip(high_shapes, first_highs, side_highs, ([], [back_of_down]))
    ]
    bit = 2 * BITS[0]
    while bit < count:
        keep, got = next_half(keep, got, bit)
        bit *= 2

    def finished(own_ref, back, side, odd, cut):
        value = own_ref[:, cut] + back[:, cut].astype(F32)
        return value + kept(side[:, cut], odd, four, False) if four else value

    def final_down(own_ref, back, side, out):
        odd = is_odd()
        for at in range(0, half, TILE):
            cut = slice(at, at + TILE)
            value = finished(own_ref, back, side, odd, cut)
            out[:, cut] = value[:rows]
            out[:, half + at : half + at + TILE] = value[rows:]

    def ready_sums(low_ref, low_back, low_side, high_a, high_b, side_a, side_b, gate_low, up_low, sum_a, sum_b):
        odd = is_odd()
        for cut in tiles(low_columns):
            value = finished(low_ref, low_back, low_side, odd, cut)
            gate_low[:, cut] = value[:rows]
            up_low[:, cut] = value[rows:]
        for own_ref, side, out in ((high_a, side_a, sum_a), (high_b, side_b, sum_b)):
            for cut in tiles(out.shape[1]):
                value = own_ref[:, cut]
                out[:, cut] = value + kept(side[:, cut], odd, four, False) if four else value

    def final_pair(gate_low, up_low, sum_a, sum_b, back_a, back_b, keep, got, out_gate, out_up, out):
        for cut in tiles(low_columns):
            out_gate[:, cut] = gate_low[:, cut]
            out_up[:, cut] = up_low[:, cut]
        for own_sum, back, offset in ((sum_a, back_a, low_columns), (sum_b, back_b, low_columns + cut_at)):
            for cut in tiles(back.shape[1]):
                value = own_sum[:, cut] + back[:, cut].astype(F32)
                out_gate[:, shifted(cut, offset)] = value[:rows]
                out_up[:, shifted(cut, offset)] = value[rows:]
        final_output(keep, got, out)

    whole = ((rows, wide), F32)
    grad_down = step(final_down, whole, [own_down, back_of_down, side_down])
    ready = step(
        ready_sums,
        [((rows, low_columns), F32)] * 2 + [(shape, F32) for shape in high_shapes],
        [own_low, back_of_low, side_low, *own_highs, *side_highs],
    )
    grad_gate, grad_up, output = step(
        final_pair, [whole, whole, ((tokens, width), BF)], [*ready, *backs_of_high, keep, got]
    )
    return (output, grad_gate, grad_up, grad_down)


def solution(mesh):
    placed = (
        P("section", None),
        P("section", None),
        P(("section", "tensor"), None),
        P(("section", "tensor"), None),
        P(("section", "tensor"), None),
    )
    return jax.shard_map(
        on_device,
        mesh=mesh,
        in_specs=placed,
        out_specs=(
            P("section", "tensor"),
            P(("section", "tensor"), None),
            P(("section", "tensor"), None),
            P(("section", "tensor"), None),
        ),
        check_vma=False,
    )
```

```python
import jax
import jax.numpy as jnp
from jax import lax
from jax.experimental import pallas as pl
from jax.experimental.pallas import tpu as pltpu
from jax.sharding import PartitionSpec as P

BF = jnp.bfloat16
F32 = jnp.float32
NN = (((1,), (0,)), ((), ()))
NT = (((1,), (1,)), ((), ()))
TN = (((0,), (0,)), ((), ()))
TILE = 512
SWAP = 1
SECOND = 2
BITS = (4,)


def dot(left, right, dims):
    return lax.dot_general(left, right, dims, preferred_element_type=F32)


class Steps:
    def __init__(self):
        self.mark = None

    def __call__(self, body, outs, ins, also=(), far=0, scratch=()):
        marks = [*also] if self.mark is None else [*also, self.mark]
        count = len(ins)
        ins = [pltpu.with_memory_space_constraint(v, pltpu.HBM) if k < far else v for k, v in enumerate(ins)]

        def kernel(*refs):
            last = count + len(marks) + len(shapes)
            body(*refs[:count], *refs[count + len(marks) : last - 1], *refs[last:])
            refs[last - 1][...] = jnp.zeros_like(refs[last - 1])

        single = isinstance(outs, tuple)
        shapes = ([outs] if single else list(outs)) + [((8, 128), F32)]
        *got, self.mark = pl.pallas_call(
            kernel,
            out_shape=[jax.ShapeDtypeStruct(*s) for s in shapes],
            in_specs=[pl.BlockSpec(memory_space=pltpu.HBM)] * far
            + [pl.BlockSpec(memory_space=pltpu.VMEM)] * (count + len(marks) - far),
            out_specs=[pl.BlockSpec(memory_space=pltpu.VMEM)] * len(shapes),
            scratch_shapes=list(scratch),
            compiler_params=pltpu.CompilerParams(vmem_limit_bytes=24 * 1024 * 1024),
            cost_estimate=pl.CostEstimate(flops=1, bytes_accessed=1, transcendentals=0),
        )(*ins, *marks)
        return got[0] if single else got

    def hold(self, value):
        value, self.mark = lax.optimization_barrier((value, self.mark))
        return value


def either(bit, run):
    for value in range(2):
        pl.when(bit == value)(lambda value=value: run(value))


def tensor_bit(bit):
    return lax.rem(lax.div(lax.axis_index("tensor"), bit), 2)


def both_bits(run):
    either(tensor_bit(SECOND), lambda here: either(tensor_bit(BITS[0]), lambda mine: run(here, mine)))


def is_odd():
    return lax.rem(lax.axis_index("section"), 2) == 1


def top_rows(like):
    return lax.broadcasted_iota(jnp.int32, like.shape, 0) < like.shape[0] // 2


def placed(rows):
    shape = (2 * rows, rows)
    place = lax.broadcasted_iota(jnp.int32, shape, 0) - lax.broadcasted_iota(jnp.int32, shape, 1)
    return [(place == shift).astype(F32).astype(BF) for shift in (0, rows)]


def stacked(out, upper, lower, upper_at=0, lower_at=0):
    top, bottom = placed(upper.shape[0])
    for at in range(0, out.shape[1], TILE):
        first, second = slice(upper_at + at, upper_at + at + TILE), slice(lower_at + at, lower_at + at + TILE)
        out[:, at : at + TILE] = (dot(top, upper[:, first], NN) + dot(bottom, lower[:, second], NN)).astype(BF)


def runs(width, wide):
    return [(SWAP * width * j, 2 * SWAP * width * j) for j in range(wide // (2 * SWAP * width))]


def packed(width, gate, up, down, high, keep, send, gate_here, up_here, down_here, sems):
    copies = [
        pltpu.make_async_copy(there, here, sems.at[k])
        for k, (there, here) in enumerate(((gate, gate_here), (up, up_here), (down, down_here)))
    ]
    for copy in copies:
        copy.start()
    half = high.shape[1]
    copies[0].wait()
    copies[1].wait()
    stacked(high, gate_here, up_here, half, half)
    copies[2].wait()

    def run(mine):
        for near, there in runs(width, 2 * half):
            here = slice(near, near + SWAP * width)
            for out, which in ((keep, mine), (send, 1 - mine)):
                at = there + SWAP * width * which
                out[:, here] = down_here[:, at : at + SWAP * width]

    either(tensor_bit(SWAP), run)


def project_tiles(x, low, high):
    half = low.shape[1]
    tile = min(half, 1024)
    total = jnp.zeros((low.shape[0], x.shape[0]), F32)
    for at in range(0, half, tile):
        cut = slice(at, at + tile)
        total += dot(low[:, cut], x[:, cut], NT)
        total += dot(high[:, cut], x[:, half + at : half + at + tile], NT)
    return total


def project(x, low, high, both, hid_a, hid_b):
    rows = low.shape[0] // 2
    total = project_tiles(x, low, high)
    both[...] = total
    hidden = total * jax.nn.sigmoid(total) * pltpu.roll(total, rows, 0)
    hidden = jnp.where(top_rows(total), hidden, 0.0)
    hid_a[...] = hidden.astype(BF)
    hid_b[...] = pltpu.roll(hidden, rows, 0).astype(BF)


def project_first(x_there, g_there, low, high, x, g, both, hid_a, hid_b, sems):
    copies = [pltpu.make_async_copy(x_there, x, sems.at[0]), pltpu.make_async_copy(g_there, g, sems.at[1])]
    for copy in copies:
        copy.start()
    copies[0].wait()
    project(x, low, high, both, hid_a, hid_b)
    copies[1].wait()


def shares(width, g, down, part):
    wide = g.shape[1]
    tile = min(SWAP * width, 1024)

    def run(mine):
        total = jnp.zeros(part.shape, F32)
        for near, there in runs(width, wide):
            for at in range(0, SWAP * width, tile):
                far = there + SWAP * width * mine + at
                total += dot(down[:, near + at : near + at + tile], g[:, far : far + tile], NT)
        part[...] = total

    either(tensor_bit(SWAP), run)


def sent_share(part, hid_b):
    share = part[...]
    return jnp.where(top_rows(share), pltpu.roll(share, share.shape[0] // 2, 0), hid_b[...].astype(F32))


def finish(both, part, got, hid_a, pair, hid_pair):
    rows = both.shape[0] // 2
    gate, got = both[...], got[...]
    dhid = part[...] + got
    sig = jax.nn.sigmoid(gate)
    dgate = dhid * pltpu.roll(gate, rows, 0) * sig * (1.0 + gate * (1.0 - sig))
    dup = pltpu.roll(dhid * (gate * sig), rows, 0)
    first = top_rows(gate)
    pair[...] = jnp.where(first, dgate, dup).astype(BF)
    hid_pair[...] = jnp.where(first, hid_a[...].astype(F32), got).astype(BF)


def down_columns(g, hid_a, hid_b, at, half):
    cut = slice(at, at + TILE)
    return dot(hid_a[...], g[:, cut], NN) + dot(hid_b[...], g[:, half + at : half + at + TILE], NN)


def tiles(size):
    return [slice(at, min(at + TILE, size)) for at in range(0, size, TILE)]


def shifted(cut, offset):
    return slice(cut.start + offset, cut.stop + offset)


def own_grads(x, g, hid_a, hid_b, pair, low, high, down):
    half = down.shape[1]
    for out, offset in ((low, 0), (high, low.shape[1])):
        for cut in tiles(out.shape[1]):
            out[:, cut] = dot(pair[...], x[:, shifted(cut, offset)], NN)
    for at in range(0, half, TILE):
        down[:, at : at + TILE] = down_columns(g, hid_a, hid_b, at, half)


def sent_down(g, hid_a, hid_b, out):
    half = out.shape[1]
    for at in range(0, half, TILE):
        out[:, at : at + TILE] = down_columns(g, hid_a, hid_b, at, half).astype(BF)


def sent_pair(x, pair, low, high):
    for out, offset in ((low, 0), (high, low.shape[1])):
        for cut in tiles(out.shape[1]):
            out[:, cut] = dot(pair[...], x[:, shifted(cut, offset)], NN).astype(BF)


def kept(side, odd, four, wanted):
    value = side.astype(F32)
    return jnp.where(odd == wanted, value, 0.0) if four else value


def picked(here, piece, out):
    @pl.when(is_odd())
    def _():
        out[...] = here[...]

    @pl.when(jnp.logical_not(is_odd()))
    def _():
        out[...] = piece[...]


def other_columns(width, down, out, at):
    def run(mine):
        for k in range(down.shape[1] // (2 * width)):
            column = (2 * k + 1 - mine) * width
            out[:, at + k * width : at + (k + 1) * width] = down[:, column : column + width]

    either(tensor_bit(SECOND), run)


def output_sums(width, *refs):
    hids, downs, (two, last, send, keep) = refs[:3], refs[3:6], refs[6:]
    tokens, quarter = send.shape[0], downs[0].shape[1] // 2
    gots = ((two, 0), (two, quarter), (last, 0))
    tile = min(width, TILE)

    def run(here, mine):
        for block in range(2 * keep.shape[1] // width):
            out = keep if block % 2 == mine else send
            for at in range(0, width, tile):
                near, far = (2 * block + here) * width + at, block * width + at
                total = 0.0
                for k, (hid, down, (got, offset)) in enumerate(zip(hids, downs, gots)):
                    total += dot(hid[...], down[:, near : near + tile], TN)
                    other = last[:, quarter + k * tokens : quarter + (k + 1) * tokens]
                    total += dot(other, got[:, offset + far : offset + far + tile], TN)
                column = block // 2 * width + at
                out[:, column : column + tile] = total.astype(out.dtype)

    both_bits(run)


def halved(bit, width, keep, got, send, left):
    tile = min(width, TILE)

    def run(mine):
        for block in range(left.shape[1] // width):
            for out, which in ((send, 1 - mine), (left, mine)):
                for at in range(0, width, tile):
                    cols = slice((2 * block + which) * width + at, (2 * block + which) * width + at + tile)
                    value = keep[:, cols] + got[:, cols].astype(F32)
                    out[:, block * width + at : block * width + at + tile] = value.astype(out.dtype)

    either(tensor_bit(bit), run)


def final_output(keep, got, out):
    out[...] = (keep[...] + got[...].astype(F32)).astype(BF)


def exchanged(value, axis, bit):
    count = lax.axis_size(axis)
    return lax.ppermute(value, axis, [(source, source ^ bit) for source in range(count)])


def ring_passed(value, steps):
    count = lax.axis_size("section")
    return lax.ppermute(value, "section", [(source, (source + steps) % count) for source in range(count)])


def on_device(x, g, gate_weight, up_weight, down_weight):
    rows, wide = gate_weight.shape
    half, both_rows, tokens = wide // 2, 2 * rows, x.shape[0]
    count = lax.axis_size("tensor")
    assert count > BITS[0] and count & (count - 1) == 0
    width = wide // count
    four = lax.axis_size("section") == 4
    piece, narrow = ((both_rows, half), BF), ((rows, half), BF)
    small, small_bf = ((both_rows, tokens), F32), ((both_rows, tokens), BF)
    step = Steps()

    def with_width(body):
        def run(*refs):
            body(width, *refs)

        return run

    def one_hop(value):
        return exchanged(value, "section", 2) if four else ring_passed(value, 1)

    def relay(here, value):
        if not four:
            return ring_passed(here, 1)
        return exchanged(step(picked, piece, [here, value]), "section", 1)

    def outward(value):
        return exchanged(value, "section", 1) if four else ring_passed(value, -1)

    def backward(value):
        return exchanged(value, "section", 2) if four else ring_passed(value, -1)

    own, first, second = [None] * 3, [None] * 3, [None] * 3
    own[1], down_keep, down_send, gate_here, up_here = step(
        with_width(packed),
        [piece, narrow, narrow, ((rows, wide), BF), ((rows, wide), BF)],
        [gate_weight, up_weight, down_weight],
        far=3,
        scratch=[pltpu.VMEM((rows, wide), BF), pltpu.SemaphoreType.DMA((3,))],
    )
    first[1] = one_hop(own[1])
    down_got = exchanged(down_send, "tensor", SWAP)

    def joined(keep, got, out):
        stacked(out, keep, got)

    own[2] = step(joined, piece, [down_keep, down_got])
    if four:
        crossed = exchanged(own[2], "section", 1)
        onward = lax.ppermute(crossed, "section", [(source, source ^ 2) for source in (0, 2)])
    first[2] = one_hop(own[2])
    own[0] = step(joined, piece, [gate_here, up_here])
    x, g, both_own, *hid_own = step(
        project_first,
        [(x.shape, BF), (g.shape, BF), small, small_bf, small_bf],
        [x, g, own[0], own[1]],
        far=2,
        scratch=[pltpu.SemaphoreType.DMA((2,))],
    )
    first[0] = one_hop(step.hold(own[0]))
    share = with_width(shares)
    share_own = step(share, small, [g, own[2]])
    second[1] = relay(first[1], own[1])
    second[0] = relay(first[0], own[0])
    both_first, *hid_first = step(project, [small, small_bf, small_bf], [x, first[0], first[1]], also=[second[1]])
    second[2] = step(picked, piece, [crossed, onward]) if four else ring_passed(first[2], 1)
    share_second = step(share, small, [g, second[2]])

    def two_other(down_a, down_b, out):
        other_columns(width, down_a, out, 0)
        other_columns(width, down_b, out, half // 2)

    two_theirs = exchanged(step(two_other, piece, [own[2], second[2]]), "tensor", SECOND)
    both_second, *hid_second = step(project, [small, small_bf, small_bf], [x, second[0], second[1]])

    def two_sent(share_a, hid_a, share_b, hid_b, out):
        out[:both_rows, :] = sent_share(share_a, hid_a)
        out[both_rows:, :] = sent_share(share_b, hid_b)

    sent = step(two_sent, ((2 * both_rows, tokens), F32), [share_own, hid_own[1], share_second, hid_second[1]])
    got_two = exchanged(sent, "tensor", SWAP)
    side_down = outward(step(sent_down, piece, [g, *hid_second]))

    def finish_two(both_a, part_a, hid_a, both_b, part_b, hid_b, got, pair_a, out_a, pair_b, out_b):
        finish(both_a, part_a, got.at[:both_rows, :], hid_a, pair_a, out_a)
        finish(both_b, part_b, got.at[both_rows:, :], hid_b, pair_b, out_b)

    pair_own, wide_own, pair_second, wide_second = step(
        finish_two, [small_bf] * 4, [both_own, share_own, hid_own[0], both_second, share_second, hid_second[0], got_two]
    )
    low_columns = half + 128
    low_shape, high_shape = (both_rows, low_columns), (both_rows, wide - low_columns)
    low, high = step(sent_pair, [(low_shape, BF), (high_shape, BF)], [x, pair_second])

    grads_f32 = [(low_shape, F32), (high_shape, F32), ((both_rows, half), F32)]
    own_low, own_high, own_down = step(own_grads, grads_f32, [x, g, *hid_own, pair_own])

    def one_sent(gr, down, hid, part, out):
        shares(width, gr, down, part)
        out[...] = sent_share(part, hid)

    share_first, sent = step(one_sent, [small, small], [g, first[2], hid_first[1]], also=[two_theirs])
    got_one = exchanged(sent, "tensor", SWAP)
    side_low = outward(step.hold(low))

    def finish_last(both, share, got, hid, wide_a, wide_b, down, pair, wide_out, out):
        finish(both, share, got, hid, pair, wide_out)
        other_columns(width, down, out, 0)
        for k, ref in enumerate((wide_a, wide_b, wide_out)):
            out[:, half // 2 + k * tokens : half // 2 + (k + 1) * tokens] = ref[...]

    pair_first, wide_first, sent = step(
        finish_last,
        [small_bf, small_bf, ((both_rows, half // 2 + 3 * tokens), BF)],
        [both_first, share_first, got_one, hid_first[0], wide_own, wide_second, first[2]],
    )
    last_theirs = exchanged(sent, "tensor", SECOND)
    def back_down(gr, a, b, side, out):
        odd = is_odd()
        for at in range(0, half, TILE):
            value = down_columns(gr, a, b, at, half) + kept(side[:, at : at + TILE], odd, four, True)
            out[:, at : at + TILE] = value.astype(BF)

    def back_pair(offset):
        def body(xr, pair, side, out):
            odd = is_odd()
            for cut in tiles(out.shape[1]):
                value = dot(pair[...], xr[:, shifted(cut, offset)], NN)
                out[:, cut] = (value + kept(side[:, cut], odd, four, True)).astype(BF)

        return body

    back_of_down = backward(step(back_down, piece, [g, *hid_first, side_down]))
    side_high = outward(step.hold(high))
    back_of_low = backward(step(back_pair(0), (low_shape, BF), [x, pair_first, side_low]))
    send, keep = step(
        with_width(output_sums),
        [((tokens, wide // 8), BF), ((tokens, wide // 8), F32)],
        [wide_own, wide_second, wide_first, own[2], second[2], first[2], two_theirs, last_theirs],
    )
    got = exchanged(send, "tensor", BITS[0])

    def next_half(keep, got, bit):
        cols = keep.shape[1] // 2

        def body(*refs):
            halved(bit, width, *refs)

        send, keep = step(body, [((tokens, cols), BF), ((tokens, cols), F32)], [keep, got])
        return keep, exchanged(send, "tensor", bit)

    high_columns = wide - low_columns
    cut_at = high_columns // 256 * 128
    high_shapes = [(both_rows, cut_at), (both_rows, high_columns - cut_at)]

    def back_last(xr, pair, side, out_a, out_b):
        odd = is_odd()
        for out, offset in ((out_a, 0), (out_b, cut_at)):
            for cut in tiles(out.shape[1]):
                value = dot(pair[...], xr[:, shifted(cut, low_columns + offset)], NN)
                value += kept(side[:, shifted(cut, offset)], odd, four, True)
                out[:, cut] = value.astype(BF)

    backs_of_high = [
        backward(value)
        for value in step(
            back_last, [(shape, BF) for shape in high_shapes], [x, pair_first, side_high], also=[back_of_down]
        )
    ]
    bit = 2 * BITS[0]
    while bit < count:
        keep, got = next_half(keep, got, bit)
        bit *= 2

    def finished(own_ref, back, side, odd, cut):
        value = own_ref[:, cut] + back[:, cut].astype(F32)
        return value + kept(side[:, cut], odd, four, False) if four else value

    def final_down(own_ref, back, side, out):
        odd = is_odd()
        for at in range(0, half, TILE):
            cut = slice(at, at + TILE)
            value = finished(own_ref, back, side, odd, cut)
            out[:, cut] = value[:rows]
            out[:, half + at : half + at + TILE] = value[rows:]

    def ready_sums(low_ref, low_back, low_side, high_ref, high_side, gate_low, up_low, high_sum):
        odd = is_odd()
        for cut in tiles(low_columns):
            value = finished(low_ref, low_back, low_side, odd, cut)
            gate_low[:, cut] = value[:rows]
            up_low[:, cut] = value[rows:]
        for cut in tiles(high_columns):
            value = high_ref[:, cut]
            high_sum[:, cut] = value + kept(high_side[:, cut], odd, four, False) if four else value

    def final_pair(gate_low, up_low, high_sum, back_a, back_b, keep, got, out_gate, out_up, out):
        for cut in tiles(low_columns):
            out_gate[:, cut] = gate_low[:, cut]
            out_up[:, cut] = up_low[:, cut]
        for back, inside, columns in ((back_a, 0, cut_at), (back_b, cut_at, high_columns - cut_at)):
            for cut in tiles(columns):
                value = high_sum[:, shifted(cut, inside)] + back[:, cut].astype(F32)
                out_gate[:, shifted(cut, low_columns + inside)] = value[:rows]
                out_up[:, shifted(cut, low_columns + inside)] = value[rows:]
        final_output(keep, got, out)

    whole = ((rows, wide), F32)
    grad_down = step(final_down, whole, [own_down, back_of_down, side_down])
    ready = step(
        ready_sums,
        [((rows, low_columns), F32)] * 2 + [((both_rows, high_columns), F32)],
        [own_low, back_of_low, side_low, own_high, side_high],
    )
    grad_gate, grad_up, output = step(
        final_pair, [whole, whole, ((tokens, width), BF)], [*ready, *backs_of_high, keep, got]
    )
    return (output, grad_gate, grad_up, grad_down)


def solution(mesh):
    placed = (
        P("section", None),
        P("section", None),
        P(("section", "tensor"), None),
        P(("section", "tensor"), None),
        P(("section", "tensor"), None),
    )
    return jax.shard_map(
        on_device,
        mesh=mesh,
        in_specs=placed,
        out_specs=(
            P("section", "tensor"),
            P(("section", "tensor"), None),
            P(("section", "tensor"), None),
            P(("section", "tensor"), None),
        ),
        check_vma=False,
    )
```
